512 devices in a mesh: gx: 16 (over z_hi, x, core), gy: 32 (over y, z_lo).
Axes of the slice: x: 4, y: 8, z: 8 (z_hi: 2, z_lo: 4; z = z_hi * 4 + z_lo), core: 2. Of those that a mesh axis runs over, the one named last changes fastest.
Arguments:
- grid_field: bfloat16 [1, 4, 16, 128, 128, 128], P(None, None, None, 'gx', 'gy'), may hold values from -6 to 6
- spectral_weight: bfloat16 [16, 16, 64, 32, 512], P(None, None, 'gx', 'gy'), may hold values from -3 to 3
- point_weight: bfloat16 [16, 16], replicated, may hold values from -1.5 to 1.5
- cotangent: bfloat16 [1, 4, 16, 128, 128, 128], P(None, None, None, 'gx', 'gy'), may hold values from -6 to 6
Outputs:
- layer_out: bfloat16 [1, 4, 16, 128, 128, 128], P(None, None, None, 'gx', 'gy')
- grad_field: bfloat16 [1, 4, 16, 128, 128, 128], P(None, None, None, 'gx', 'gy')
- grad_spectral: bfloat16 [16, 16, 64, 32, 512], P(None, None, 'gx', 'gy')
The draws below stay inside these ranges and needn't reach their ends.
All inputs are finite; a program needn't handle non-finite values.
Results may differ from the reference program's by a relative error of at most 0.022.
Values may be sent and summed in bfloat16 or wider, within the bound.
No kernel may reach another device: no remote copies, remote signals or barrier semaphores. Data moves between devices by JAX's collectives and lax.ppermute only.
A program may use at most 128 MiB of HBM per device.

```python
import math
import jax
import jax.numpy as jnp
from jax import lax

B = 1
T_SIZE = 4
C = 16
X = 128
Y = 128
Z = 128
MX = 64
MY = 64
MZ = 32


def shard_levels(key, dims, shards, smallest, largest):
    def one(axis_at, blocks):
        draws = jax.random.uniform(jax.random.fold_in(jax.random.fold_in(key, 6), axis_at), (blocks,), jnp.float32, smallest / len(shards), largest / len(shards))
        return jnp.repeat(jnp.exp(draws), dims[axis_at] // blocks).reshape((-1,) + (1,) * (len(dims) - axis_at - 1))

    loudness = one(*shards[0])
    for cut in shards[1:]:
        loudness = loudness * one(*cut)
    return loudness


def scatter_about(rng, shape, scale, most, pieces=(), held_as=jnp.bfloat16):
    loudness = shard_levels(rng, shape, pieces, -0.22, 0.18) if pieces else 1.0
    entries = jax.random.normal(rng, shape, jnp.float32) * scale * loudness
    return jnp.minimum(jnp.maximum(entries, -most), most).astype(held_as)


def setup_inputs(seed: int = 0) -> dict:
    streams_of = jax.random.split(jax.random.key(seed), 5)
    grid_field = scatter_about(streams_of[0], (B, T_SIZE, C, X, Y, Z), 1.0, 6.0, ((3, 16), (4, 32)))
    spectral_weight = scatter_about(streams_of[1], (C, C, MY, MZ, 2 * T_SIZE * MX), (C // 4) ** -0.5, 3.0, ((2, 16), (3, 32)))
    point_weight = scatter_about(streams_of[2], (C, C), C ** -0.5, 1.5)
    cotangent = scatter_about(streams_of[3], (B, T_SIZE, C, X, Y, Z), 1.0, 6.0, ((3, 16), (4, 32)))
    return {"grid_field": grid_field, "spectral_weight": spectral_weight, "point_weight": point_weight, "cotangent": cotangent}


root_two_over_pi = math.sqrt(2.0 / math.pi)
gelu_cubic = 0.044715

def signed_frequency(kept_count):
    ordinal = jnp.arange(kept_count, dtype=jnp.int32)
    return jnp.where(ordinal < kept_count // 2, ordinal, ordinal - kept_count)

def angle_grid(frequency, length):
    positions = jnp.arange(length, dtype=jnp.int32)
    residue = jnp.mod(frequency[:, None] * positions[None, :], length)
    return residue.astype(jnp.float32) * (2.0 * math.pi / length)

def rotation(angles, direction):
    cosine_part = jnp.cos(angles)
    sine_part = direction * jnp.sin(angles)
    return jnp.stack([jnp.stack([cosine_part, sine_part], -1), jnp.stack([-sine_part, cosine_part], -1)], 0)

def dft_tables():
    z_angles = angle_grid(jnp.arange(MZ, dtype=jnp.int32), Z)
    z_forward = jnp.stack([jnp.cos(z_angles).T, -jnp.sin(z_angles).T], -1).reshape(Z, 2 * MZ)
    z_backward = jnp.transpose(rotation(z_angles, 1.0), (1, 0, 3, 2)).reshape(2 * MZ, 2 * Z)
    t_angles = angle_grid(jnp.arange(T_SIZE, dtype=jnp.int32), T_SIZE)
    t_forward = jnp.transpose(rotation(t_angles, -1.0), (0, 2, 1, 3))
    t_backward = jnp.stack([jnp.cos(t_angles), -jnp.sin(t_angles)], 0)
    y_angles = angle_grid(signed_frequency(MY), Y)
    y_forward = jnp.transpose(rotation(y_angles, -1.0), (0, 2, 1, 3))
    y_backward = rotation(y_angles, 1.0)
    x_angles = angle_grid(signed_frequency(MX), X)
    x_forward = jnp.transpose(rotation(x_angles, -1.0), (0, 2, 1, 3))
    x_backward = rotation(x_angles, 1.0)
    return (z_forward.astype(jnp.bfloat16), z_backward.astype(jnp.bfloat16), t_forward, t_backward, y_forward.astype(jnp.bfloat16), y_backward.astype(jnp.bfloat16), x_forward.astype(jnp.bfloat16), x_backward.astype(jnp.bfloat16))

def mode_scaling(kz_index):
    return jnp.where(kz_index == 0, 1.0, 2.0).astype(jnp.float32) / float(X * Y * Z * T_SIZE)

def gelu_value(preact):
    inner_arg = root_two_over_pi * (preact + gelu_cubic * preact * preact * preact)
    return 0.5 * preact * (1.0 + jnp.tanh(inner_arg))

def gelu_slope(preact):
    inner_arg = root_two_over_pi * (preact + gelu_cubic * preact * preact * preact)
    hyper = jnp.tanh(inner_arg)
    return 0.5 * (1.0 + hyper) + 0.5 * preact * (1.0 - hyper * hyper) * root_two_over_pi * (1.0 + 3.0 * gelu_cubic * preact * preact)

def split_parts(array):
    extent = array.shape
    halved = array.reshape(extent[:-1] + (2, extent[-1] // 2))
    return (halved[..., 0, :], halved[..., 1, :])

def join_parts(real_part, imag_part):
    joined = jnp.stack([real_part, imag_part], -2)
    return joined.reshape(real_part.shape[:-1] + (2 * real_part.shape[-1],))

def to_modes(values, tables):
    z_forward, z_backward, t_forward, t_backward, y_forward, y_backward, x_forward, x_backward = tables
    spread = jnp.einsum('btcxyz,zk->btcxyk', values.astype(jnp.float32), z_forward.astype(jnp.float32))
    spread = spread.reshape(B, T_SIZE, C, X, Y, MZ, 2)
    turned = jnp.einsum('btcxyqp,ptks->bkcxyqs', spread, t_forward, precision=lax.Precision.HIGHEST).astype(jnp.bfloat16)
    along_y = jnp.einsum('bkcxyqp,pyjs->bkcxjqs', turned.astype(jnp.float32), y_forward.astype(jnp.float32)).astype(jnp.bfloat16)
    along_x = jnp.einsum('bkcxjqp,pxms->bcjqskm', along_y.astype(jnp.float32), x_forward.astype(jnp.float32)).astype(jnp.bfloat16)
    return along_x.reshape(B, C, MY, MZ, 2 * T_SIZE * MX)

def from_modes(spectrum_in, tables):
    z_forward, z_backward, t_forward, t_backward, y_forward, y_backward, x_forward, x_backward = tables
    sectioned = spectrum_in.astype(jnp.float32).reshape(B, C, MY, MZ, 2, T_SIZE, MX)
    along_x = jnp.einsum('bojqptm,pmxs->btoqjsx', sectioned, x_backward.astype(jnp.float32)).astype(jnp.bfloat16)
    along_y = jnp.einsum('btoqjpx,pjys->btoxqsy', along_x.astype(jnp.float32), y_backward.astype(jnp.float32)).astype(jnp.bfloat16)
    flattened = jnp.moveaxis(along_y.reshape(B, T_SIZE, C, X, 2 * MZ, Y), 2, 0)
    z_table = z_backward.astype(jnp.float32)

    def one_channel(segment):
        spread = jnp.einsum('btxky,kw->btxyw', segment.astype(jnp.float32), z_table)
        spread = spread.reshape(B, T_SIZE, X, Y, 2, Z)
        return jnp.einsum('btxypz,ptu->buxyz', spread, t_backward, precision=lax.Precision.HIGHEST)
    result = lax.map(one_channel, flattened)
    return jnp.moveaxis(result, 0, 2)

def per_row(function, arrays):
    shifted = tuple((jnp.moveaxis(operand, 2, 0) for operand in arrays))
    result = lax.map(function, shifted)
    return jax.tree.map(lambda member: jnp.moveaxis(member, 0, 2), result)

def mix_row(operands):
    spectrum_row, weight_row = operands
    spec_real, spec_imag = split_parts(spectrum_row.astype(jnp.float32))
    weight_real, weight_imag = split_parts(weight_row.astype(jnp.float32))
    real_part = jnp.einsum('bcqm,coqm->boqm', spec_real, weight_real) - jnp.einsum('bcqm,coqm->boqm', spec_imag, weight_imag)
    imag_part = jnp.einsum('bcqm,coqm->boqm', spec_real, weight_imag) + jnp.einsum('bcqm,coqm->boqm', spec_imag, weight_real)
    scaling = mode_scaling(jnp.arange(MZ, dtype=jnp.int32))[:, None]
    return join_parts(real_part * scaling, imag_part * scaling).astype(jnp.bfloat16)

def grads_row(operands):
    spectrum_row, weight_row, adjoint_row = operands
    spec_real, spec_imag = split_parts(spectrum_row.astype(jnp.float32))
    weight_real, weight_imag = split_parts(weight_row.astype(jnp.float32))
    adj_real, adj_imag = split_parts(adjoint_row.astype(jnp.float32))
    scaling = mode_scaling(jnp.arange(MZ, dtype=jnp.int32))[:, None]
    grad_real = jnp.einsum('bcqm,boqm->coqm', spec_real, adj_real) + jnp.einsum('bcqm,boqm->coqm', spec_imag, adj_imag)
    grad_imag = jnp.einsum('bcqm,boqm->coqm', spec_real, adj_imag) - jnp.einsum('bcqm,boqm->coqm', spec_imag, adj_real)
    back_real = jnp.einsum('boqm,coqm->bcqm', adj_real, weight_real) + jnp.einsum('boqm,coqm->bcqm', adj_imag, weight_imag)
    back_imag = jnp.einsum('boqm,coqm->bcqm', adj_imag, weight_real) - jnp.einsum('boqm,coqm->bcqm', adj_real, weight_imag)
    return (join_parts(grad_real * scaling, grad_imag * scaling).astype(jnp.bfloat16), join_parts(back_real * scaling, back_imag * scaling).astype(jnp.bfloat16))

def reference(grid_field, spectral_weight, point_weight, cotangent):
    tables = dft_tables()
    spectrum = to_modes(grid_field, tables)
    mixture = per_row(mix_row, (spectrum, spectral_weight))
    point_full = point_weight.astype(jnp.float32)
    preact = from_modes(mixture, tables) + jnp.einsum('btcxyz,co->btoxyz', grid_field.astype(jnp.float32), point_full)
    layer_out = gelu_value(preact).astype(jnp.bfloat16)
    slope_term = (cotangent.astype(jnp.float32) * gelu_slope(preact)).astype(jnp.bfloat16)
    adjoint = to_modes(slope_term, tables)
    grad_spectral, grad_modes = per_row(grads_row, (spectrum, spectral_weight, adjoint))
    grad_field = from_modes(grad_modes, tables) + jnp.einsum('btoxyz,co->btcxyz', slope_term.astype(jnp.float32), point_full)
    return (layer_out, grad_field.astype(jnp.bfloat16), grad_spectral)
```

```python
import math

import jax
import jax.numpy as jnp
import numpy as np
from jax import lax
from jax.experimental import pallas as pl
from jax.experimental.pallas import tpu as pltpu
from jax.sharding import PartitionSpec as P

T = 4
C = 16
X = 128
Y = 128
Z = 128
MX = 64
MY = 64
MZ = 32
GX = 16
GY = 32
XL = X // GX
YL = Y // GY
JL = MY // GX
LANES = 128

F32 = jnp.float32
BF16 = jnp.bfloat16

root_two_over_pi = math.sqrt(2.0 / math.pi)
gelu_cubic = 0.044715


def signed(kept):
    j = np.arange(kept)
    return np.where(j < kept // 2, j, j - kept)


def cos_sin(freq, length):
    q = np.mod(freq[:, None] * np.arange(length)[None, :], length)
    angle = q * (2.0 * np.pi / length)
    return np.cos(angle).astype(BF16), np.sin(angle).astype(BF16)


def tables():
    cz, sz = (a.astype(np.float64) for a in cos_sin(np.arange(MZ), Z))
    quarter = np.mod(np.arange(T)[:, None] * np.arange(T)[None, :], T)
    ct = np.array([1.0, 0.0, -1.0, 0.0])[quarter]
    st = np.array([0.0, 1.0, 0.0, -1.0])[quarter]
    both_cos = (
        cz[None, :, None, :] * ct[:, None, :, None] - sz[None, :, None, :] * st[:, None, :, None]
    )
    both_sin = (
        sz[None, :, None, :] * ct[:, None, :, None] + cz[None, :, None, :] * st[:, None, :, None]
    )
    zt_fwd = np.stack([both_cos, -both_sin], 1).reshape(T * 2 * MZ, T * Z)
    zt_bwd = zt_fwd

    cy, sy = (a.astype(np.float64) for a in cos_sin(signed(MY), Y))
    fwd = np.empty((MY, 2, Y, 2))
    fwd[:, 0, :, 0] = cy
    fwd[:, 0, :, 1] = sy
    fwd[:, 1, :, 0] = -sy
    fwd[:, 1, :, 1] = cy
    y_fwd = fwd.reshape(GX, JL, 2, Y * 2).transpose(1, 2, 0, 3).reshape(MY * 2, Y * 2)
    bwd = np.empty((Y, 2, MY, 2))
    bwd[:, 0, :, 0] = cy.T
    bwd[:, 0, :, 1] = -sy.T
    bwd[:, 1, :, 0] = sy.T
    bwd[:, 1, :, 1] = cy.T
    y_bwd = bwd.reshape(Y * 2, MY * 2)

    cx, sx = (a.astype(np.float64) for a in cos_sin(signed(MX), X))
    fwd = np.empty((X, 2, 2, MX))
    fwd[:, 0, 0, :] = cx.T
    fwd[:, 1, 0, :] = sx.T
    fwd[:, 0, 1, :] = -sx.T
    fwd[:, 1, 1, :] = cx.T
    x_fwd = fwd.reshape(X * 2, 2 * MX)
    bwd = np.empty((X, 2, 2, MX))
    bwd[:, 0, 0, :] = cx.T
    bwd[:, 0, 1, :] = -sx.T
    bwd[:, 1, 0, :] = sx.T
    bwd[:, 1, 1, :] = cx.T
    x_bwd = bwd.reshape(GX, XL, 2, 2 * MX).transpose(1, 2, 0, 3).reshape(X * 2, 2 * MX)
    return tuple(a.astype(BF16) for a in (zt_fwd, zt_bwd, y_fwd, y_bwd, x_fwd, x_bwd))


def dot(left, right, left_dim=1, right_dim=0):
    return lax.dot_general(
        left, right, (((left_dim,), (right_dim,)), ((), ())), preferred_element_type=F32
    )


def swap_bit(low, high, step):
    lane = lax.broadcasted_iota(jnp.int32, low.shape, 1)
    upper = (lane & step) != 0
    first = jnp.where(upper, pltpu.roll(high, step, 1), low)
    second = jnp.where(upper, high, pltpu.roll(low, LANES - step, 1))
    return first, second


def swap_eight(parts):
    parts = list(parts)
    for step in (1, 2, 4):
        for i in range(8):
            if not i & step:
                parts[i], parts[i | step] = swap_bit(parts[i], parts[i | step], step)
    return parts


def gelu_parts(pre):
    inner = root_two_over_pi * (pre + gelu_cubic * pre * pre * pre)
    hyper = jnp.tanh(inner)
    value = 0.5 * pre * (1.0 + hyper)
    slope = 0.5 * (1.0 + hyper) + 0.5 * pre * (1.0 - hyper * hyper) * root_two_over_pi * (
        1.0 + 3.0 * gelu_cubic * pre * pre
    )
    return value, slope


def cells_of(wide_ref, y):
    return jnp.concatenate(
        [wide_ref[pl.ds(t * C * XL * YL + y, C * XL, stride=YL), :] for t in range(T)], 1
    )


def put_cells(wide_ref, y, value):
    for t in range(T):
        wide_ref[pl.ds(t * C * XL * YL + y, C * XL, stride=YL), :] = value[:, t * Z : (t + 1) * Z]


def pack(spread_ref, out_ref):
    for k in range(spread_ref.shape[0]):
        out_ref[:, k * LANES : (k + 1) * LANES] = spread_ref[k].astype(BF16)


def unpack(in_ref, spread_ref):
    for k in range(spread_ref.shape[0]):
        spread_ref[k] = in_ref[:, k * LANES : (k + 1) * LANES].astype(F32)


def put_modes(spread_ref, y, cells, zt_fwd):
    turned = dot(zt_fwd, cells, 1, 1)
    for kt in range(T):
        for p in range(2):
            row = (kt * 2 + p) * MZ
            spread_ref[kt, pl.ds(y * 2 + p, MZ, stride=2 * YL), :] = turned[row : row + MZ]


def modes_of(spread_ref, y):
    return jnp.concatenate(
        [
            spread_ref[kt, pl.ds(y * 2 + p, MZ, stride=2 * YL), :]
            for kt in range(T)
            for p in range(2)
        ],
        0,
    )


def open_kernel(field_ref, zt_ref, out_ref, wide, spread):
    wide[...] = field_ref[...].astype(F32)
    for y in range(YL):
        put_modes(spread, y, cells_of(wide, y).astype(BF16), zt_ref[...])
    pack(spread, out_ref)


def y_forward_kernel(in_ref, table_ref, out_ref, spread):
    along_y = dot(table_ref[...], in_ref[...])
    for low in range(2):
        parts = [
            along_y[
                j * 2 * GX : (j + 1) * 2 * GX,
                (kth * 2 + low) * LANES : (kth * 2 + low + 1) * LANES,
            ]
            for kth in range(2)
            for j in range(JL)
        ]
        for x, part in enumerate(swap_eight(parts)):
            for s in range(2):
                spread[low, pl.ds(x * 2 + s, GX, stride=2 * XL), :] = part[s * GX : (s + 1) * GX]
    pack(spread, out_ref)


def to_spectrum(in_ref, x_fwd_ref):
    low, high = (
        dot(in_ref[:, k * LANES : (k + 1) * LANES], x_fwd_ref[...], 0, 0)
        .astype(BF16)
        .astype(F32)
        for k in range(2)
    )
    return swap_bit(low, high, MX)


def from_spectrum(real, imag, x_bwd_ref, out_ref, spread):
    for low, modes in enumerate(swap_bit(real, imag, MX)):
        along_x = dot(x_bwd_ref[...], modes.astype(BF16), 1, 1)
        parts = [along_x[x * 2 * GX : (x + 1) * 2 * GX] for x in range(XL)]
        for i, part in enumerate(swap_eight(parts)):
            kth, j = divmod(i, JL)
            for s in range(2):
                spread[kth * 2 + low, pl.ds(j * 2 + s, GX, stride=2 * JL), :] = part[
                    s * GX : (s + 1) * GX
                ]
    pack(spread, out_ref)


def weight_parts(w_ref, c):
    w = w_ref[c].astype(F32).reshape(C, 2, 8, LANES)
    return w[:, 0], w[:, 1]


def at_channel(ref, c):
    return ref[pl.ds(pl.multiple_of(c * 8, 8), 8), :]


def mix_kernel(
    in_ref, w_ref, scale_ref, x_fwd_ref, x_bwd_ref, out_ref, real_ref, imag_ref, spread
):
    real, imag = to_spectrum(in_ref, x_fwd_ref)
    real_ref[...] = real
    imag_ref[...] = imag

    def add(c, total):
        s_real = at_channel(real_ref, c)[None]
        s_imag = at_channel(imag_ref, c)[None]
        w_real, w_imag = weight_parts(w_ref, c)
        return (
            total[0] + (s_real * w_real - s_imag * w_imag),
            total[1] + (s_real * w_imag + s_imag * w_real),
        )

    zero = jnp.zeros((C, 8, LANES), F32)
    mix_real, mix_imag = lax.fori_loop(0, C, add, (zero, zero))
    scale = scale_ref[0]
    from_spectrum(
        (mix_real * scale).reshape(C * 8, LANES),
        (mix_imag * scale).reshape(C * 8, LANES),
        x_bwd_ref,
        out_ref,
        spread,
    )


def back_kernel(
    in_ref,
    w_ref,
    scale_ref,
    x_fwd_ref,
    x_bwd_ref,
    out_ref,
    real_ref,
    imag_ref,
    back_real,
    back_imag,
    spread,
):
    real, imag = to_spectrum(in_ref, x_fwd_ref)
    real_ref[...] = real
    imag_ref[...] = imag

    def one(c, carry):
        a_real = real_ref[...].reshape(C, 8, LANES)
        a_imag = imag_ref[...].reshape(C, 8, LANES)
        w_real, w_imag = weight_parts(w_ref, c)
        row = pl.ds(pl.multiple_of(c * 8, 8), 8)
        back_real[row, :] = jnp.sum(a_real * w_real + a_imag * w_imag, 0)
        back_imag[row, :] = jnp.sum(a_imag * w_real - a_real * w_imag, 0)
        return carry

    lax.fori_loop(0, C, one, 0)
    scale = scale_ref[0]
    from_spectrum(back_real[...] * scale, back_imag[...] * scale, x_bwd_ref, out_ref, spread)


def grad_kernel(s_real_ref, s_imag_ref, a_real_ref, a_imag_ref, scale_ref, out_ref):
    def one(c, carry):
        s_real = (at_channel(s_real_ref, c) * scale_ref[0])[None]
        s_imag = (at_channel(s_imag_ref, c) * scale_ref[0])[None]
        a_real = a_real_ref[...].reshape(C, 1, 8, LANES)
        a_imag = a_imag_ref[...].reshape(C, 1, 8, LANES)
        both = jnp.concatenate(
            [s_real * a_real + s_imag * a_imag, s_real * a_imag - s_imag * a_real], 1
        )
        out_ref[c] = both.reshape(C * 2 * 8, LANES).astype(BF16)
        return carry

    lax.fori_loop(0, C, one, 0)


def y_backward_kernel(in_ref, table_ref, out_ref):
    out_ref[...] = dot(table_ref[...], in_ref[...]).astype(BF16)


def point_kernel(field_ref, cotangent_ref, point_ref, point_out, cotangent_out, wide, other):
    wide[...] = field_ref[...].astype(F32)
    other[...] = cotangent_ref[...].astype(F32)
    for y in range(YL):
        point_out[y] = dot(point_ref[...], cells_of(wide, y).astype(BF16))
        cotangent_out[y] = cells_of(other, y).astype(BF16)


def cell_kernel(
    in_ref, point_ref, cotangent_ref, zt_bwd_ref, zt_fwd_ref, out_ref, slope_ref, layer_ref, spread
):
    unpack(in_ref, spread)
    modes = [modes_of(spread, y).astype(BF16) for y in range(YL)]
    for y in range(YL):
        pre = dot(modes[y], zt_bwd_ref[...], 0, 0) + point_ref[y]
        value, slope = gelu_parts(pre)
        layer_ref[y] = value.astype(BF16)
        slope_ref[y] = (cotangent_ref[y].astype(F32) * slope).astype(BF16)
    for y in range(YL):
        put_modes(spread, y, slope_ref[y], zt_fwd_ref[...])
    pack(spread, out_ref)


def after_kernel(slope_ref, layer_ref, point_ref, point_out, layer_out, wide):
    for y in range(YL):
        point_out[y] = dot(point_ref[...], slope_ref[y])
        put_cells(wide, y, layer_ref[y].astype(F32))
    layer_out[...] = wide[...].astype(BF16)


def close_kernel(in_ref, point_ref, zt_bwd_ref, out_ref, spread, wide):
    unpack(in_ref, spread)
    for y in range(YL):
        modes = modes_of(spread, y).astype(BF16)
        put_cells(wide, y, dot(modes, zt_bwd_ref[...], 0, 0) + point_ref[y])
    out_ref[...] = wide[...].astype(BF16)


ROWS = T * C * XL * YL
ZT = (MZ * YL * 2, T * LANES)
AFTER_Y = (GX * XL * 2, 2 * LANES)
AFTER_X = (GX * JL * 2, T * LANES)
ZT_SPREAD = (T, MZ * YL * 2, LANES)
Y_SPREAD = (2, GX * XL * 2, LANES)
X_SPREAD = (T, GX * JL * 2, LANES)
CELLS = (YL, C * XL, T * Z)
PARTS = (C * 8, LANES)


def call(kernel, outs, operands, scratch=(), scalars=(), flops=10**8):
    vmem = pl.BlockSpec(memory_space=pltpu.VMEM)
    smem = pl.BlockSpec(memory_space=pltpu.SMEM)
    single = len(outs) == 1
    specs = [smem if i in scalars else vmem for i in range(len(operands))]
    moved = sum(math.prod(o.shape) * o.dtype.itemsize for o in list(outs) + list(operands))
    return pl.pallas_call(
        kernel,
        out_shape=outs[0] if single else tuple(outs),
        in_specs=specs,
        out_specs=vmem if single else (vmem,) * len(outs),
        scratch_shapes=[pltpu.VMEM(shape, F32) for shape in scratch],
        cost_estimate=pl.CostEstimate(flops=flops, bytes_accessed=moved, transcendentals=0),
        compiler_params=pltpu.CompilerParams(vmem_limit_bytes=24 * 1024 * 1024),
    )(*operands)


def shaped(shape, dtype=BF16):
    return jax.ShapeDtypeStruct(shape, dtype)


def exchange(block, axis):
    return lax.all_to_all(block, axis, split_axis=0, concat_axis=0, tiled=True)


def on_device(grid_field, spectral_weight, point_weight, cotangent):
    zt_fwd, zt_bwd, y_fwd, y_bwd, x_fwd, x_bwd = (jnp.asarray(a) for a in tables())
    field = grid_field.reshape(ROWS, Z)
    cotan = cotangent.reshape(ROWS, Z)
    weight = (
        spectral_weight.reshape(C, C, JL, 4, LANES)
        .transpose(0, 1, 3, 2, 4)
        .reshape(C, C * 2 * 8, LANES)
    )
    eye = jnp.eye(XL, dtype=BF16)
    point_back = jnp.kron(point_weight, eye)
    point_fwd = jnp.kron(point_weight.T, eye)
    kz = lax.axis_index("gy")
    scale = (jnp.where(kz == 0, 1.0, 2.0).astype(F32) / float(X * Y * Z * T)).reshape(1)
    wide = (ROWS, Z)

    opened = call(open_kernel, [shaped(ZT)], [field, zt_fwd], [wide, ZT_SPREAD])
    opened = exchange(opened, "gy")
    point, cotan = call(
        point_kernel,
        [shaped(CELLS, F32), shaped(CELLS)],
        [field, cotan, point_fwd],
        [wide, wide],
    )
    halved = call(y_forward_kernel, [shaped(AFTER_Y)], [opened, y_fwd], [Y_SPREAD])
    halved = exchange(halved, "gx")
    mixed, spec_real, spec_imag = call(
        mix_kernel,
        [shaped(AFTER_X), shaped(PARTS, F32), shaped(PARTS, F32)],
        [halved, weight, scale, x_fwd, x_bwd],
        [X_SPREAD],
        (2,),
    )
    mixed = exchange(mixed, "gx")
    along_y = call(y_backward_kernel, [shaped(ZT)], [mixed, y_bwd])
    along_y = exchange(along_y, "gy")
    turned, slope, layer = call(
        cell_kernel,
        [shaped(ZT), shaped(CELLS), shaped(CELLS)],
        [along_y, point, cotan, zt_bwd, zt_fwd],
        [ZT_SPREAD],
    )
    turned = exchange(turned, "gy")
    point, layer_out = call(
        after_kernel, [shaped(CELLS, F32), shaped(wide)], [slope, layer, point_back], [wide]
    )
    halved = call(y_forward_kernel, [shaped(AFTER_Y)], [turned, y_fwd], [Y_SPREAD])
    halved = exchange(halved, "gx")
    back, adj_real, adj_imag = call(
        back_kernel,
        [shaped(AFTER_X), shaped(PARTS, F32), shaped(PARTS, F32)],
        [halved, weight, scale, x_fwd, x_bwd],
        [PARTS, PARTS, X_SPREAD],
        (2,),
    )
    back = exchange(back, "gx")
    grad_spectral = call(
        grad_kernel,
        [shaped((C, C * 2 * 8, LANES))],
        [spec_real, spec_imag, adj_real, adj_imag, scale],
        (),
        (4,),
    )
    along_y = call(y_backward_kernel, [shaped(ZT)], [back, y_bwd])
    along_y = exchange(along_y, "gy")
    grad_field = call(close_kernel, [shaped(wide)], [along_y, point, zt_bwd], [ZT_SPREAD, wide])

    grad_spectral = (
        grad_spectral.reshape(C, C, 4, JL, LANES)
        .transpose(0, 1, 3, 2, 4)
        .reshape(spectral_weight.shape)
    )
    return (
        layer_out.reshape(grid_field.shape),
        grad_field.reshape(grid_field.shape),
        grad_spectral,
    )


def solution(mesh):
    field = P(None, None, None, "gx", "gy", None)
    modes = P(None, None, "gx", "gy", None)
    return jax.shard_map(
        on_device,
        mesh=mesh,
        in_specs=(field, modes, P(), field),
        out_specs=(field, field, modes),
        check_vma=False,
    )
```

```python
import math

import jax
import jax.numpy as jnp
import numpy as np
from jax import lax
from jax.experimental import pallas as pl
from jax.experimental.pallas import tpu as pltpu
from jax.sharding import PartitionSpec as P

T = 4
C = 16
X = 128
Y = 128
Z = 128
MX = 64
MY = 64
MZ = 32
GX = 16
GY = 32
XL = X // GX
YL = Y // GY
JL = MY // GX
LANES = 128
GY_ORDER = [y * 4 + z for y in (0, 4, 2, 6, 1, 5, 3, 7) for z in range(4)]

F32 = jnp.float32
BF16 = jnp.bfloat16

root_two_over_pi = math.sqrt(2.0 / math.pi)
gelu_cubic = 0.044715


def signed(kept):
    j = np.arange(kept)
    return np.where(j < kept // 2, j, j - kept)


def cos_sin(freq, length):
    q = np.mod(freq[:, None] * np.arange(length)[None, :], length)
    angle = q * (2.0 * np.pi / length)
    return np.cos(angle).astype(BF16), np.sin(angle).astype(BF16)


def tables():
    cz, sz = (a.astype(np.float64) for a in cos_sin(np.arange(MZ), Z))
    quarter = np.mod(np.arange(T)[:, None] * np.arange(T)[None, :], T)
    ct = np.array([1.0, 0.0, -1.0, 0.0])[quarter]
    st = np.array([0.0, 1.0, 0.0, -1.0])[quarter]
    cz, sz = cz[GY_ORDER], sz[GY_ORDER]
    both_cos = (
        cz[None, :, None, :] * ct[:, None, :, None] - sz[None, :, None, :] * st[:, None, :, None]
    )
    both_sin = (
        sz[None, :, None, :] * ct[:, None, :, None] + cz[None, :, None, :] * st[:, None, :, None]
    )
    zt_fwd = np.stack([both_cos, -both_sin], 1).reshape(T * 2 * MZ, T * Z)
    zt_bwd = zt_fwd

    cy, sy = (a.astype(np.float64) for a in cos_sin(signed(MY), Y))
    fwd = np.empty((MY, 2, Y, 2))
    fwd[:, 0, :, 0] = cy
    fwd[:, 0, :, 1] = sy
    fwd[:, 1, :, 0] = -sy
    fwd[:, 1, :, 1] = cy
    fwd = fwd.reshape(MY * 2, GY, YL * 2)[:, GY_ORDER]
    y_fwd = fwd.reshape(GX, JL, 2, Y * 2).transpose(1, 2, 0, 3).reshape(MY * 2, Y * 2)
    bwd = np.empty((Y, 2, MY, 2))
    bwd[:, 0, :, 0] = cy.T
    bwd[:, 0, :, 1] = -sy.T
    bwd[:, 1, :, 0] = sy.T
    bwd[:, 1, :, 1] = cy.T
    y_bwd = bwd.reshape(GY, YL * 2, MY * 2)[GY_ORDER].reshape(Y * 2, MY * 2)

    cx, sx = (a.astype(np.float64) for a in cos_sin(signed(MX), X))
    fwd = np.empty((X, 2, 2, MX))
    fwd[:, 0, 0, :] = cx.T
    fwd[:, 1, 0, :] = sx.T
    fwd[:, 0, 1, :] = -sx.T
    fwd[:, 1, 1, :] = cx.T
    x_fwd = fwd.reshape(X * 2, 2 * MX)
    bwd = np.empty((X, 2, 2, MX))
    bwd[:, 0, 0, :] = cx.T
    bwd[:, 0, 1, :] = -sx.T
    bwd[:, 1, 0, :] = sx.T
    bwd[:, 1, 1, :] = cx.T
    x_bwd = bwd.reshape(GX, XL, 2, 2 * MX).transpose(1, 2, 0, 3).reshape(X * 2, 2 * MX)
    return tuple(a.astype(BF16) for a in (zt_fwd, zt_bwd, y_fwd, y_bwd, x_fwd, x_bwd))


def dot(left, right, left_dim=1, right_dim=0):
    return lax.dot_general(
        left, right, (((left_dim,), (right_dim,)), ((), ())), preferred_element_type=F32
    )


def swap_bit(low, high, step):
    lane = lax.broadcasted_iota(jnp.int32, low.shape, 1)
    upper = (lane & step) != 0
    first = jnp.where(upper, pltpu.roll(high, step, 1), low)
    second = jnp.where(upper, high, pltpu.roll(low, LANES - step, 1))
    return first, second


def swap_eight(parts):
    parts = list(parts)
    for step in (1, 2, 4):
        for i in range(8):
            if not i & step:
                parts[i], parts[i | step] = swap_bit(parts[i], parts[i | step], step)
    return parts


def gelu_parts(pre):
    inner = root_two_over_pi * (pre + gelu_cubic * pre * pre * pre)
    hyper = jnp.tanh(inner)
    value = 0.5 * pre * (1.0 + hyper)
    slope = 0.5 * (1.0 + hyper) + 0.5 * pre * (1.0 - hyper * hyper) * root_two_over_pi * (
        1.0 + 3.0 * gelu_cubic * pre * pre
    )
    return value, slope


def cells_of(wide_ref, y):
    return jnp.concatenate(
        [wide_ref[pl.ds(t * C * XL * YL + y, C * XL, stride=YL), :] for t in range(T)], 1
    )


def put_cells(wide_ref, y, value):
    for t in range(T):
        wide_ref[pl.ds(t * C * XL * YL + y, C * XL, stride=YL), :] = value[:, t * Z : (t + 1) * Z]


def pack(spread_ref, out_ref):
    for k in range(spread_ref.shape[0]):
        out_ref[:, k * LANES : (k + 1) * LANES] = spread_ref[k].astype(BF16)


def unpack(in_ref, spread_ref):
    for k in range(spread_ref.shape[0]):
        spread_ref[k] = in_ref[:, k * LANES : (k + 1) * LANES].astype(F32)


def put_modes(spread_ref, y, cells, zt_fwd):
    turned = dot(zt_fwd, cells, 1, 1)
    for kt in range(T):
        for p in range(2):
            row = (kt * 2 + p) * MZ
            spread_ref[kt, pl.ds(y * 2 + p, MZ, stride=2 * YL), :] = turned[row : row + MZ]


def modes_of(spread_ref, y):
    return jnp.concatenate(
        [
            spread_ref[kt, pl.ds(y * 2 + p, MZ, stride=2 * YL), :]
            for kt in range(T)
            for p in range(2)
        ],
        0,
    )


def open_kernel(field_hbm, zt_hbm, out_ref, field, zt_fwd, wide, spread, sems):
    rows = C * XL * YL
    copies = [pltpu.make_async_copy(zt_hbm, zt_fwd, sems.at[T])]
    for t in range(T):
        part = pl.ds(t * rows, rows)
        copies.append(pltpu.make_async_copy(field_hbm.at[part], field.at[part], sems.at[t]))
    for copy in copies:
        copy.start()
    for t in range(T):
        copies[1 + t].wait()
        wide[t * rows : (t + 1) * rows] = field[t * rows : (t + 1) * rows].astype(F32)
    copies[0].wait()
    for y in range(YL):
        put_modes(spread, y, cells_of(wide, y).astype(BF16), zt_fwd[...])
    pack(spread, out_ref)


def y_forward_kernel(in_ref, table_ref, out_ref, spread):
    along_y = dot(table_ref[...], in_ref[...])
    for low in range(2):
        parts = [
            along_y[
                j * 2 * GX : (j + 1) * 2 * GX,
                (kth * 2 + low) * LANES : (kth * 2 + low + 1) * LANES,
            ]
            for kth in range(2)
            for j in range(JL)
        ]
        for x, part in enumerate(swap_eight(parts)):
            for s in range(2):
                spread[low, pl.ds(x * 2 + s, GX, stride=2 * XL), :] = part[s * GX : (s + 1) * GX]
    pack(spread, out_ref)


def to_spectrum(in_ref, x_fwd_ref):
    low, high = (
        dot(in_ref[:, k * LANES : (k + 1) * LANES], x_fwd_ref[...], 0, 0)
        .astype(BF16)
        .astype(F32)
        for k in range(2)
    )
    return swap_bit(low, high, MX)


def from_spectrum(real, imag, x_bwd_ref, out_ref, spread):
    for low, modes in enumerate(swap_bit(real, imag, MX)):
        along_x = dot(x_bwd_ref[...], modes.astype(BF16), 1, 1)
        parts = [along_x[x * 2 * GX : (x + 1) * 2 * GX] for x in range(XL)]
        for i, part in enumerate(swap_eight(parts)):
            kth, j = divmod(i, JL)
            for s in range(2):
                spread[kth * 2 + low, pl.ds(j * 2 + s, GX, stride=2 * JL), :] = part[
                    s * GX : (s + 1) * GX
                ]
    pack(spread, out_ref)


def weight_parts(w_ref, c):
    w = w_ref[c].astype(F32).reshape(C, 2, 8, LANES)
    return w[:, 0], w[:, 1]


def at_channel(ref, c):
    return ref[pl.ds(pl.multiple_of(c * 8, 8), 8), :]


def mix_kernel(
    in_ref, w_ref, scale_ref, x_fwd_ref, x_bwd_ref, out_ref, real_ref, imag_ref, spread
):
    real, imag = to_spectrum(in_ref, x_fwd_ref)
    real_ref[...] = real
    imag_ref[...] = imag

    def add(c, total):
        s_real = at_channel(real_ref, c)[None]
        s_imag = at_channel(imag_ref, c)[None]
        w_real, w_imag = weight_parts(w_ref, c)
        return (
            total[0] + (s_real * w_real - s_imag * w_imag),
            total[1] + (s_real * w_imag + s_imag * w_real),
        )

    zero = jnp.zeros((C, 8, LANES), F32)
    mix_real, mix_imag = lax.fori_loop(0, C, add, (zero, zero))
    scale = scale_ref[0]
    from_spectrum(
        (mix_real * scale).reshape(C * 8, LANES),
        (mix_imag * scale).reshape(C * 8, LANES),
        x_bwd_ref,
        out_ref,
        spread,
    )


def back_kernel(
    in_ref,
    w_ref,
    scale_ref,
    x_fwd_ref,
    x_bwd_ref,
    s_real_ref,
    s_imag_ref,
    out_ref,
    grad_hbm,
    real_ref,
    imag_ref,
    back_real,
    back_imag,
    spread,
    grad,
    sem,
):
    real, imag = to_spectrum(in_ref, x_fwd_ref)
    real_ref[...] = real
    imag_ref[...] = imag

    def outer(c, carry):
        s_real = (at_channel(s_real_ref, c).astype(F32) * scale_ref[0])[None, None]
        s_imag = (at_channel(s_imag_ref, c).astype(F32) * scale_ref[0])[None, None]
        a_real = real_ref[...].reshape(C, 1, 8, LANES)
        a_imag = imag_ref[...].reshape(C, 1, 8, LANES)
        both = jnp.concatenate(
            [s_real * a_real + s_imag * a_imag, s_real * a_imag - s_imag * a_real], 1
        )
        grad[c] = both.reshape(C * 2 * 8, LANES).astype(BF16)
        return carry

    lax.fori_loop(0, C, outer, 0)
    send = pltpu.make_async_copy(grad, grad_hbm, sem)
    send.start()

    def one(c, carry):
        a_real = real_ref[...].reshape(C, 8, LANES)
        a_imag = imag_ref[...].reshape(C, 8, LANES)
        w_real, w_imag = weight_parts(w_ref, c)
        row = pl.ds(pl.multiple_of(c * 8, 8), 8)
        back_real[row, :] = jnp.sum(a_real * w_real + a_imag * w_imag, 0)
        back_imag[row, :] = jnp.sum(a_imag * w_real - a_real * w_imag, 0)
        return carry

    lax.fori_loop(0, C, one, 0)
    scale = scale_ref[0]
    from_spectrum(back_real[...] * scale, back_imag[...] * scale, x_bwd_ref, out_ref, spread)
    send.wait()


def y_backward_kernel(in_ref, table_ref, out_ref):
    out_ref[...] = dot(table_ref[...], in_ref[...]).astype(BF16)


def point_table(point_ref, back):
    shape = (C * XL, C)
    row = lax.broadcasted_iota(jnp.int32, shape, 0)
    pick = (row // XL == lax.broadcasted_iota(jnp.int32, shape, 1)).astype(F32).astype(BF16)
    half = dot(pick, point_ref[...], 1, 0 if back else 1).astype(BF16)
    full = dot(half, pick, 1, 1)
    row = lax.broadcasted_iota(jnp.int32, full.shape, 0)
    column = lax.broadcasted_iota(jnp.int32, full.shape, 1)
    return jnp.where(row % XL == column % XL, full, 0.0).astype(BF16)


def cell_kernel(
    in_ref,
    field_hbm,
    cotangent_hbm,
    point_ref,
    zt_bwd_ref,
    zt_fwd_ref,
    out_ref,
    slope_ref,
    layer_hbm,
    field,
    cotangent,
    wide,
    other,
    spread,
    sems,
):
    copies = [
        pltpu.make_async_copy(field_hbm, field, sems.at[0]),
        pltpu.make_async_copy(cotangent_hbm, cotangent, sems.at[1]),
    ]
    for copy in copies:
        copy.start()
    point = point_table(point_ref, False)
    unpack(in_ref, spread)
    modes = [modes_of(spread, y).astype(BF16) for y in range(YL)]
    copies[0].wait()
    wide[...] = field[...].astype(F32)
    copies[1].wait()
    other[...] = cotangent[...].astype(F32)
    for y in range(YL):
        pre = dot(modes[y], zt_bwd_ref[...], 0, 0) + dot(point, cells_of(wide, y).astype(BF16))
        value, slope = gelu_parts(pre)
        put_cells(wide, y, value)
        slope_ref[y] = (cells_of(other, y) * slope).astype(BF16)
    field[...] = wide[...].astype(BF16)
    send = pltpu.make_async_copy(field, layer_hbm, sems.at[2])
    send.start()
    for y in range(YL):
        put_modes(spread, y, slope_ref[y], zt_fwd_ref[...])
    pack(spread, out_ref)
    send.wait()


def close_kernel(in_ref, slope_ref, point_ref, zt_bwd_ref, out_ref, spread, wide):
    point = point_table(point_ref, True)
    unpack(in_ref, spread)
    for y in range(YL):
        modes = modes_of(spread, y).astype(BF16)
        put_cells(wide, y, dot(modes, zt_bwd_ref[...], 0, 0) + dot(point, slope_ref[y]))
    out_ref[...] = wide[...].astype(BF16)


ROWS = T * C * XL * YL
ZT = (MZ * YL * 2, T * LANES)
AFTER_Y = (GX * XL * 2, 2 * LANES)
AFTER_X = (GX * JL * 2, T * LANES)
ZT_SPREAD = (T, MZ * YL * 2, LANES)
Y_SPREAD = (2, GX * XL * 2, LANES)
X_SPREAD = (T, GX * JL * 2, LANES)
CELLS = (YL, C * XL, T * Z)
PARTS = (C * 8, LANES)


WIDE = (ROWS, Z)
GRAD = (C, C * 2 * 8, LANES)


def vmem(shape, dtype=F32):
    return pltpu.VMEM(shape, dtype)


def call(kernel, outs, operands, scratch=(), scalars=(), far=(), far_outs=(), flops=10**8):
    near = pl.BlockSpec(memory_space=pltpu.VMEM)
    smem = pl.BlockSpec(memory_space=pltpu.SMEM)
    anywhere = pl.BlockSpec(memory_space=pltpu.HBM)
    specs = [
        smem if i in scalars else anywhere if i in far else near for i in range(len(operands))
    ]
    out_specs = tuple(anywhere if i in far_outs else near for i in range(len(outs)))
    single = len(outs) == 1
    moved = sum(math.prod(o.shape) * o.dtype.itemsize for o in list(outs) + list(operands))
    return pl.pallas_call(
        kernel,
        out_shape=outs[0] if single else tuple(outs),
        in_specs=specs,
        out_specs=out_specs[0] if single else out_specs,
        scratch_shapes=list(scratch),
        cost_estimate=pl.CostEstimate(flops=flops, bytes_accessed=moved, transcendentals=0),
        compiler_params=pltpu.CompilerParams(vmem_limit_bytes=16 * 1024 * 1024),
    )(*operands)


def shaped(shape, dtype=BF16):
    return jax.ShapeDtypeStruct(shape, dtype)


def exchange(block, axis):
    groups = [GY_ORDER] if axis == "gy" else None
    return lax.all_to_all(
        block, axis, split_axis=0, concat_axis=0, axis_index_groups=groups, tiled=True
    )


def open_stage(field, zt_fwd):
    scratch = [vmem(WIDE, BF16), vmem(ZT, BF16), vmem(WIDE), vmem(ZT_SPREAD)]
    scratch.append(pltpu.SemaphoreType.DMA((T + 1,)))
    return call(open_kernel, [shaped(ZT)], [field, zt_fwd], scratch, far=(0, 1))


def y_forward_stage(block, y_fwd):
    return call(y_forward_kernel, [shaped(AFTER_Y)], [block, y_fwd], [vmem(Y_SPREAD)])


def mix_stage(block, weight, scale, x_fwd, x_bwd):
    return call(
        mix_kernel,
        [shaped(AFTER_X), shaped(PARTS, F32), shaped(PARTS, F32)],
        [block, weight, scale, x_fwd, x_bwd],
        [vmem(X_SPREAD)],
        scalars=(2,),
    )


def y_backward_stage(block, y_bwd):
    return call(y_backward_kernel, [shaped(ZT)], [block, y_bwd])


def cell_stage(block, field, cotangent, point_weight, zt_bwd, zt_fwd):
    scratch = [vmem(WIDE, BF16), vmem(WIDE, BF16), vmem(WIDE), vmem(WIDE), vmem(ZT_SPREAD)]
    scratch.append(pltpu.SemaphoreType.DMA((3,)))
    return call(
        cell_kernel,
        [shaped(ZT), shaped(CELLS), shaped(WIDE)],
        [block, field, cotangent, point_weight, zt_bwd, zt_fwd],
        scratch,
        far=(1, 2),
        far_outs=(2,),
    )


def back_stage(block, weight, scale, x_fwd, x_bwd, spec_real, spec_imag):
    scratch = [vmem(PARTS)] * 4 + [vmem(X_SPREAD), vmem(GRAD, BF16), pltpu.SemaphoreType.DMA]
    return call(
        back_kernel,
        [shaped(AFTER_X), shaped(GRAD)],
        [block, weight, scale, x_fwd, x_bwd, spec_real, spec_imag],
        scratch,
        scalars=(2,),
        far_outs=(1,),
    )


def close_stage(block, slope, point_weight, zt_bwd):
    return call(
        close_kernel,
        [shaped(WIDE)],
        [block, slope, point_weight, zt_bwd],
        [vmem(ZT_SPREAD), vmem(WIDE)],
    )


def on_device(grid_field, spectral_weight, point_weight, cotangent):
    zt_fwd, zt_bwd, y_fwd, y_bwd, x_fwd, x_bwd = (jnp.asarray(a) for a in tables())
    field = grid_field.reshape(WIDE)
    cotan = cotangent.reshape(WIDE)
    weight = spectral_weight.reshape(C, C, JL, 4, LANES).transpose(0, 1, 3, 2, 4).reshape(GRAD)
    kz = lax.axis_index("gy")
    scale = (jnp.where(kz == 0, 1.0, 2.0).astype(F32) / float(X * Y * Z * T)).reshape(1)

    opened = open_stage(field, zt_fwd)
    opened, scale = lax.optimization_barrier((opened, scale))
    halved = y_forward_stage(exchange(opened, "gy"), y_fwd)
    mixed, spec_real, spec_imag = mix_stage(exchange(halved, "gx"), weight, scale, x_fwd, x_bwd)
    along_y = y_backward_stage(exchange(mixed, "gx"), y_bwd)
    turned, slope, layer_out = cell_stage(
        exchange(along_y, "gy"), field, cotan, point_weight, zt_bwd, zt_fwd
    )
    halved = y_forward_stage(exchange(turned, "gy"), y_fwd)
    back, grad_spectral = back_stage(
        exchange(halved, "gx"), weight, scale, x_fwd, x_bwd, spec_real, spec_imag
    )
    along_y = y_backward_stage(exchange(back, "gx"), y_bwd)
    grad_field = close_stage(exchange(along_y, "gy"), slope, point_weight, zt_bwd)

    grad_spectral = (
        grad_spectral.reshape(C, C, 4, JL, LANES)
        .transpose(0, 1, 3, 2, 4)
        .reshape(spectral_weight.shape)
    )
    return (
        layer_out.reshape(grid_field.shape),
        grad_field.reshape(grid_field.shape),
        grad_spectral,
    )


def solution(mesh):
    field = P(None, None, None, "gx", "gy", None)
    modes = P(None, None, "gx", "gy", None)
    return jax.shard_map(
        on_device,
        mesh=mesh,
        in_specs=(field, modes, P(), field),
        out_specs=(field, field, modes),
        check_vma=False,
    )
```

```python
import math

import jax
import jax.numpy as jnp
import numpy as np
from jax import lax
from jax.experimental import pallas as pl
from jax.experimental.pallas import tpu as pltpu
from jax.sharding import PartitionSpec as P

T = 4
C = 16
X = 128
Y = 128
Z = 128
MX = 64
MY = 64
MZ = 32
GX = 16
GY = 32
XL = X // GX
YL = Y // GY
JL = MY // GX
LANES = 128
GX_ORDER = list(range(GX))[::-1]

F32 = jnp.float32
BF16 = jnp.bfloat16

root_two_over_pi = math.sqrt(2.0 / math.pi)
gelu_cubic = 0.044715


def signed(kept):
    j = np.arange(kept)
    return np.where(j < kept // 2, j, j - kept)


def cos_sin(freq, length):
    q = np.mod(freq[:, None] * np.arange(length)[None, :], length)
    angle = q * (2.0 * np.pi / length)
    return np.cos(angle).astype(BF16), np.sin(angle).astype(BF16)


def tables():
    cz, sz = (a.astype(np.float64) for a in cos_sin(np.arange(MZ), Z))
    quarter = np.mod(np.arange(T)[:, None] * np.arange(T)[None, :], T)
    ct = np.array([1.0, 0.0, -1.0, 0.0])[quarter]
    st = np.array([0.0, 1.0, 0.0, -1.0])[quarter]
    both_cos = (
        cz[None, :, None, :] * ct[:, None, :, None] - sz[None, :, None, :] * st[:, None, :, None]
    )
    both_sin = (
        sz[None, :, None, :] * ct[:, None, :, None] + cz[None, :, None, :] * st[:, None, :, None]
    )
    zt_fwd = np.stack([both_cos, -both_sin], 1).reshape(T * 2 * MZ, T * Z)
    zt_bwd = zt_fwd

    cy, sy = (a.astype(np.float64) for a in cos_sin(signed(MY), Y))
    fwd = np.empty((MY, 2, Y, 2))
    fwd[:, 0, :, 0] = cy
    fwd[:, 0, :, 1] = sy
    fwd[:, 1, :, 0] = -sy
    fwd[:, 1, :, 1] = cy
    fwd = fwd.reshape(GX, JL, 2, Y * 2)[GX_ORDER]
    y_fwd = fwd.transpose(1, 2, 0, 3).reshape(MY * 2, Y * 2)
    bwd = np.empty((Y, 2, MY, 2))
    bwd[:, 0, :, 0] = cy.T
    bwd[:, 0, :, 1] = -sy.T
    bwd[:, 1, :, 0] = sy.T
    bwd[:, 1, :, 1] = cy.T
    y_bwd = bwd.reshape(Y * 2, GX, JL * 2)[:, GX_ORDER].reshape(Y * 2, MY * 2)

    cx, sx = (a.astype(np.float64) for a in cos_sin(signed(MX), X))
    fwd = np.empty((X, 2, 2, MX))
    fwd[:, 0, 0, :] = cx.T
    fwd[:, 1, 0, :] = sx.T
    fwd[:, 0, 1, :] = -sx.T
    fwd[:, 1, 1, :] = cx.T
    x_fwd = fwd.reshape(GX, XL * 2, 2 * MX)[GX_ORDER].reshape(X * 2, 2 * MX)
    bwd = np.empty((X, 2, 2, MX))
    bwd[:, 0, 0, :] = cx.T
    bwd[:, 0, 1, :] = -sx.T
    bwd[:, 1, 0, :] = sx.T
    bwd[:, 1, 1, :] = cx.T
    bwd = bwd.reshape(GX, XL, 2, 2 * MX)[GX_ORDER]
    x_bwd = bwd.transpose(1, 2, 0, 3).reshape(X * 2, 2 * MX)
    return tuple(a.astype(BF16) for a in (zt_fwd, zt_bwd, y_fwd, y_bwd, x_fwd, x_bwd))


def dot(left, right, left_dim=1, right_dim=0):
    return lax.dot_general(
        left, right, (((left_dim,), (right_dim,)), ((), ())), preferred_element_type=F32
    )


def swap_bit(low, high, step):
    lane = lax.broadcasted_iota(jnp.int32, low.shape, 1)
    upper = (lane & step) != 0
    first = jnp.where(upper, pltpu.roll(high, step, 1), low)
    second = jnp.where(upper, high, pltpu.roll(low, LANES - step, 1))
    return first, second


def swap_eight(parts):
    parts = list(parts)
    for step in (1, 2, 4):
        for i in range(8):
            if not i & step:
                parts[i], parts[i | step] = swap_bit(parts[i], parts[i | step], step)
    return parts


def gelu_parts(pre):
    square = pre * pre
    inner = pre * (root_two_over_pi + (root_two_over_pi * gelu_cubic) * square)
    half = 0.5 + 0.5 * jnp.tanh(inner)
    rise = pre * (2.0 * root_two_over_pi + (6.0 * root_two_over_pi * gelu_cubic) * square)
    return pre * half, half * (1.0 + (1.0 - half) * rise)


def cells_of(wide_ref, y):
    return jnp.concatenate(
        [wide_ref[pl.ds(t * C * XL * YL + y, C * XL, stride=YL), :] for t in range(T)], 1
    )


def put_cells(wide_ref, y, value):
    for t in range(T):
        wide_ref[pl.ds(t * C * XL * YL + y, C * XL, stride=YL), :] = value[:, t * Z : (t + 1) * Z]


def pack(spread_ref, out_ref):
    for k in range(spread_ref.shape[0]):
        out_ref[:, k * LANES : (k + 1) * LANES] = spread_ref[k].astype(BF16)


def unpack(in_ref, spread_ref):
    for k in range(spread_ref.shape[0]):
        spread_ref[k] = in_ref[:, k * LANES : (k + 1) * LANES].astype(F32)


def put_modes(spread_ref, y, cells, zt_fwd):
    turned = dot(zt_fwd, cells, 1, 1)
    for kt in range(T):
        for p in range(2):
            row = (kt * 2 + p) * MZ
            spread_ref[kt, pl.ds(y * 2 + p, MZ, stride=2 * YL), :] = turned[row : row + MZ]


def modes_of(spread_ref, y):
    return jnp.concatenate(
        [
            spread_ref[kt, pl.ds(y * 2 + p, MZ, stride=2 * YL), :]
            for kt in range(T)
            for p in range(2)
        ],
        0,
    )


def open_kernel(field_ref, zt_fwd_ref, out_ref, wide, spread):
    wide[...] = field_ref[...].astype(F32)
    for y in range(YL):
        put_modes(spread, y, cells_of(wide, y).astype(BF16), zt_fwd_ref[...])
    pack(spread, out_ref)


def y_forward_kernel(in_ref, table_ref, out_ref, spread):
    along_y = dot(table_ref[...], in_ref[...])
    for low in range(2):
        parts = [
            along_y[
                j * 2 * GX : (j + 1) * 2 * GX,
                (kth * 2 + low) * LANES : (kth * 2 + low + 1) * LANES,
            ]
            for kth in range(2)
            for j in range(JL)
        ]
        for x, part in enumerate(swap_eight(parts)):
            for s in range(2):
                spread[low, pl.ds(x * 2 + s, GX, stride=2 * XL), :] = part[s * GX : (s + 1) * GX]
    pack(spread, out_ref)


def to_spectrum(in_ref, x_fwd_ref):
    low, high = (
        dot(in_ref[:, k * LANES : (k + 1) * LANES], x_fwd_ref[...], 0, 0)
        .astype(BF16)
        .astype(F32)
        for k in range(2)
    )
    return swap_bit(low, high, MX)


def from_spectrum(real, imag, x_bwd_ref, out_ref, spread):
    for low, modes in enumerate(swap_bit(real, imag, MX)):
        along_x = dot(x_bwd_ref[...], modes.astype(BF16), 1, 1)
        parts = [along_x[x * 2 * GX : (x + 1) * 2 * GX] for x in range(XL)]
        for i, part in enumerate(swap_eight(parts)):
            kth, j = divmod(i, JL)
            for s in range(2):
                spread[kth * 2 + low, pl.ds(j * 2 + s, GX, stride=2 * JL), :] = part[
                    s * GX : (s + 1) * GX
                ]
    pack(spread, out_ref)


def weight_parts(w_ref, c):
    w = w_ref[c].astype(F32).reshape(C, 2, 8, LANES)
    return w[:, 0], w[:, 1]


def at_channel(ref, c):
    return ref[pl.ds(pl.multiple_of(c * 8, 8), 8), :]


def mix_kernel(
    in_ref, w_ref, scale_ref, x_fwd_ref, x_bwd_ref, out_ref, real_ref, imag_ref, spread
):
    real, imag = to_spectrum(in_ref, x_fwd_ref)
    real_ref[...] = real
    imag_ref[...] = imag

    def add(c, total):
        s_real = at_channel(real_ref, c)[None]
        s_imag = at_channel(imag_ref, c)[None]
        w_real, w_imag = weight_parts(w_ref, c)
        return (
            total[0] + (s_real * w_real - s_imag * w_imag),
            total[1] + (s_real * w_imag + s_imag * w_real),
        )

    zero = jnp.zeros((C, 8, LANES), F32)
    mix_real, mix_imag = lax.fori_loop(0, C, add, (zero, zero))
    scale = scale_ref[0]
    from_spectrum(
        (mix_real * scale).reshape(C * 8, LANES),
        (mix_imag * scale).reshape(C * 8, LANES),
        x_bwd_ref,
        out_ref,
        spread,
    )


def back_kernel(
    in_ref,
    w_ref,
    scale_ref,
    x_fwd_ref,
    x_bwd_ref,
    s_real_ref,
    s_imag_ref,
    out_ref,
    grad_hbm,
    real_ref,
    imag_ref,
    back_real,
    back_imag,
    spread,
    grad,
    sem,
):
    real, imag = to_spectrum(in_ref, x_fwd_ref)
    real_ref[...] = real
    imag_ref[...] = imag

    def outer(c, carry):
        s_real = (at_channel(s_real_ref, c).astype(F32) * scale_ref[0])[None, None]
        s_imag = (at_channel(s_imag_ref, c).astype(F32) * scale_ref[0])[None, None]
        a_real = real_ref[...].reshape(C, 1, 8, LANES)
        a_imag = imag_ref[...].reshape(C, 1, 8, LANES)
        both = jnp.concatenate(
            [s_real * a_real + s_imag * a_imag, s_real * a_imag - s_imag * a_real], 1
        )
        grad[c] = both.reshape(C * 2 * 8, LANES).astype(BF16)
        return carry

    lax.fori_loop(0, C, outer, 0)
    send = pltpu.make_async_copy(grad, grad_hbm, sem)
    send.start()

    def one(c, carry):
        a_real = real_ref[...].reshape(C, 8, LANES)
        a_imag = imag_ref[...].reshape(C, 8, LANES)
        w_real, w_imag = weight_parts(w_ref, c)
        row = pl.ds(pl.multiple_of(c * 8, 8), 8)
        back_real[row, :] = jnp.sum(a_real * w_real + a_imag * w_imag, 0)
        back_imag[row, :] = jnp.sum(a_imag * w_real - a_real * w_imag, 0)
        return carry

    lax.fori_loop(0, C, one, 0)
    scale = scale_ref[0]
    from_spectrum(back_real[...] * scale, back_imag[...] * scale, x_bwd_ref, out_ref, spread)
    send.wait()


def y_backward_kernel(in_ref, table_ref, out_ref):
    out_ref[...] = dot(table_ref[...], in_ref[...]).astype(BF16)


def point_table(point_ref, back):
    shape = (C * XL, C)
    row = lax.broadcasted_iota(jnp.int32, shape, 0)
    pick = (row // XL == lax.broadcasted_iota(jnp.int32, shape, 1)).astype(F32).astype(BF16)
    half = dot(pick, point_ref[...], 1, 0 if back else 1).astype(BF16)
    full = dot(half, pick, 1, 1)
    row = lax.broadcasted_iota(jnp.int32, full.shape, 0)
    column = lax.broadcasted_iota(jnp.int32, full.shape, 1)
    return jnp.where(row % XL == column % XL, full, 0.0).astype(BF16)


def cell_kernel(
    in_ref,
    field_ref,
    cotangent_ref,
    point_ref,
    zt_bwd_ref,
    zt_fwd_ref,
    out_ref,
    slope_ref,
    layer_hbm,
    wide,
    other,
    spread,
    layer,
    sem,
):
    point = point_table(point_ref, False)
    unpack(in_ref, spread)
    modes = [modes_of(spread, y).astype(BF16) for y in range(YL)]
    wide[...] = field_ref[...].astype(F32)
    other[...] = cotangent_ref[...].astype(F32)
    for y in range(YL):
        pre = dot(modes[y], zt_bwd_ref[...], 0, 0) + dot(point, cells_of(wide, y).astype(BF16))
        value, slope = gelu_parts(pre)
        put_cells(wide, y, value)
        slope_ref[y] = (cells_of(other, y) * slope).astype(BF16)
    layer[...] = wide[...].astype(BF16)
    send = pltpu.make_async_copy(layer, layer_hbm, sem)
    send.start()
    for y in range(YL):
        put_modes(spread, y, slope_ref[y], zt_fwd_ref[...])
    pack(spread, out_ref)
    send.wait()


def close_kernel(in_ref, slope_ref, point_ref, zt_bwd_ref, out_hbm, spread, wide, out, sems):
    point = point_table(point_ref, True)
    unpack(in_ref, spread)
    for y in range(YL):
        modes = modes_of(spread, y).astype(BF16)
        put_cells(wide, y, dot(modes, zt_bwd_ref[...], 0, 0) + dot(point, slope_ref[y]))
    copies = []
    for t in range(T):
        rows = pl.ds(t * C * XL * YL, C * XL * YL)
        out[rows, :] = wide[rows, :].astype(BF16)
        copies.append(pltpu.make_async_copy(out.at[rows], out_hbm.at[rows], sems.at[t]))
        copies[t].start()
    for copy in copies:
        copy.wait()


ROWS = T * C * XL * YL
ZT = (MZ * YL * 2, T * LANES)
AFTER_Y = (GX * XL * 2, 2 * LANES)
AFTER_X = (GX * JL * 2, T * LANES)
ZT_SPREAD = (T, MZ * YL * 2, LANES)
Y_SPREAD = (2, GX * XL * 2, LANES)
X_SPREAD = (T, GX * JL * 2, LANES)
CELLS = (YL, C * XL, T * Z)
PARTS = (C * 8, LANES)


WIDE = (ROWS, Z)
GRAD = (C, C * 2 * 8, LANES)


def vmem(shape, dtype=F32):
    return pltpu.VMEM(shape, dtype)


def call(kernel, outs, operands, scratch=(), scalars=(), far_outs=(), flops=10**8):
    near = pl.BlockSpec(memory_space=pltpu.VMEM)
    smem = pl.BlockSpec(memory_space=pltpu.SMEM)
    anywhere = pl.BlockSpec(memory_space=pltpu.HBM)
    specs = [smem if i in scalars else near for i in range(len(operands))]
    out_specs = tuple(anywhere if i in far_outs else near for i in range(len(outs)))
    single = len(outs) == 1
    moved = sum(math.prod(o.shape) * o.dtype.itemsize for o in list(outs) + list(operands))
    return pl.pallas_call(
        kernel,
        out_shape=outs[0] if single else tuple(outs),
        in_specs=specs,
        out_specs=out_specs[0] if single else out_specs,
        scratch_shapes=list(scratch),
        cost_estimate=pl.CostEstimate(flops=flops, bytes_accessed=moved, transcendentals=0),
        compiler_params=pltpu.CompilerParams(vmem_limit_bytes=16 * 1024 * 1024),
    )(*operands)


def shaped(shape, dtype=BF16):
    return jax.ShapeDtypeStruct(shape, dtype)


def exchange(block, axis):
    groups = [GX_ORDER] if axis == "gx" else None
    return lax.all_to_all(
        block, axis, split_axis=0, concat_axis=0, axis_index_groups=groups, tiled=True
    )


def open_stage(field, zt_fwd):
    scratch = [vmem(WIDE), vmem(ZT_SPREAD)]
    return call(open_kernel, [shaped(ZT)], [field, zt_fwd], scratch)


def y_forward_stage(block, y_fwd):
    return call(y_forward_kernel, [shaped(AFTER_Y)], [block, y_fwd], [vmem(Y_SPREAD)])


def mix_stage(block, weight, scale, x_fwd, x_bwd):
    return call(
        mix_kernel,
        [shaped(AFTER_X), shaped(PARTS, F32), shaped(PARTS, F32)],
        [block, weight, scale, x_fwd, x_bwd],
        [vmem(X_SPREAD)],
        scalars=(2,),
    )


def y_backward_stage(block, y_bwd):
    return call(y_backward_kernel, [shaped(ZT)], [block, y_bwd])


def cell_stage(block, field, cotangent, point_weight, zt_bwd, zt_fwd):
    scratch = [vmem(WIDE), vmem(WIDE), vmem(ZT_SPREAD), vmem(WIDE, BF16)]
    scratch.append(pltpu.SemaphoreType.DMA)
    return call(
        cell_kernel,
        [shaped(ZT), shaped(CELLS), shaped(WIDE)],
        [block, field, cotangent, point_weight, zt_bwd, zt_fwd],
        scratch,
        far_outs=(2,),
    )


def back_stage(block, weight, scale, x_fwd, x_bwd, spec_real, spec_imag):
    scratch = [vmem(PARTS)] * 4 + [vmem(X_SPREAD), vmem(GRAD, BF16), pltpu.SemaphoreType.DMA]
    return call(
        back_kernel,
        [shaped(AFTER_X), shaped(GRAD)],
        [block, weight, scale, x_fwd, x_bwd, spec_real, spec_imag],
        scratch,
        scalars=(2,),
        far_outs=(1,),
    )


def close_stage(block, slope, point_weight, zt_bwd):
    return call(
        close_kernel,
        [shaped(WIDE)],
        [block, slope, point_weight, zt_bwd],
        [vmem(ZT_SPREAD), vmem(WIDE), vmem(WIDE, BF16), pltpu.SemaphoreType.DMA((T,))],
        far_outs=(0,),
    )


def on_device(grid_field, spectral_weight, point_weight, cotangent):
    zt_fwd, zt_bwd, y_fwd, y_bwd, x_fwd, x_bwd = (jnp.asarray(a) for a in tables())
    field = grid_field.reshape(WIDE)
    cotan = cotangent.reshape(WIDE)
    weight = spectral_weight.reshape(C, C, JL, 4, LANES).transpose(0, 1, 3, 2, 4).reshape(GRAD)
    kz = lax.axis_index("gy")
    scale = (jnp.where(kz == 0, 1.0, 2.0).astype(F32) / float(X * Y * Z * T)).reshape(1)

    opened = open_stage(field, zt_fwd)
    opened, scale = lax.optimization_barrier((opened, scale))
    halved = y_forward_stage(exchange(opened, "gy"), y_fwd)
    mixed, spec_real, spec_imag = mix_stage(exchange(halved, "gx"), weight, scale, x_fwd, x_bwd)
    along_y = y_backward_stage(exchange(mixed, "gx"), y_bwd)
    turned, slope, layer_out = cell_stage(
        exchange(along_y, "gy"), field, cotan, point_weight, zt_bwd, zt_fwd
    )
    halved = y_forward_stage(exchange(turned, "gy"), y_fwd)
    back, grad_spectral = back_stage(
        exchange(halved, "gx"), weight, scale, x_fwd, x_bwd, spec_real, spec_imag
    )
    along_y = y_backward_stage(exchange(back, "gx"), y_bwd)
    grad_field = close_stage(exchange(along_y, "gy"), slope, point_weight, zt_bwd)

    grad_spectral = (
        grad_spectral.reshape(C, C, 4, JL, LANES)
        .transpose(0, 1, 3, 2, 4)
        .reshape(spectral_weight.shape)
    )
    return (
        layer_out.reshape(grid_field.shape),
        grad_field.reshape(grid_field.shape),
        grad_spectral,
    )


def solution(mesh):
    field = P(None, None, None, "gx", "gy", None)
    modes = P(None, None, "gx", "gy", None)
    return jax.shard_map(
        on_device,
        mesh=mesh,
        in_specs=(field, modes, P(), field),
        out_specs=(field, field, modes),
        check_vma=False,
    )
```

```python
import math

import jax
import jax.numpy as jnp
import numpy as np
from jax import lax
from jax.experimental import pallas as pl
from jax.experimental.pallas import tpu as pltpu
from jax.sharding import PartitionSpec as P

T = 4
C = 16
X = 128
Y = 128
Z = 128
MX = 64
MY = 64
MZ = 32
GX = 16
GY = 32
XL = X // GX
YL = Y // GY
JL = MY // GX
LANES = 128
GX_ORDER = list(range(GX))[::-1]

F32 = jnp.float32
BF16 = jnp.bfloat16

root_two_over_pi = math.sqrt(2.0 / math.pi)
gelu_cubic = 0.044715


def signed(kept):
    j = np.arange(kept)
    return np.where(j < kept // 2, j, j - kept)


def cos_sin(freq, length):
    q = np.mod(freq[:, None] * np.arange(length)[None, :], length)
    angle = q * (2.0 * np.pi / length)
    return np.cos(angle).astype(BF16), np.sin(angle).astype(BF16)


def tables():
    cz, sz = (a.astype(np.float64) for a in cos_sin(np.arange(MZ), Z))
    quarter = np.mod(np.arange(T)[:, None] * np.arange(T)[None, :], T)
    ct = np.array([1.0, 0.0, -1.0, 0.0])[quarter]
    st = np.array([0.0, 1.0, 0.0, -1.0])[quarter]
    both_cos = (
        cz[None, :, None, :] * ct[:, None, :, None] - sz[None, :, None, :] * st[:, None, :, None]
    )
    both_sin = (
        sz[None, :, None, :] * ct[:, None, :, None] + cz[None, :, None, :] * st[:, None, :, None]
    )
    zt_fwd = np.stack([both_cos, -both_sin], 1).reshape(T * 2 * MZ, T * Z)
    zt_bwd = zt_fwd

    cy, sy = (a.astype(np.float64) for a in cos_sin(signed(MY), Y))
    fwd = np.empty((MY, 2, Y, 2))
    fwd[:, 0, :, 0] = cy
    fwd[:, 0, :, 1] = sy
    fwd[:, 1, :, 0] = -sy
    fwd[:, 1, :, 1] = cy
    fwd = fwd.reshape(GX, JL, 2, Y * 2)[GX_ORDER]
    y_fwd = fwd.transpose(1, 2, 0, 3).reshape(MY * 2, Y * 2)
    bwd = np.empty((Y, 2, MY, 2))
    bwd[:, 0, :, 0] = cy.T
    bwd[:, 0, :, 1] = -sy.T
    bwd[:, 1, :, 0] = sy.T
    bwd[:, 1, :, 1] = cy.T
    y_bwd = bwd.reshape(Y * 2, GX, JL * 2)[:, GX_ORDER].reshape(Y * 2, MY * 2)

    cx, sx = (a.astype(np.float64) for a in cos_sin(signed(MX), X))
    fwd = np.empty((X, 2, 2, MX))
    fwd[:, 0, 0, :] = cx.T
    fwd[:, 1, 0, :] = sx.T
    fwd[:, 0, 1, :] = -sx.T
    fwd[:, 1, 1, :] = cx.T
    x_fwd = fwd.reshape(GX, XL * 2, 2 * MX)[GX_ORDER].reshape(X * 2, 2 * MX)
    bwd = np.empty((X, 2, 2, MX))
    bwd[:, 0, 0, :] = cx.T
    bwd[:, 0, 1, :] = -sx.T
    bwd[:, 1, 0, :] = sx.T
    bwd[:, 1, 1, :] = cx.T
    bwd = bwd.reshape(GX, XL, 2, 2 * MX)[GX_ORDER]
    x_bwd = bwd.transpose(1, 2, 0, 3).reshape(X * 2, 2 * MX)
    return tuple(a.astype(BF16) for a in (zt_fwd, zt_bwd, y_fwd, y_bwd, x_fwd, x_bwd))


def dot(left, right, left_dim=1, right_dim=0):
    return lax.dot_general(
        left, right, (((left_dim,), (right_dim,)), ((), ())), preferred_element_type=F32
    )


def swap_bit(low, high, step):
    lane = lax.broadcasted_iota(jnp.int32, low.shape, 1)
    upper = (lane & step) != 0
    first = jnp.where(upper, pltpu.roll(high, step, 1), low)
    second = jnp.where(upper, high, pltpu.roll(low, LANES - step, 1))
    return first, second


def swap_eight(parts):
    parts = list(parts)
    for step in (1, 2, 4):
        for i in range(8):
            if not i & step:
                parts[i], parts[i | step] = swap_bit(parts[i], parts[i | step], step)
    return parts


def gelu_parts(pre):
    square = pre * pre
    inner = pre * (root_two_over_pi + (root_two_over_pi * gelu_cubic) * square)
    half = 0.5 + 0.5 * jnp.tanh(inner)
    rise = pre * (2.0 * root_two_over_pi + (6.0 * root_two_over_pi * gelu_cubic) * square)
    return pre * half, half * (1.0 + (1.0 - half) * rise)


def cells_of(wide_ref, y):
    return jnp.concatenate(
        [wide_ref[pl.ds(t * C * XL * YL + y, C * XL, stride=YL), :] for t in range(T)], 1
    )


def put_cells(wide_ref, y, value):
    for t in range(T):
        wide_ref[pl.ds(t * C * XL * YL + y, C * XL, stride=YL), :] = value[:, t * Z : (t + 1) * Z]


def pack(spread_ref, out_ref):
    for k in range(spread_ref.shape[0]):
        out_ref[:, k * LANES : (k + 1) * LANES] = spread_ref[k].astype(BF16)


def unpack(in_ref, spread_ref):
    for k in range(spread_ref.shape[0]):
        spread_ref[k] = in_ref[:, k * LANES : (k + 1) * LANES].astype(F32)


def put_modes(spread_ref, y, cells, zt_fwd):
    turned = dot(zt_fwd, cells, 1, 1)
    for kt in range(T):
        for p in range(2):
            row = (kt * 2 + p) * MZ
            spread_ref[kt, pl.ds(y * 2 + p, MZ, stride=2 * YL), :] = turned[row : row + MZ]


def modes_of(spread_ref, y):
    return jnp.concatenate(
        [
            spread_ref[kt, pl.ds(y * 2 + p, MZ, stride=2 * YL), :]
            for kt in range(T)
            for p in range(2)
        ],
        0,
    )


def build_zt(table):
    shape = (MZ, Z)
    turns = lax.broadcasted_iota(jnp.int32, shape, 0) * lax.broadcasted_iota(jnp.int32, shape, 1)
    angle = (turns & (Z - 1)).astype(F32) * (2.0 * math.pi / Z)
    cosine = jnp.cos(angle)
    sine = jnp.sin(angle)
    real = (cosine, -sine, -cosine, sine)
    imag = (-sine, -cosine, sine, cosine)
    for kt in range(T):
        for p, part in enumerate((real, imag)):
            row = (kt * 2 + p) * MZ
            for t in range(T):
                table[row : row + MZ, t * Z : (t + 1) * Z] = part[kt * t % T].astype(BF16)


def open_kernel(field_ref, out_ref, wide, spread, table):
    build_zt(table)
    wide[...] = field_ref[...].astype(F32)
    for y in range(YL):
        put_modes(spread, y, cells_of(wide, y).astype(BF16), table[...])
    pack(spread, out_ref)


def split_kernel(field_ref, cotangent_ref, field_out, cotangent_out, wide, other):
    wide[...] = field_ref[...].astype(F32)
    other[...] = cotangent_ref[...].astype(F32)
    for y in range(YL):
        field_out[y] = cells_of(wide, y).astype(BF16)
        cotangent_out[y] = cells_of(other, y).astype(BF16)


def y_forward_kernel(in_ref, table_ref, out_ref, spread):
    along_y = dot(table_ref[...], in_ref[...])
    for low in range(2):
        parts = [
            along_y[
                j * 2 * GX : (j + 1) * 2 * GX,
                (kth * 2 + low) * LANES : (kth * 2 + low + 1) * LANES,
            ]
            for kth in range(2)
            for j in range(JL)
        ]
        for x, part in enumerate(swap_eight(parts)):
            for s in range(2):
                spread[low, pl.ds(x * 2 + s, GX, stride=2 * XL), :] = part[s * GX : (s + 1) * GX]
    pack(spread, out_ref)


def to_spectrum(in_ref, x_fwd_ref):
    low, high = (
        dot(in_ref[:, k * LANES : (k + 1) * LANES], x_fwd_ref[...], 0, 0)
        .astype(BF16)
        .astype(F32)
        for k in range(2)
    )
    return swap_bit(low, high, MX)


def from_spectrum(real, imag, x_bwd_ref, out_ref, spread):
    for low, modes in enumerate(swap_bit(real, imag, MX)):
        along_x = dot(x_bwd_ref[...], modes.astype(BF16), 1, 1)
        parts = [along_x[x * 2 * GX : (x + 1) * 2 * GX] for x in range(XL)]
        for i, part in enumerate(swap_eight(parts)):
            kth, j = divmod(i, JL)
            for s in range(2):
                spread[kth * 2 + low, pl.ds(j * 2 + s, GX, stride=2 * JL), :] = part[
                    s * GX : (s + 1) * GX
                ]
    pack(spread, out_ref)


def weight_parts(w_ref, c):
    w = w_ref[c].astype(F32).reshape(C, 2, 8, LANES)
    return w[:, 0], w[:, 1]


def at_channel(ref, c):
    return ref[pl.ds(pl.multiple_of(c * 8, 8), 8), :]


def mix_kernel(
    in_ref,
    w_ref,
    scale_ref,
    x_fwd_ref,
    x_bwd_ref,
    out_ref,
    real_out,
    imag_out,
    real_ref,
    imag_ref,
    spread,
):
    real, imag = to_spectrum(in_ref, x_fwd_ref)
    real_ref[...] = real
    imag_ref[...] = imag
    real_out[...] = real.astype(BF16)
    imag_out[...] = imag.astype(BF16)

    def add(c, total):
        s_real = at_channel(real_ref, c)[None]
        s_imag = at_channel(imag_ref, c)[None]
        w_real, w_imag = weight_parts(w_ref, c)
        return (
            total[0] + (s_real * w_real - s_imag * w_imag),
            total[1] + (s_real * w_imag + s_imag * w_real),
        )

    zero = jnp.zeros((C, 8, LANES), F32)
    mix_real, mix_imag = lax.fori_loop(0, C, add, (zero, zero))
    scale = scale_ref[0]
    from_spectrum(
        (mix_real * scale).reshape(C * 8, LANES),
        (mix_imag * scale).reshape(C * 8, LANES),
        x_bwd_ref,
        out_ref,
        spread,
    )


def back_kernel(
    in_ref,
    w_ref,
    scale_ref,
    x_fwd_ref,
    x_bwd_ref,
    out_ref,
    real_out,
    imag_out,
    real_ref,
    imag_ref,
    back_real,
    back_imag,
    spread,
):
    real, imag = to_spectrum(in_ref, x_fwd_ref)
    real_ref[...] = real
    imag_ref[...] = imag
    real_out[...] = real.astype(BF16)
    imag_out[...] = imag.astype(BF16)

    def one(c, carry):
        a_real = real_ref[...].reshape(C, 8, LANES)
        a_imag = imag_ref[...].reshape(C, 8, LANES)
        w_real, w_imag = weight_parts(w_ref, c)
        row = pl.ds(pl.multiple_of(c * 8, 8), 8)
        back_real[row, :] = jnp.sum(a_real * w_real + a_imag * w_imag, 0)
        back_imag[row, :] = jnp.sum(a_imag * w_real - a_real * w_imag, 0)
        return carry

    lax.fori_loop(0, C, one, 0)
    scale = scale_ref[0]
    from_spectrum(back_real[...] * scale, back_imag[...] * scale, x_bwd_ref, out_ref, spread)


def grad_kernel(
    s_real_in, s_imag_in, a_real_in, a_imag_in, scale_ref, out_ref, s_real, s_imag, a_real, a_imag
):
    scale = scale_ref[0]
    s_real[...] = s_real_in[...].astype(F32) * scale
    s_imag[...] = s_imag_in[...].astype(F32) * scale
    a_real[...] = a_real_in[...].astype(F32)
    a_imag[...] = a_imag_in[...].astype(F32)

    def one(c, carry):
        c_real = at_channel(s_real, c)[None, None]
        c_imag = at_channel(s_imag, c)[None, None]
        o_real = a_real[...].reshape(C, 1, 8, LANES)
        o_imag = a_imag[...].reshape(C, 1, 8, LANES)
        both = jnp.concatenate(
            [c_real * o_real + c_imag * o_imag, c_real * o_imag - c_imag * o_real], 1
        )
        out_ref[c] = both.reshape(C * 2 * 8, LANES).astype(BF16)
        return carry

    lax.fori_loop(0, C, one, 0)


def y_backward_kernel(in_ref, table_ref, out_ref):
    out_ref[...] = dot(table_ref[...], in_ref[...]).astype(BF16)


def point_table(point_ref, back):
    shape = (C * XL, C)
    row = lax.broadcasted_iota(jnp.int32, shape, 0)
    pick = (row // XL == lax.broadcasted_iota(jnp.int32, shape, 1)).astype(F32).astype(BF16)
    half = dot(pick, point_ref[...], 1, 0 if back else 1).astype(BF16)
    full = dot(half, pick, 1, 1)
    row = lax.broadcasted_iota(jnp.int32, full.shape, 0)
    column = lax.broadcasted_iota(jnp.int32, full.shape, 1)
    return jnp.where(row % XL == column % XL, full, 0.0).astype(BF16)


def cell_kernel(
    in_ref,
    field_ref,
    cotangent_ref,
    point_ref,
    zt_bwd_ref,
    zt_fwd_ref,
    out_ref,
    slope_ref,
    layer_ref,
    spread,
):
    point = point_table(point_ref, False)
    unpack(in_ref, spread)
    modes = [modes_of(spread, y).astype(BF16) for y in range(YL)]
    for y in range(YL):
        pre = dot(modes[y], zt_bwd_ref[...], 0, 0) + dot(point, field_ref[y])
        value, slope = gelu_parts(pre)
        layer_ref[y] = value.astype(BF16)
        slope_ref[y] = (cotangent_ref[y].astype(F32) * slope).astype(BF16)
    for y in range(YL):
        put_modes(spread, y, slope_ref[y], zt_fwd_ref[...])
    pack(spread, out_ref)


def layer_kernel(layer_ref, out_ref, wide):
    for y in range(YL):
        put_cells(wide, y, layer_ref[y].astype(F32))
    out_ref[...] = wide[...].astype(BF16)


def close_kernel(in_ref, slope_ref, point_ref, zt_bwd_ref, out_hbm, spread, wide, out, sems):
    point = point_table(point_ref, True)
    unpack(in_ref, spread)
    for y in range(YL):
        modes = modes_of(spread, y).astype(BF16)
        put_cells(wide, y, dot(modes, zt_bwd_ref[...], 0, 0) + dot(point, slope_ref[y]))
    copies = []
    for t in range(T):
        rows = pl.ds(t * C * XL * YL, C * XL * YL)
        out[rows, :] = wide[rows, :].astype(BF16)
        copies.append(pltpu.make_async_copy(out.at[rows], out_hbm.at[rows], sems.at[t]))
        copies[t].start()
    for copy in copies:
        copy.wait()


ROWS = T * C * XL * YL
ZT = (MZ * YL * 2, T * LANES)
AFTER_Y = (GX * XL * 2, 2 * LANES)
AFTER_X = (GX * JL * 2, T * LANES)
ZT_SPREAD = (T, MZ * YL * 2, LANES)
Y_SPREAD = (2, GX * XL * 2, LANES)
X_SPREAD = (T, GX * JL * 2, LANES)
CELLS = (YL, C * XL, T * Z)
PARTS = (C * 8, LANES)


WIDE = (ROWS, Z)
GRAD = (C, C * 2 * 8, LANES)


def vmem(shape, dtype=F32):
    return pltpu.VMEM(shape, dtype)


def call(kernel, outs, operands, scratch=(), scalars=(), far_outs=(), flops=10**8):
    near = pl.BlockSpec(memory_space=pltpu.VMEM)
    smem = pl.BlockSpec(memory_space=pltpu.SMEM)
    anywhere = pl.BlockSpec(memory_space=pltpu.HBM)
    specs = [smem if i in scalars else near for i in range(len(operands))]
    out_specs = tuple(anywhere if i in far_outs else near for i in range(len(outs)))
    single = len(outs) == 1
    moved = sum(math.prod(o.shape) * o.dtype.itemsize for o in list(outs) + list(operands))
    return pl.pallas_call(
        kernel,
        out_shape=outs[0] if single else tuple(outs),
        in_specs=specs,
        out_specs=out_specs[0] if single else out_specs,
        scratch_shapes=list(scratch),
        cost_estimate=pl.CostEstimate(flops=flops, bytes_accessed=moved, transcendentals=0),
        compiler_params=pltpu.CompilerParams(vmem_limit_bytes=16 * 1024 * 1024),
    )(*operands)


def shaped(shape, dtype=BF16):
    return jax.ShapeDtypeStruct(shape, dtype)


def exchange(block, axis):
    groups = [GX_ORDER] if axis == "gx" else None
    return lax.all_to_all(
        block, axis, split_axis=0, concat_axis=0, axis_index_groups=groups, tiled=True
    )


def open_stage(field):
    scratch = [vmem(WIDE), vmem(ZT_SPREAD), vmem((T * 2 * MZ, T * Z), BF16)]
    return call(open_kernel, [shaped(ZT)], [field], scratch)


def split_stage(field, cotangent):
    return call(
        split_kernel, [shaped(CELLS)] * 2, [field, cotangent], [vmem(WIDE), vmem(WIDE)]
    )


def y_forward_stage(block, y_fwd):
    return call(y_forward_kernel, [shaped(AFTER_Y)], [block, y_fwd], [vmem(Y_SPREAD)])


def mix_stage(block, weight, scale, x_fwd, x_bwd):
    return call(
        mix_kernel,
        [shaped(AFTER_X), shaped(PARTS), shaped(PARTS)],
        [block, weight, scale, x_fwd, x_bwd],
        [vmem(PARTS), vmem(PARTS), vmem(X_SPREAD)],
        scalars=(2,),
    )


def y_backward_stage(block, y_bwd):
    return call(y_backward_kernel, [shaped(ZT)], [block, y_bwd])


def cell_stage(block, field, cotangent, point_weight, zt_bwd, zt_fwd):
    return call(
        cell_kernel,
        [shaped(ZT), shaped(CELLS), shaped(CELLS)],
        [block, field, cotangent, point_weight, zt_bwd, zt_fwd],
        [vmem(ZT_SPREAD)],
    )


def layer_stage(layer):
    return call(layer_kernel, [shaped(WIDE)], [layer], [vmem(WIDE)])


def back_stage(block, weight, scale, x_fwd, x_bwd):
    return call(
        back_kernel,
        [shaped(AFTER_X), shaped(PARTS), shaped(PARTS)],
        [block, weight, scale, x_fwd, x_bwd],
        [vmem(PARTS)] * 4 + [vmem(X_SPREAD)],
        scalars=(2,),
    )


def grad_stage(spec, adj, scale):
    return call(
        grad_kernel, [shaped(GRAD)], [*spec, *adj, scale], [vmem(PARTS)] * 4, scalars=(4,)
    )


def close_stage(block, slope, point_weight, zt_bwd):
    return call(
        close_kernel,
        [shaped(WIDE)],
        [block, slope, point_weight, zt_bwd],
        [vmem(ZT_SPREAD), vmem(WIDE), vmem(WIDE, BF16), pltpu.SemaphoreType.DMA((T,))],
        far_outs=(0,),
    )


def on_device(grid_field, spectral_weight, point_weight, cotangent):
    zt_fwd, zt_bwd, y_fwd, y_bwd, x_fwd, x_bwd = (jnp.asarray(a) for a in tables())
    field = grid_field.reshape(WIDE)
    cotan = cotangent.reshape(WIDE)
    weight = spectral_weight.reshape(C, C, JL, 4, LANES).transpose(0, 1, 3, 2, 4).reshape(GRAD)
    kz = lax.axis_index("gy")
    scale = (jnp.where(kz == 0, 1.0, 2.0).astype(F32) / float(X * Y * Z * T)).reshape(1)

    opened = open_stage(field)
    opened, scale = lax.optimization_barrier((opened, scale))
    halved = y_forward_stage(exchange(opened, "gy"), y_fwd)
    mixed, *spec = mix_stage(exchange(halved, "gx"), weight, scale, x_fwd, x_bwd)
    along_y = y_backward_stage(exchange(mixed, "gx"), y_bwd)
    field, cotan = split_stage(field, cotan)
    turned, slope, layer = cell_stage(
        exchange(along_y, "gy"), field, cotan, point_weight, zt_bwd, zt_fwd
    )
    halved = y_forward_stage(exchange(turned, "gy"), y_fwd)
    back, *adj = back_stage(exchange(halved, "gx"), weight, scale, x_fwd, x_bwd)
    along_y = y_backward_stage(exchange(back, "gx"), y_bwd)
    layer_out = layer_stage(layer)
    grad_spectral = grad_stage(spec, adj, scale)
    grad_field = close_stage(exchange(along_y, "gy"), slope, point_weight, zt_bwd)

    grad_spectral = (
        grad_spectral.reshape(C, C, 4, JL, LANES)
        .transpose(0, 1, 3, 2, 4)
        .reshape(spectral_weight.shape)
    )
    return (
        layer_out.reshape(grid_field.shape),
        grad_field.reshape(grid_field.shape),
        grad_spectral,
    )


def solution(mesh):
    field = P(None, None, None, "gx", "gy", None)
    modes = P(None, None, "gx", "gy", None)
    return jax.shard_map(
        on_device,
        mesh=mesh,
        in_specs=(field, modes, P(), field),
        out_specs=(field, field, modes),
        check_vma=False,
    )
```

```python
import math

import jax
import jax.numpy as jnp
import numpy as np
from jax import lax
from jax.experimental import pallas as pl
from jax.experimental.pallas import tpu as pltpu
from jax.sharding import PartitionSpec as P

T = 4
C = 16
X = 128
Y = 128
Z = 128
MX = 64
MY = 64
MZ = 32
GX = 16
GY = 32
XL = X // GX
YL = Y // GY
JL = MY // GX
LANES = 128
GX_ORDER = list(range(GX))[::-1]

F32 = jnp.float32
BF16 = jnp.bfloat16

root_two_over_pi = math.sqrt(2.0 / math.pi)
gelu_cubic = 0.044715


def signed(kept):
    j = np.arange(kept)
    return np.where(j < kept // 2, j, j - kept)


def cos_sin(freq, length):
    q = np.mod(freq[:, None] * np.arange(length)[None, :], length)
    angle = q * (2.0 * np.pi / length)
    return np.cos(angle).astype(BF16), np.sin(angle).astype(BF16)


def tables():
    cz, sz = (a.astype(np.float64) for a in cos_sin(np.arange(MZ), Z))
    quarter = np.mod(np.arange(T)[:, None] * np.arange(T)[None, :], T)
    ct = np.array([1.0, 0.0, -1.0, 0.0])[quarter]
    st = np.array([0.0, 1.0, 0.0, -1.0])[quarter]
    both_cos = (
        cz[None, :, None, :] * ct[:, None, :, None] - sz[None, :, None, :] * st[:, None, :, None]
    )
    both_sin = (
        sz[None, :, None, :] * ct[:, None, :, None] + cz[None, :, None, :] * st[:, None, :, None]
    )
    zt_fwd = np.stack([both_cos, -both_sin], 1).reshape(T * 2 * MZ, T * Z)
    zt_bwd = zt_fwd

    cy, sy = (a.astype(np.float64) for a in cos_sin(signed(MY), Y))
    fwd = np.empty((MY, 2, Y, 2))
    fwd[:, 0, :, 0] = cy
    fwd[:, 0, :, 1] = sy
    fwd[:, 1, :, 0] = -sy
    fwd[:, 1, :, 1] = cy
    fwd = fwd.reshape(GX, JL, 2, Y * 2)[GX_ORDER]
    y_fwd = fwd.transpose(1, 2, 0, 3).reshape(MY * 2, Y * 2)
    bwd = np.empty((Y, 2, MY, 2))
    bwd[:, 0, :, 0] = cy.T
    bwd[:, 0, :, 1] = -sy.T
    bwd[:, 1, :, 0] = sy.T
    bwd[:, 1, :, 1] = cy.T
    y_bwd = bwd.reshape(Y * 2, GX, JL * 2)[:, GX_ORDER].reshape(Y * 2, MY * 2)

    cx, sx = (a.astype(np.float64) for a in cos_sin(signed(MX), X))
    fwd = np.empty((X, 2, 2, MX))
    fwd[:, 0, 0, :] = cx.T
    fwd[:, 1, 0, :] = sx.T
    fwd[:, 0, 1, :] = -sx.T
    fwd[:, 1, 1, :] = cx.T
    x_fwd = fwd.reshape(GX, XL * 2, 2 * MX)[GX_ORDER].reshape(X * 2, 2 * MX)
    bwd = np.empty((X, 2, 2, MX))
    bwd[:, 0, 0, :] = cx.T
    bwd[:, 0, 1, :] = -sx.T
    bwd[:, 1, 0, :] = sx.T
    bwd[:, 1, 1, :] = cx.T
    bwd = bwd.reshape(GX, XL, 2, 2 * MX)[GX_ORDER]
    x_bwd = bwd.transpose(1, 2, 0, 3).reshape(X * 2, 2 * MX)
    return tuple(a.astype(BF16) for a in (zt_fwd, zt_bwd, y_fwd, y_bwd, x_fwd, x_bwd))


def dot(left, right, left_dim=1, right_dim=0):
    return lax.dot_general(
        left, right, (((left_dim,), (right_dim,)), ((), ())), preferred_element_type=F32
    )


def swap_bit(low, high, step):
    lane = lax.broadcasted_iota(jnp.int32, low.shape, 1)
    upper = (lane & step) != 0
    first = jnp.where(upper, pltpu.roll(high, step, 1), low)
    second = jnp.where(upper, high, pltpu.roll(low, LANES - step, 1))
    return first, second


def swap_eight(parts):
    parts = list(parts)
    for step in (1, 2, 4):
        for i in range(8):
            if not i & step:
                parts[i], parts[i | step] = swap_bit(parts[i], parts[i | step], step)
    return parts


def gelu_parts(pre):
    square = pre * pre
    inner = pre * (root_two_over_pi + (root_two_over_pi * gelu_cubic) * square)
    half = 0.5 + 0.5 * jnp.tanh(inner)
    rise = pre * (2.0 * root_two_over_pi + (6.0 * root_two_over_pi * gelu_cubic) * square)
    return pre * half, half * (1.0 + (1.0 - half) * rise)


def cells_of(wide_ref, y):
    return jnp.concatenate(
        [wide_ref[pl.ds(t * C * XL * YL + y, C * XL, stride=YL), :] for t in range(T)], 1
    )


def put_cells(wide_ref, y, value):
    for t in range(T):
        wide_ref[pl.ds(t * C * XL * YL + y, C * XL, stride=YL), :] = value[:, t * Z : (t + 1) * Z]


def pack(spread_ref, out_ref):
    for k in range(spread_ref.shape[0]):
        out_ref[:, k * LANES : (k + 1) * LANES] = spread_ref[k].astype(BF16)


def unpack(in_ref, spread_ref):
    for k in range(spread_ref.shape[0]):
        spread_ref[k] = in_ref[:, k * LANES : (k + 1) * LANES].astype(F32)


def put_modes(spread_ref, y, cells, zt_fwd):
    turned = dot(zt_fwd, cells, 1, 1)
    for kt in range(T):
        for p in range(2):
            row = (kt * 2 + p) * MZ
            spread_ref[kt, pl.ds(y * 2 + p, MZ, stride=2 * YL), :] = turned[row : row + MZ]


def modes_of(spread_ref, y):
    return jnp.concatenate(
        [
            spread_ref[kt, pl.ds(y * 2 + p, MZ, stride=2 * YL), :]
            for kt in range(T)
            for p in range(2)
        ],
        0,
    )


def build_zt(table):
    shape = (MZ, Z)
    turns = lax.broadcasted_iota(jnp.int32, shape, 0) * lax.broadcasted_iota(jnp.int32, shape, 1)
    angle = (turns & (Z - 1)).astype(F32) * (2.0 * math.pi / Z)
    cosine = jnp.cos(angle)
    sine = jnp.sin(angle)
    real = (cosine, -sine, -cosine, sine)
    imag = (-sine, -cosine, sine, cosine)
    for kt in range(T):
        for p, part in enumerate((real, imag)):
            row = (kt * 2 + p) * MZ
            for t in range(T):
                table[row : row + MZ, t * Z : (t + 1) * Z] = part[kt * t % T].astype(BF16)


def open_kernel(field_ref, out_ref, wide, spread, table):
    build_zt(table)
    wide[...] = field_ref[...].astype(F32)
    for y in range(YL):
        put_modes(spread, y, cells_of(wide, y).astype(BF16), table[...])
    pack(spread, out_ref)


def y_forward_kernel(in_ref, table_ref, out_ref, spread):
    along_y = dot(table_ref[...], in_ref[...])
    for low in range(2):
        parts = [
            along_y[
                j * 2 * GX : (j + 1) * 2 * GX,
                (kth * 2 + low) * LANES : (kth * 2 + low + 1) * LANES,
            ]
            for kth in range(2)
            for j in range(JL)
        ]
        for x, part in enumerate(swap_eight(parts)):
            for s in range(2):
                spread[low, pl.ds(x * 2 + s, GX, stride=2 * XL), :] = part[s * GX : (s + 1) * GX]
    pack(spread, out_ref)


def to_spectrum(in_ref, x_fwd_ref):
    low, high = (
        dot(in_ref[:, k * LANES : (k + 1) * LANES], x_fwd_ref[...], 0, 0)
        .astype(BF16)
        .astype(F32)
        for k in range(2)
    )
    return swap_bit(low, high, MX)


def from_spectrum(real, imag, x_bwd_ref, out_ref, spread):
    for low, modes in enumerate(swap_bit(real, imag, MX)):
        along_x = dot(x_bwd_ref[...], modes.astype(BF16), 1, 1)
        parts = [along_x[x * 2 * GX : (x + 1) * 2 * GX] for x in range(XL)]
        for i, part in enumerate(swap_eight(parts)):
            kth, j = divmod(i, JL)
            for s in range(2):
                spread[kth * 2 + low, pl.ds(j * 2 + s, GX, stride=2 * JL), :] = part[
                    s * GX : (s + 1) * GX
                ]
    pack(spread, out_ref)


def weight_parts(w_ref, c):
    w = w_ref[c].astype(F32).reshape(C, 2, 8, LANES)
    return w[:, 0], w[:, 1]


def at_channel(ref, c):
    return ref[pl.ds(pl.multiple_of(c * 8, 8), 8), :]


def mix_kernel(
    in_ref, w_ref, scale_ref, x_fwd_ref, x_bwd_ref, out_ref, real_ref, imag_ref, spread
):
    real, imag = to_spectrum(in_ref, x_fwd_ref)
    real_ref[...] = real
    imag_ref[...] = imag

    def add(c, total):
        s_real = at_channel(real_ref, c)[None]
        s_imag = at_channel(imag_ref, c)[None]
        w_real, w_imag = weight_parts(w_ref, c)
        return (
            total[0] + (s_real * w_real - s_imag * w_imag),
            total[1] + (s_real * w_imag + s_imag * w_real),
        )

    zero = jnp.zeros((C, 8, LANES), F32)
    mix_real, mix_imag = lax.fori_loop(0, C, add, (zero, zero), unroll=4)
    scale = scale_ref[0]
    from_spectrum(
        (mix_real * scale).reshape(C * 8, LANES),
        (mix_imag * scale).reshape(C * 8, LANES),
        x_bwd_ref,
        out_ref,
        spread,
    )


def back_kernel(
    in_ref,
    w_ref,
    scale_ref,
    x_fwd_ref,
    x_bwd_ref,
    s_real_ref,
    s_imag_ref,
    layer_ref,
    out_ref,
    grad_hbm,
    layer_hbm,
    real_ref,
    imag_ref,
    back_real,
    back_imag,
    spread,
    grad,
    sems,
):
    send_layer = pltpu.make_async_copy(layer_ref, layer_hbm, sems.at[0])
    send_layer.start()
    real, imag = to_spectrum(in_ref, x_fwd_ref)
    real_ref[...] = real
    imag_ref[...] = imag

    def outer(c, carry):
        s_real = (at_channel(s_real_ref, c).astype(F32) * scale_ref[0])[None, None]
        s_imag = (at_channel(s_imag_ref, c).astype(F32) * scale_ref[0])[None, None]
        a_real = real_ref[...].reshape(C, 1, 8, LANES)
        a_imag = imag_ref[...].reshape(C, 1, 8, LANES)
        both = jnp.concatenate(
            [s_real * a_real + s_imag * a_imag, s_real * a_imag - s_imag * a_real], 1
        )
        grad[c] = both.reshape(C * 2 * 8, LANES).astype(BF16)
        return carry

    lax.fori_loop(0, C, outer, 0, unroll=4)
    send_grad = pltpu.make_async_copy(grad, grad_hbm, sems.at[1])
    send_grad.start()

    def one(c, carry):
        a_real = real_ref[...].reshape(C, 8, LANES)
        a_imag = imag_ref[...].reshape(C, 8, LANES)
        w_real, w_imag = weight_parts(w_ref, c)
        row = pl.ds(pl.multiple_of(c * 8, 8), 8)
        back_real[row, :] = jnp.sum(a_real * w_real + a_imag * w_imag, 0)
        back_imag[row, :] = jnp.sum(a_imag * w_real - a_real * w_imag, 0)
        return carry

    lax.fori_loop(0, C, one, 0, unroll=4)
    scale = scale_ref[0]
    from_spectrum(back_real[...] * scale, back_imag[...] * scale, x_bwd_ref, out_ref, spread)
    send_layer.wait()
    send_grad.wait()


def y_backward_kernel(in_ref, table_ref, out_ref):
    out_ref[...] = dot(table_ref[...], in_ref[...]).astype(BF16)


def point_table(point_ref, back):
    shape = (C * XL, C)
    row = lax.broadcasted_iota(jnp.int32, shape, 0)
    pick = (row // XL == lax.broadcasted_iota(jnp.int32, shape, 1)).astype(F32).astype(BF16)
    half = dot(pick, point_ref[...], 1, 0 if back else 1).astype(BF16)
    full = dot(half, pick, 1, 1)
    row = lax.broadcasted_iota(jnp.int32, full.shape, 0)
    column = lax.broadcasted_iota(jnp.int32, full.shape, 1)
    return jnp.where(row % XL == column % XL, full, 0.0).astype(BF16)


def cell_kernel(
    in_ref,
    field_ref,
    cotangent_ref,
    point_ref,
    zt_bwd_ref,
    zt_fwd_ref,
    out_ref,
    slope_ref,
    layer_ref,
    wide,
    other,
    spread,
):
    point = point_table(point_ref, False)
    unpack(in_ref, spread)
    modes = [modes_of(spread, y).astype(BF16) for y in range(YL)]
    wide[...] = field_ref[...].astype(F32)
    other[...] = cotangent_ref[...].astype(F32)
    for y in range(YL):
        pre = dot(modes[y], zt_bwd_ref[...], 0, 0) + dot(point, cells_of(wide, y).astype(BF16))
        value, slope = gelu_parts(pre)
        put_cells(wide, y, value)
        slope_ref[y] = (cells_of(other, y) * slope).astype(BF16)
    layer_ref[...] = wide[...].astype(BF16)
    for y in range(YL):
        put_modes(spread, y, slope_ref[y], zt_fwd_ref[...])
    pack(spread, out_ref)


def close_kernel(in_ref, slope_ref, point_ref, zt_bwd_ref, out_hbm, spread, wide, out, sems):
    point = point_table(point_ref, True)
    unpack(in_ref, spread)
    for y in range(YL):
        modes = modes_of(spread, y).astype(BF16)
        put_cells(wide, y, dot(modes, zt_bwd_ref[...], 0, 0) + dot(point, slope_ref[y]))
    copies = []
    for t in range(T):
        rows = pl.ds(t * C * XL * YL, C * XL * YL)
        out[rows, :] = wide[rows, :].astype(BF16)
        copies.append(pltpu.make_async_copy(out.at[rows], out_hbm.at[rows], sems.at[t]))
        copies[t].start()
    for copy in copies:
        copy.wait()


ROWS = T * C * XL * YL
ZT = (MZ * YL * 2, T * LANES)
AFTER_Y = (GX * XL * 2, 2 * LANES)
AFTER_X = (GX * JL * 2, T * LANES)
ZT_SPREAD = (T, MZ * YL * 2, LANES)
Y_SPREAD = (2, GX * XL * 2, LANES)
X_SPREAD = (T, GX * JL * 2, LANES)
CELLS = (YL, C * XL, T * Z)
PARTS = (C * 8, LANES)


WIDE = (ROWS, Z)
GRAD = (C, C * 2 * 8, LANES)


def vmem(shape, dtype=F32):
    return pltpu.VMEM(shape, dtype)


def call(kernel, outs, operands, scratch=(), scalars=(), far_outs=(), flops=10**8):
    near = pl.BlockSpec(memory_space=pltpu.VMEM)
    smem = pl.BlockSpec(memory_space=pltpu.SMEM)
    anywhere = pl.BlockSpec(memory_space=pltpu.HBM)
    specs = [smem if i in scalars else near for i in range(len(operands))]
    out_specs = tuple(anywhere if i in far_outs else near for i in range(len(outs)))
    single = len(outs) == 1
    moved = sum(math.prod(o.shape) * o.dtype.itemsize for o in list(outs) + list(operands))
    return pl.pallas_call(
        kernel,
        out_shape=outs[0] if single else tuple(outs),
        in_specs=specs,
        out_specs=out_specs[0] if single else out_specs,
        scratch_shapes=list(scratch),
        cost_estimate=pl.CostEstimate(flops=flops, bytes_accessed=moved, transcendentals=0),
        compiler_params=pltpu.CompilerParams(vmem_limit_bytes=16 * 1024 * 1024),
    )(*operands)


def shaped(shape, dtype=BF16):
    return jax.ShapeDtypeStruct(shape, dtype)


def exchange(block, axis):
    groups = [GX_ORDER] if axis == "gx" else None
    return lax.all_to_all(
        block, axis, split_axis=0, concat_axis=0, axis_index_groups=groups, tiled=True
    )


def open_stage(field):
    scratch = [vmem(WIDE), vmem(ZT_SPREAD), vmem((T * 2 * MZ, T * Z), BF16)]
    return call(open_kernel, [shaped(ZT)], [field], scratch)


def y_forward_stage(block, y_fwd):
    return call(y_forward_kernel, [shaped(AFTER_Y)], [block, y_fwd], [vmem(Y_SPREAD)])


def mix_stage(block, weight, scale, x_fwd, x_bwd):
    return call(
        mix_kernel,
        [shaped(AFTER_X), shaped(PARTS, F32), shaped(PARTS, F32)],
        [block, weight, scale, x_fwd, x_bwd],
        [vmem(X_SPREAD)],
        scalars=(2,),
    )


def y_backward_stage(block, y_bwd):
    return call(y_backward_kernel, [shaped(ZT)], [block, y_bwd])


def cell_stage(block, field, cotangent, point_weight, zt_bwd, zt_fwd):
    return call(
        cell_kernel,
        [shaped(ZT), shaped(CELLS), shaped(WIDE)],
        [block, field, cotangent, point_weight, zt_bwd, zt_fwd],
        [vmem(WIDE), vmem(WIDE), vmem(ZT_SPREAD)],
    )


def back_stage(block, weight, scale, x_fwd, x_bwd, spec_real, spec_imag, layer):
    scratch = [vmem(PARTS)] * 4 + [vmem(X_SPREAD), vmem(GRAD, BF16)]
    scratch.append(pltpu.SemaphoreType.DMA((2,)))
    return call(
        back_kernel,
        [shaped(AFTER_X), shaped(GRAD), shaped(WIDE)],
        [block, weight, scale, x_fwd, x_bwd, spec_real, spec_imag, layer],
        scratch,
        scalars=(2,),
        far_outs=(1, 2),
    )


def close_stage(block, slope, point_weight, zt_bwd):
    return call(
        close_kernel,
        [shaped(WIDE)],
        [block, slope, point_weight, zt_bwd],
        [vmem(ZT_SPREAD), vmem(WIDE), vmem(WIDE, BF16), pltpu.SemaphoreType.DMA((T,))],
        far_outs=(0,),
    )


def on_device(grid_field, spectral_weight, point_weight, cotangent):
    zt_fwd, zt_bwd, y_fwd, y_bwd, x_fwd, x_bwd = (jnp.asarray(a) for a in tables())
    field = grid_field.reshape(WIDE)
    cotan = cotangent.reshape(WIDE)
    weight = spectral_weight.reshape(C, C, JL, 4, LANES).transpose(0, 1, 3, 2, 4).reshape(GRAD)
    kz = lax.axis_index("gy")
    scale = (jnp.where(kz == 0, 1.0, 2.0).astype(F32) / float(X * Y * Z * T)).reshape(1)

    opened = open_stage(field)
    opened, scale = lax.optimization_barrier((opened, scale))
    halved = y_forward_stage(exchange(opened, "gy"), y_fwd)
    mixed, spec_real, spec_imag = mix_stage(exchange(halved, "gx"), weight, scale, x_fwd, x_bwd)
    along_y = y_backward_stage(exchange(mixed, "gx"), y_bwd)
    turned, slope, layer = cell_stage(
        exchange(along_y, "gy"), field, cotan, point_weight, zt_bwd, zt_fwd
    )
    halved = y_forward_stage(exchange(turned, "gy"), y_fwd)
    back, grad_spectral, layer_out = back_stage(
        exchange(halved, "gx"), weight, scale, x_fwd, x_bwd, spec_real, spec_imag, layer
    )
    along_y = y_backward_stage(exchange(back, "gx"), y_bwd)
    grad_field = close_stage(exchange(along_y, "gy"), slope, point_weight, zt_bwd)

    grad_spectral = (
        grad_spectral.reshape(C, C, 4, JL, LANES)
        .transpose(0, 1, 3, 2, 4)
        .reshape(spectral_weight.shape)
    )
    return (
        layer_out.reshape(grid_field.shape),
        grad_field.reshape(grid_field.shape),
        grad_spectral,
    )


def solution(mesh):
    field = P(None, None, None, "gx", "gy", None)
    modes = P(None, None, "gx", "gy", None)
    return jax.shard_map(
        on_device,
        mesh=mesh,
        in_specs=(field, modes, P(), field),
        out_specs=(field, field, modes),
        check_vma=False,
    )
```

```python
import math

import jax
import jax.numpy as jnp
import numpy as np
from jax import lax
from jax.experimental import pallas as pl
from jax.experimental.pallas import tpu as pltpu
from jax.sharding import PartitionSpec as P

T = 4
C = 16
X = 128
Y = 128
Z = 128
MX = 64
MY = 64
MZ = 32
GX = 16
GY = 32
XL = X // GX
YL = Y // GY
JL = MY // GX
LANES = 128
GX_ORDER = [z * 8 + x * 2 + core for z in (1, 0) for x in (2, 0, 3, 1) for core in (1, 0)]

F32 = jnp.float32
BF16 = jnp.bfloat16

root_two_over_pi = math.sqrt(2.0 / math.pi)
gelu_cubic = 0.044715


def signed(kept):
    j = np.arange(kept)
    return np.where(j < kept // 2, j, j - kept)


def cos_sin(freq, length):
    q = np.mod(freq[:, None] * np.arange(length)[None, :], length)
    angle = q * (2.0 * np.pi / length)
    return np.cos(angle).astype(BF16), np.sin(angle).astype(BF16)


def tables():
    cz, sz = (a.astype(np.float64) for a in cos_sin(np.arange(MZ), Z))
    quarter = np.mod(np.arange(T)[:, None] * np.arange(T)[None, :], T)
    ct = np.array([1.0, 0.0, -1.0, 0.0])[quarter]
    st = np.array([0.0, 1.0, 0.0, -1.0])[quarter]
    both_cos = (
        cz[None, :, None, :] * ct[:, None, :, None] - sz[None, :, None, :] * st[:, None, :, None]
    )
    both_sin = (
        sz[None, :, None, :] * ct[:, None, :, None] + cz[None, :, None, :] * st[:, None, :, None]
    )
    zt_fwd = np.stack([both_cos, -both_sin], 1).reshape(T * 2 * MZ, T * Z)
    zt_bwd = zt_fwd

    cy, sy = (a.astype(np.float64) for a in cos_sin(signed(MY), Y))
    fwd = np.empty((MY, 2, Y, 2))
    fwd[:, 0, :, 0] = cy
    fwd[:, 0, :, 1] = sy
    fwd[:, 1, :, 0] = -sy
    fwd[:, 1, :, 1] = cy
    fwd = fwd.reshape(GX, JL, 2, Y * 2)[GX_ORDER]
    y_fwd = fwd.transpose(1, 2, 0, 3).reshape(MY * 2, Y * 2)
    bwd = np.empty((Y, 2, MY, 2))
    bwd[:, 0, :, 0] = cy.T
    bwd[:, 0, :, 1] = -sy.T
    bwd[:, 1, :, 0] = sy.T
    bwd[:, 1, :, 1] = cy.T
    y_bwd = bwd.reshape(Y * 2, GX, JL * 2)[:, GX_ORDER].reshape(Y * 2, MY * 2)

    cx, sx = (a.astype(np.float64) for a in cos_sin(signed(MX), X))
    fwd = np.empty((X, 2, 2, MX))
    fwd[:, 0, 0, :] = cx.T
    fwd[:, 1, 0, :] = sx.T
    fwd[:, 0, 1, :] = -sx.T
    fwd[:, 1, 1, :] = cx.T
    x_fwd = fwd.reshape(GX, XL * 2, 2 * MX)[GX_ORDER].reshape(X * 2, 2 * MX)
    bwd = np.empty((X, 2, 2, MX))
    bwd[:, 0, 0, :] = cx.T
    bwd[:, 0, 1, :] = -sx.T
    bwd[:, 1, 0, :] = sx.T
    bwd[:, 1, 1, :] = cx.T
    bwd = bwd.reshape(GX, XL, 2, 2 * MX)[GX_ORDER]
    x_bwd = bwd.transpose(1, 2, 0, 3).reshape(X * 2, 2 * MX)
    return tuple(a.astype(BF16) for a in (zt_fwd, zt_bwd, y_fwd, y_bwd, x_fwd, x_bwd))


def dot(left, right, left_dim=1, right_dim=0):
    return lax.dot_general(
        left, right, (((left_dim,), (right_dim,)), ((), ())), preferred_element_type=F32
    )


def swap_bit(low, high, step):
    lane = lax.broadcasted_iota(jnp.int32, low.shape, 1)
    upper = (lane & step) != 0
    first = jnp.where(upper, pltpu.roll(high, step, 1), low)
    second = jnp.where(upper, high, pltpu.roll(low, LANES - step, 1))
    return first, second


def swap_eight(parts):
    parts = list(parts)
    for step in (1, 2, 4):
        for i in range(8):
            if not i & step:
                parts[i], parts[i | step] = swap_bit(parts[i], parts[i | step], step)
    return parts


def gelu_parts(pre):
    square = pre * pre
    inner = pre * (root_two_over_pi + (root_two_over_pi * gelu_cubic) * square)
    half = 0.5 + 0.5 * jnp.tanh(inner)
    rise = pre * (2.0 * root_two_over_pi + (6.0 * root_two_over_pi * gelu_cubic) * square)
    return pre * half, half * (1.0 + (1.0 - half) * rise)


def cells_of(wide_ref, y):
    return jnp.concatenate(
        [wide_ref[pl.ds(t * C * XL * YL + y, C * XL, stride=YL), :] for t in range(T)], 1
    )


def put_cells(wide_ref, y, value):
    for t in range(T):
        wide_ref[pl.ds(t * C * XL * YL + y, C * XL, stride=YL), :] = value[:, t * Z : (t + 1) * Z]


def pack(spread_ref, out_ref):
    for k in range(spread_ref.shape[0]):
        out_ref[:, k * LANES : (k + 1) * LANES] = spread_ref[k].astype(BF16)


def unpack(in_ref, spread_ref):
    for k in range(spread_ref.shape[0]):
        spread_ref[k] = in_ref[:, k * LANES : (k + 1) * LANES].astype(F32)


def put_modes(spread_ref, y, cells, zt_fwd):
    turned = dot(zt_fwd, cells, 1, 1)
    for kt in range(T):
        for p in range(2):
            row = (kt * 2 + p) * MZ
            spread_ref[kt, pl.ds(y * 2 + p, MZ, stride=2 * YL), :] = turned[row : row + MZ]


def modes_of(spread_ref, y):
    return jnp.concatenate(
        [
            spread_ref[kt, pl.ds(y * 2 + p, MZ, stride=2 * YL), :]
            for kt in range(T)
            for p in range(2)
        ],
        0,
    )


def build_zt(table):
    shape = (MZ, Z)
    turns = lax.broadcasted_iota(jnp.int32, shape, 0) * lax.broadcasted_iota(jnp.int32, shape, 1)
    angle = (turns & (Z - 1)).astype(F32) * (2.0 * math.pi / Z)
    cosine = jnp.cos(angle)
    sine = jnp.sin(angle)
    real = (cosine, -sine, -cosine, sine)
    imag = (-sine, -cosine, sine, cosine)
    for kt in range(T):
        for p, part in enumerate((real, imag)):
            row = (kt * 2 + p) * MZ
            for t in range(T):
                table[row : row + MZ, t * Z : (t + 1) * Z] = part[kt * t % T].astype(BF16)


def open_kernel(field_ref, out_ref, wide, spread, table):
    build_zt(table)
    wide[...] = field_ref[...].astype(F32)
    for y in range(YL):
        put_modes(spread, y, cells_of(wide, y).astype(BF16), table[...])
    pack(spread, out_ref)


def y_forward_kernel(in_ref, table_ref, out_ref, spread):
    along_y = dot(table_ref[...], in_ref[...])
    for low in range(2):
        parts = [
            along_y[
                j * 2 * GX : (j + 1) * 2 * GX,
                (kth * 2 + low) * LANES : (kth * 2 + low + 1) * LANES,
            ]
            for kth in range(2)
            for j in range(JL)
        ]
        for x, part in enumerate(swap_eight(parts)):
            for s in range(2):
                spread[low, pl.ds(x * 2 + s, GX, stride=2 * XL), :] = part[s * GX : (s + 1) * GX]
    pack(spread, out_ref)


def to_spectrum(in_ref, x_fwd_ref):
    low, high = (
        dot(in_ref[:, k * LANES : (k + 1) * LANES], x_fwd_ref[...], 0, 0)
        .astype(BF16)
        .astype(F32)
        for k in range(2)
    )
    return swap_bit(low, high, MX)


def from_spectrum(real, imag, x_bwd_ref, out_ref, spread):
    for low, modes in enumerate(swap_bit(real, imag, MX)):
        along_x = dot(x_bwd_ref[...], modes.astype(BF16), 1, 1)
        parts = [along_x[x * 2 * GX : (x + 1) * 2 * GX] for x in range(XL)]
        for i, part in enumerate(swap_eight(parts)):
            kth, j = divmod(i, JL)
            for s in range(2):
                spread[kth * 2 + low, pl.ds(j * 2 + s, GX, stride=2 * JL), :] = part[
                    s * GX : (s + 1) * GX
                ]
    pack(spread, out_ref)


def weight_parts(w_ref, c):
    w = w_ref[c].astype(F32).reshape(C, 2, 8, LANES)
    return w[:, 0], w[:, 1]


def at_channel(ref, c):
    return ref[pl.ds(pl.multiple_of(c * 8, 8), 8), :]


def mix_kernel(
    in_ref, w_ref, scale_ref, x_fwd_ref, x_bwd_ref, out_ref, real_ref, imag_ref, spread
):
    real, imag = to_spectrum(in_ref, x_fwd_ref)
    real_ref[...] = real
    imag_ref[...] = imag

    def add(c, total):
        s_real = at_channel(real_ref, c)[None]
        s_imag = at_channel(imag_ref, c)[None]
        w_real, w_imag = weight_parts(w_ref, c)
        return (
            total[0] + (s_real * w_real - s_imag * w_imag),
            total[1] + (s_real * w_imag + s_imag * w_real),
        )

    zero = jnp.zeros((C, 8, LANES), F32)
    mix_real, mix_imag = lax.fori_loop(0, C, add, (zero, zero), unroll=4)
    scale = scale_ref[0]
    from_spectrum(
        (mix_real * scale).reshape(C * 8, LANES),
        (mix_imag * scale).reshape(C * 8, LANES),
        x_bwd_ref,
        out_ref,
        spread,
    )


def back_kernel(
    in_ref,
    w_ref,
    scale_ref,
    x_fwd_ref,
    x_bwd_ref,
    s_real_ref,
    s_imag_ref,
    layer_ref,
    out_ref,
    grad_hbm,
    layer_hbm,
    real_ref,
    imag_ref,
    back_real,
    back_imag,
    spread,
    grad,
    sems,
):
    send_layer = pltpu.make_async_copy(layer_ref, layer_hbm, sems.at[0])
    send_layer.start()
    real, imag = to_spectrum(in_ref, x_fwd_ref)
    real_ref[...] = real
    imag_ref[...] = imag

    def outer(c, carry):
        s_real = (at_channel(s_real_ref, c).astype(F32) * scale_ref[0])[None, None]
        s_imag = (at_channel(s_imag_ref, c).astype(F32) * scale_ref[0])[None, None]
        a_real = real_ref[...].reshape(C, 1, 8, LANES)
        a_imag = imag_ref[...].reshape(C, 1, 8, LANES)
        both = jnp.concatenate(
            [s_real * a_real + s_imag * a_imag, s_real * a_imag - s_imag * a_real], 1
        )
        grad[c] = both.reshape(C * 2 * 8, LANES).astype(BF16)
        return carry

    lax.fori_loop(0, C, outer, 0, unroll=4)
    send_grad = pltpu.make_async_copy(grad, grad_hbm, sems.at[1])
    send_grad.start()

    def one(c, carry):
        a_real = real_ref[...].reshape(C, 8, LANES)
        a_imag = imag_ref[...].reshape(C, 8, LANES)
        w_real, w_imag = weight_parts(w_ref, c)
        row = pl.ds(pl.multiple_of(c * 8, 8), 8)
        back_real[row, :] = jnp.sum(a_real * w_real + a_imag * w_imag, 0)
        back_imag[row, :] = jnp.sum(a_imag * w_real - a_real * w_imag, 0)
        return carry

    lax.fori_loop(0, C, one, 0, unroll=4)
    scale = scale_ref[0]
    from_spectrum(back_real[...] * scale, back_imag[...] * scale, x_bwd_ref, out_ref, spread)
    send_layer.wait()
    send_grad.wait()


def y_backward_kernel(in_ref, table_ref, out_ref):
    out_ref[...] = dot(table_ref[...], in_ref[...]).astype(BF16)


def point_table(point_ref, back):
    shape = (C * XL, C)
    row = lax.broadcasted_iota(jnp.int32, shape, 0)
    pick = (row // XL == lax.broadcasted_iota(jnp.int32, shape, 1)).astype(F32).astype(BF16)
    half = dot(pick, point_ref[...], 1, 0 if back else 1).astype(BF16)
    full = dot(half, pick, 1, 1)
    row = lax.broadcasted_iota(jnp.int32, full.shape, 0)
    column = lax.broadcasted_iota(jnp.int32, full.shape, 1)
    return jnp.where(row % XL == column % XL, full, 0.0).astype(BF16)


def cell_kernel(
    in_ref,
    field_ref,
    cotangent_ref,
    point_ref,
    zt_bwd_ref,
    zt_fwd_ref,
    out_ref,
    slope_ref,
    layer_ref,
    back_ref,
    wide,
    other,
    spread,
):
    point = point_table(point_ref, False)
    back_ref[...] = point_table(point_ref, True)
    unpack(in_ref, spread)
    modes = [modes_of(spread, y).astype(BF16) for y in range(YL)]
    wide[...] = field_ref[...].astype(F32)
    other[...] = cotangent_ref[...].astype(F32)
    for y in range(YL):
        pre = dot(modes[y], zt_bwd_ref[...], 0, 0) + dot(point, cells_of(wide, y).astype(BF16))
        value, slope = gelu_parts(pre)
        put_cells(wide, y, value)
        slope_ref[y] = (cells_of(other, y) * slope).astype(BF16)
    layer_ref[...] = wide[...].astype(BF16)
    for y in range(YL):
        put_modes(spread, y, slope_ref[y], zt_fwd_ref[...])
    pack(spread, out_ref)


def close_kernel(in_ref, slope_ref, point_ref, zt_bwd_ref, out_hbm, spread, wide, out, sems):
    point = point_ref[...]
    unpack(in_ref, spread)
    for y in range(YL):
        modes = modes_of(spread, y).astype(BF16)
        put_cells(wide, y, dot(modes, zt_bwd_ref[...], 0, 0) + dot(point, slope_ref[y]))
    copies = []
    for t in range(T):
        rows = pl.ds(t * C * XL * YL, C * XL * YL)
        out[rows, :] = wide[rows, :].astype(BF16)
        copies.append(pltpu.make_async_copy(out.at[rows], out_hbm.at[rows], sems.at[t]))
        copies[t].start()
    for copy in copies:
        copy.wait()


ROWS = T * C * XL * YL
ZT = (MZ * YL * 2, T * LANES)
AFTER_Y = (GX * XL * 2, 2 * LANES)
AFTER_X = (GX * JL * 2, T * LANES)
ZT_SPREAD = (T, MZ * YL * 2, LANES)
Y_SPREAD = (2, GX * XL * 2, LANES)
X_SPREAD = (T, GX * JL * 2, LANES)
CELLS = (YL, C * XL, T * Z)
PARTS = (C * 8, LANES)


WIDE = (ROWS, Z)
GRAD = (C, C * 2 * 8, LANES)


def vmem(shape, dtype=F32):
    return pltpu.VMEM(shape, dtype)


def call(kernel, outs, operands, scratch=(), scalars=(), far_outs=(), flops=10**8):
    near = pl.BlockSpec(memory_space=pltpu.VMEM)
    smem = pl.BlockSpec(memory_space=pltpu.SMEM)
    anywhere = pl.BlockSpec(memory_space=pltpu.HBM)
    specs = [smem if i in scalars else near for i in range(len(operands))]
    out_specs = tuple(anywhere if i in far_outs else near for i in range(len(outs)))
    single = len(outs) == 1
    moved = sum(math.prod(o.shape) * o.dtype.itemsize for o in list(outs) + list(operands))
    return pl.pallas_call(
        kernel,
        out_shape=outs[0] if single else tuple(outs),
        in_specs=specs,
        out_specs=out_specs[0] if single else out_specs,
        scratch_shapes=list(scratch),
        cost_estimate=pl.CostEstimate(flops=flops, bytes_accessed=moved, transcendentals=0),
        compiler_params=pltpu.CompilerParams(vmem_limit_bytes=16 * 1024 * 1024),
    )(*operands)


def shaped(shape, dtype=BF16):
    return jax.ShapeDtypeStruct(shape, dtype)


def exchange(block, axis):
    groups = [GX_ORDER] if axis == "gx" else None
    return lax.all_to_all(
        block, axis, split_axis=0, concat_axis=0, axis_index_groups=groups, tiled=True
    )


def open_stage(field):
    scratch = [vmem(WIDE), vmem(ZT_SPREAD), vmem((T * 2 * MZ, T * Z), BF16)]
    return call(open_kernel, [shaped(ZT)], [field], scratch)


def y_forward_stage(block, y_fwd):
    return call(y_forward_kernel, [shaped(AFTER_Y)], [block, y_fwd], [vmem(Y_SPREAD)])


def mix_stage(block, weight, scale, x_fwd, x_bwd):
    return call(
        mix_kernel,
        [shaped(AFTER_X), shaped(PARTS, F32), shaped(PARTS, F32)],
        [block, weight, scale, x_fwd, x_bwd],
        [vmem(X_SPREAD)],
        scalars=(2,),
    )


def y_backward_stage(block, y_bwd):
    return call(y_backward_kernel, [shaped(ZT)], [block, y_bwd])


def cell_stage(block, field, cotangent, point_weight, zt_bwd, zt_fwd):
    return call(
        cell_kernel,
        [shaped(ZT), shaped(CELLS), shaped(WIDE), shaped((C * XL, C * XL))],
        [block, field, cotangent, point_weight, zt_bwd, zt_fwd],
        [vmem(WIDE), vmem(WIDE), vmem(ZT_SPREAD)],
    )


def back_stage(block, weight, scale, x_fwd, x_bwd, spec_real, spec_imag, layer):
    scratch = [vmem(PARTS)] * 4 + [vmem(X_SPREAD), vmem(GRAD, BF16)]
    scratch.append(pltpu.SemaphoreType.DMA((2,)))
    return call(
        back_kernel,
        [shaped(AFTER_X), shaped(GRAD), shaped(WIDE)],
        [block, weight, scale, x_fwd, x_bwd, spec_real, spec_imag, layer],
        scratch,
        scalars=(2,),
        far_outs=(1, 2),
    )


def close_stage(block, slope, point_back, zt_bwd):
    return call(
        close_kernel,
        [shaped(WIDE)],
        [block, slope, point_back, zt_bwd],
        [vmem(ZT_SPREAD), vmem(WIDE), vmem(WIDE, BF16), pltpu.SemaphoreType.DMA((T,))],
        far_outs=(0,),
    )


def on_device(grid_field, spectral_weight, point_weight, cotangent):
    zt_fwd, zt_bwd, y_fwd, y_bwd, x_fwd, x_bwd = (jnp.asarray(a) for a in tables())
    field = grid_field.reshape(WIDE)
    cotan = cotangent.reshape(WIDE)
    weight = spectral_weight.reshape(C, C, JL, 4, LANES).transpose(0, 1, 3, 2, 4).reshape(GRAD)
    kz = lax.axis_index("gy")
    scale = (jnp.where(kz == 0, 1.0, 2.0).astype(F32) / float(X * Y * Z * T)).reshape(1)

    opened = open_stage(field)
    opened, scale = lax.optimization_barrier((opened, scale))
    halved = y_forward_stage(exchange(opened, "gy"), y_fwd)
    mixed, spec_real, spec_imag = mix_stage(exchange(halved, "gx"), weight, scale, x_fwd, x_bwd)
    along_y = y_backward_stage(exchange(mixed, "gx"), y_bwd)
    turned, slope, layer, point_back = cell_stage(
        exchange(along_y, "gy"), field, cotan, point_weight, zt_bwd, zt_fwd
    )
    halved = y_forward_stage(exchange(turned, "gy"), y_fwd)
    back, grad_spectral, layer_out = back_stage(
        exchange(halved, "gx"), weight, scale, x_fwd, x_bwd, spec_real, spec_imag, layer
    )
    along_y = y_backward_stage(exchange(back, "gx"), y_bwd)
    grad_field = close_stage(exchange(along_y, "gy"), slope, point_back, zt_bwd)

    grad_spectral = (
        grad_spectral.reshape(C, C, 4, JL, LANES)
        .transpose(0, 1, 3, 2, 4)
        .reshape(spectral_weight.shape)
    )
    return (
        layer_out.reshape(grid_field.shape),
        grad_field.reshape(grid_field.shape),
        grad_spectral,
    )


def solution(mesh):
    field = P(None, None, None, "gx", "gy", None)
    modes = P(None, None, "gx", "gy", None)
    return jax.shard_map(
        on_device,
        mesh=mesh,
        in_specs=(field, modes, P(), field),
        out_specs=(field, field, modes),
        check_vma=False,
    )
```

```python
import math

import jax
import jax.numpy as jnp
import numpy as np
from jax import lax
from jax.experimental import pallas as pl
from jax.experimental.pallas import tpu as pltpu
from jax.sharding import PartitionSpec as P

T = 4
C = 16
X = 128
Y = 128
Z = 128
MX = 64
MY = 64
MZ = 32
GX = 16
GY = 32
XL = X // GX
YL = Y // GY
JL = MY // GX
LANES = 128
GX_ORDER = [z * 8 + x * 2 + core for z in (1, 0) for x in (2, 0, 3, 1) for core in (1, 0)]

F32 = jnp.float32
BF16 = jnp.bfloat16

root_two_over_pi = math.sqrt(2.0 / math.pi)
gelu_cubic = 0.044715


def signed(kept):
    j = np.arange(kept)
    return np.where(j < kept // 2, j, j - kept)


def cos_sin(freq, length):
    q = np.mod(freq[:, None] * np.arange(length)[None, :], length)
    angle = q * (2.0 * np.pi / length)
    return np.cos(angle).astype(BF16), np.sin(angle).astype(BF16)


def tables():
    cz, sz = (a.astype(np.float64) for a in cos_sin(np.arange(MZ), Z))
    quarter = np.mod(np.arange(T)[:, None] * np.arange(T)[None, :], T)
    ct = np.array([1.0, 0.0, -1.0, 0.0])[quarter]
    st = np.array([0.0, 1.0, 0.0, -1.0])[quarter]
    both_cos = (
        cz[None, :, None, :] * ct[:, None, :, None] - sz[None, :, None, :] * st[:, None, :, None]
    )
    both_sin = (
        sz[None, :, None, :] * ct[:, None, :, None] + cz[None, :, None, :] * st[:, None, :, None]
    )
    zt_fwd = np.stack([both_cos, -both_sin], 1).reshape(T * 2 * MZ, T * Z)
    zt_bwd = zt_fwd

    cy, sy = (a.astype(np.float64) for a in cos_sin(signed(MY), Y))
    fwd = np.empty((MY, 2, Y, 2))
    fwd[:, 0, :, 0] = cy
    fwd[:, 0, :, 1] = sy
    fwd[:, 1, :, 0] = -sy
    fwd[:, 1, :, 1] = cy
    fwd = fwd.reshape(GX, JL, 2, Y * 2)[GX_ORDER]
    y_fwd = fwd.transpose(1, 2, 0, 3).reshape(MY * 2, Y * 2)
    bwd = np.empty((Y, 2, MY, 2))
    bwd[:, 0, :, 0] = cy.T
    bwd[:, 0, :, 1] = -sy.T
    bwd[:, 1, :, 0] = sy.T
    bwd[:, 1, :, 1] = cy.T
    y_bwd = bwd.reshape(Y * 2, GX, JL * 2)[:, GX_ORDER].reshape(Y * 2, MY * 2)

    cx, sx = (a.astype(np.float64) for a in cos_sin(signed(MX), X))
    fwd = np.empty((X, 2, 2, MX))
    fwd[:, 0, 0, :] = cx.T
    fwd[:, 1, 0, :] = sx.T
    fwd[:, 0, 1, :] = -sx.T
    fwd[:, 1, 1, :] = cx.T
    x_fwd = fwd.reshape(GX, XL * 2, 2 * MX)[GX_ORDER].reshape(X * 2, 2 * MX)
    bwd = np.empty((X, 2, 2, MX))
    bwd[:, 0, 0, :] = cx.T
    bwd[:, 0, 1, :] = -sx.T
    bwd[:, 1, 0, :] = sx.T
    bwd[:, 1, 1, :] = cx.T
    bwd = bwd.reshape(GX, XL, 2, 2 * MX)[GX_ORDER]
    x_bwd = bwd.transpose(1, 2, 0, 3).reshape(X * 2, 2 * MX)
    return tuple(a.astype(BF16) for a in (zt_fwd, zt_bwd, y_fwd, y_bwd, x_fwd, x_bwd))


def dot(left, right, left_dim=1, right_dim=0):
    return lax.dot_general(
        left, right, (((left_dim,), (right_dim,)), ((), ())), preferred_element_type=F32
    )


def swap_bit(low, high, step):
    lane = lax.broadcasted_iota(jnp.int32, low.shape, 1)
    upper = (lane & step) != 0
    first = jnp.where(upper, pltpu.roll(high, step, 1), low)
    second = jnp.where(upper, high, pltpu.roll(low, LANES - step, 1))
    return first, second


def swap_eight(parts):
    parts = list(parts)
    for step in (1, 2, 4):
        for i in range(8):
            if not i & step:
                parts[i], parts[i | step] = swap_bit(parts[i], parts[i | step], step)
    return parts


def gelu_parts(pre):
    square = pre * pre
    inner = pre * (root_two_over_pi + (root_two_over_pi * gelu_cubic) * square)
    half = 0.5 + 0.5 * jnp.tanh(inner)
    rise = pre * (2.0 * root_two_over_pi + (6.0 * root_two_over_pi * gelu_cubic) * square)
    return pre * half, half * (1.0 + (1.0 - half) * rise)


def cells_of(wide_ref, y):
    return jnp.concatenate(
        [wide_ref[pl.ds(t * C * XL * YL + y, C * XL, stride=YL), :] for t in range(T)], 1
    )


def put_cells(wide_ref, y, value):
    for t in range(T):
        wide_ref[pl.ds(t * C * XL * YL + y, C * XL, stride=YL), :] = value[:, t * Z : (t + 1) * Z]


def pack(spread_ref, out_ref):
    for k in range(spread_ref.shape[0]):
        out_ref[:, k * LANES : (k + 1) * LANES] = spread_ref[k].astype(BF16)


def unpack(in_ref, spread_ref):
    for k in range(spread_ref.shape[0]):
        spread_ref[k] = in_ref[:, k * LANES : (k + 1) * LANES].astype(F32)


def put_modes(spread_ref, y, cells, zt_fwd):
    turned = dot(zt_fwd, cells, 1, 1)
    for kt in range(T):
        for p in range(2):
            row = (kt * 2 + p) * MZ
            spread_ref[kt, pl.ds(y * 2 + p, MZ, stride=2 * YL), :] = turned[row : row + MZ]


def modes_of(spread_ref, y):
    return jnp.concatenate(
        [
            spread_ref[kt, pl.ds(y * 2 + p, MZ, stride=2 * YL), :]
            for kt in range(T)
            for p in range(2)
        ],
        0,
    )


def build_zt(table):
    shape = (MZ, Z)
    turns = lax.broadcasted_iota(jnp.int32, shape, 0) * lax.broadcasted_iota(jnp.int32, shape, 1)
    angle = (turns & (Z - 1)).astype(F32) * (2.0 * math.pi / Z)
    cosine = jnp.cos(angle)
    sine = jnp.sin(angle)
    real = (cosine, -sine, -cosine, sine)
    imag = (-sine, -cosine, sine, cosine)
    for kt in range(T):
        for p, part in enumerate((real, imag)):
            row = (kt * 2 + p) * MZ
            for t in range(T):
                table[row : row + MZ, t * Z : (t + 1) * Z] = part[kt * t % T].astype(BF16)


def open_kernel(field_hbm, out_ref, field, wide, spread, table, sems):
    copies = []
    for t in range(T):
        rows = pl.ds(t * C * XL * YL, C * XL * YL)
        copies.append(pltpu.make_async_copy(field_hbm.at[rows], field.at[rows], sems.at[t]))
        copies[t].start()
    build_zt(table)
    for t in range(T):
        rows = pl.ds(t * C * XL * YL, C * XL * YL)
        copies[t].wait()
        wide[rows, :] = field[rows, :].astype(F32)
    for y in range(YL):
        put_modes(spread, y, cells_of(wide, y).astype(BF16), table[...])
    pack(spread, out_ref)


def y_forward_kernel(in_ref, table_ref, out_ref, spread):
    along_y = dot(table_ref[...], in_ref[...])
    for low in range(2):
        parts = [
            along_y[
                j * 2 * GX : (j + 1) * 2 * GX,
                (kth * 2 + low) * LANES : (kth * 2 + low + 1) * LANES,
            ]
            for kth in range(2)
            for j in range(JL)
        ]
        for x, part in enumerate(swap_eight(parts)):
            for s in range(2):
                spread[low, pl.ds(x * 2 + s, GX, stride=2 * XL), :] = part[s * GX : (s + 1) * GX]
    pack(spread, out_ref)


def to_spectrum(in_ref, x_fwd_ref):
    low, high = (
        dot(in_ref[:, k * LANES : (k + 1) * LANES], x_fwd_ref[...], 0, 0)
        .astype(BF16)
        .astype(F32)
        for k in range(2)
    )
    return swap_bit(low, high, MX)


def from_spectrum(real, imag, x_bwd_ref, out_ref, spread):
    for low, modes in enumerate(swap_bit(real, imag, MX)):
        along_x = dot(x_bwd_ref[...], modes.astype(BF16), 1, 1)
        parts = [along_x[x * 2 * GX : (x + 1) * 2 * GX] for x in range(XL)]
        for i, part in enumerate(swap_eight(parts)):
            kth, j = divmod(i, JL)
            for s in range(2):
                spread[kth * 2 + low, pl.ds(j * 2 + s, GX, stride=2 * JL), :] = part[
                    s * GX : (s + 1) * GX
                ]
    pack(spread, out_ref)


def weight_parts(w_ref, c):
    w = w_ref[c].astype(F32).reshape(C, 2, 8, LANES)
    return w[:, 0], w[:, 1]


def at_channel(ref, c):
    return ref[pl.ds(pl.multiple_of(c * 8, 8), 8), :]


def mix_kernel(
    in_ref, w_ref, scale_ref, x_fwd_ref, x_bwd_ref, out_ref, real_ref, imag_ref, spread
):
    real, imag = to_spectrum(in_ref, x_fwd_ref)
    real_ref[...] = real
    imag_ref[...] = imag

    def add(c, total):
        s_real = at_channel(real_ref, c)[None]
        s_imag = at_channel(imag_ref, c)[None]
        w_real, w_imag = weight_parts(w_ref, c)
        return (
            total[0] + (s_real * w_real - s_imag * w_imag),
            total[1] + (s_real * w_imag + s_imag * w_real),
        )

    zero = jnp.zeros((C, 8, LANES), F32)
    mix_real, mix_imag = lax.fori_loop(0, C, add, (zero, zero), unroll=4)
    scale = scale_ref[0]
    from_spectrum(
        (mix_real * scale).reshape(C * 8, LANES),
        (mix_imag * scale).reshape(C * 8, LANES),
        x_bwd_ref,
        out_ref,
        spread,
    )


def back_kernel(
    in_ref,
    w_ref,
    scale_ref,
    x_fwd_ref,
    x_bwd_ref,
    s_real_ref,
    s_imag_ref,
    layer_ref,
    out_ref,
    grad_hbm,
    layer_hbm,
    real_ref,
    imag_ref,
    back_real,
    back_imag,
    spread,
    grad,
    sems,
):
    send_layer = pltpu.make_async_copy(layer_ref, layer_hbm, sems.at[0])
    send_layer.start()
    real, imag = to_spectrum(in_ref, x_fwd_ref)
    real_ref[...] = real
    imag_ref[...] = imag

    def outer(c, carry):
        s_real = (at_channel(s_real_ref, c).astype(F32) * scale_ref[0])[None, None]
        s_imag = (at_channel(s_imag_ref, c).astype(F32) * scale_ref[0])[None, None]
        a_real = real_ref[...].reshape(C, 1, 8, LANES)
        a_imag = imag_ref[...].reshape(C, 1, 8, LANES)
        both = jnp.concatenate(
            [s_real * a_real + s_imag * a_imag, s_real * a_imag - s_imag * a_real], 1
        )
        grad[c] = both.reshape(C * 2 * 8, LANES).astype(BF16)
        return carry

    lax.fori_loop(0, C, outer, 0, unroll=4)
    send_grad = pltpu.make_async_copy(grad, grad_hbm, sems.at[1])
    send_grad.start()

    def one(c, carry):
        a_real = real_ref[...].reshape(C, 8, LANES)
        a_imag = imag_ref[...].reshape(C, 8, LANES)
        w_real, w_imag = weight_parts(w_ref, c)
        row = pl.ds(pl.multiple_of(c * 8, 8), 8)
        back_real[row, :] = jnp.sum(a_real * w_real + a_imag * w_imag, 0)
        back_imag[row, :] = jnp.sum(a_imag * w_real - a_real * w_imag, 0)
        return carry

    lax.fori_loop(0, C, one, 0, unroll=4)
    scale = scale_ref[0]
    from_spectrum(back_real[...] * scale, back_imag[...] * scale, x_bwd_ref, out_ref, spread)
    send_layer.wait()
    send_grad.wait()


def y_backward_kernel(in_ref, table_ref, out_ref):
    out_ref[...] = dot(table_ref[...], in_ref[...]).astype(BF16)


def point_table(point_ref, back):
    shape = (C * XL, C)
    row = lax.broadcasted_iota(jnp.int32, shape, 0)
    pick = (row // XL == lax.broadcasted_iota(jnp.int32, shape, 1)).astype(F32).astype(BF16)
    half = dot(pick, point_ref[...], 1, 0 if back else 1).astype(BF16)
    full = dot(half, pick, 1, 1)
    row = lax.broadcasted_iota(jnp.int32, full.shape, 0)
    column = lax.broadcasted_iota(jnp.int32, full.shape, 1)
    return jnp.where(row % XL == column % XL, full, 0.0).astype(BF16)


def cell_kernel(
    in_ref,
    field_ref,
    cotangent_ref,
    point_ref,
    zt_bwd_ref,
    zt_fwd_ref,
    out_ref,
    slope_ref,
    layer_ref,
    back_ref,
    wide,
    other,
    spread,
):
    point = point_table(point_ref, False)
    back_ref[...] = point_table(point_ref, True)
    unpack(in_ref, spread)
    modes = [modes_of(spread, y).astype(BF16) for y in range(YL)]
    wide[...] = field_ref[...].astype(F32)
    other[...] = cotangent_ref[...].astype(F32)
    for y in range(YL):
        pre = dot(modes[y], zt_bwd_ref[...], 0, 0) + dot(point, cells_of(wide, y).astype(BF16))
        value, slope = gelu_parts(pre)
        put_cells(wide, y, value)
        slope_ref[y] = (cells_of(other, y) * slope).astype(BF16)
    layer_ref[...] = wide[...].astype(BF16)
    for y in range(YL):
        put_modes(spread, y, slope_ref[y], zt_fwd_ref[...])
    pack(spread, out_ref)


def close_kernel(in_ref, slope_ref, point_ref, zt_bwd_ref, out_hbm, spread, wide, out, sems):
    point = point_ref[...]
    unpack(in_ref, spread)
    for y in range(YL):
        modes = modes_of(spread, y).astype(BF16)
        put_cells(wide, y, dot(modes, zt_bwd_ref[...], 0, 0) + dot(point, slope_ref[y]))
    copies = []
    for t in range(T):
        rows = pl.ds(t * C * XL * YL, C * XL * YL)
        out[rows, :] = wide[rows, :].astype(BF16)
        copies.append(pltpu.make_async_copy(out.at[rows], out_hbm.at[rows], sems.at[t]))
        copies[t].start()
    for copy in copies:
        copy.wait()


ROWS = T * C * XL * YL
ZT = (MZ * YL * 2, T * LANES)
AFTER_Y = (GX * XL * 2, 2 * LANES)
AFTER_X = (GX * JL * 2, T * LANES)
ZT_SPREAD = (T, MZ * YL * 2, LANES)
Y_SPREAD = (2, GX * XL * 2, LANES)
X_SPREAD = (T, GX * JL * 2, LANES)
CELLS = (YL, C * XL, T * Z)
PARTS = (C * 8, LANES)


WIDE = (ROWS, Z)
GRAD = (C, C * 2 * 8, LANES)
GRANT = 16 * 1024 * 1024
OPEN_GRANT = 64 * 1024 * 1024 - 448 * 1024


def vmem(shape, dtype=F32):
    return pltpu.VMEM(shape, dtype)


def call(kernel, outs, operands, scratch=(), scalars=(), far=(), far_outs=(), grant=GRANT):
    near = pl.BlockSpec(memory_space=pltpu.VMEM)
    smem = pl.BlockSpec(memory_space=pltpu.SMEM)
    anywhere = pl.BlockSpec(memory_space=pltpu.HBM)
    specs = [
        smem if i in scalars else anywhere if i in far else near for i in range(len(operands))
    ]
    out_specs = tuple(anywhere if i in far_outs else near for i in range(len(outs)))
    single = len(outs) == 1
    moved = sum(math.prod(o.shape) * o.dtype.itemsize for o in list(outs) + list(operands))
    return pl.pallas_call(
        kernel,
        out_shape=outs[0] if single else tuple(outs),
        in_specs=specs,
        out_specs=out_specs[0] if single else out_specs,
        scratch_shapes=list(scratch),
        cost_estimate=pl.CostEstimate(flops=10**8, bytes_accessed=moved, transcendentals=0),
        compiler_params=pltpu.CompilerParams(vmem_limit_bytes=grant),
    )(*operands)


def shaped(shape, dtype=BF16):
    return jax.ShapeDtypeStruct(shape, dtype)


def exchange(block, axis):
    groups = [GX_ORDER] if axis == "gx" else None
    return lax.all_to_all(
        block, axis, split_axis=0, concat_axis=0, axis_index_groups=groups, tiled=True
    )


def open_stage(field):
    scratch = [vmem(WIDE, BF16), vmem(WIDE), vmem(ZT_SPREAD), vmem((T * 2 * MZ, T * Z), BF16)]
    scratch.append(pltpu.SemaphoreType.DMA((T,)))
    return call(open_kernel, [shaped(ZT)], [field], scratch, far=(0,), grant=OPEN_GRANT)


def y_forward_stage(block, y_fwd):
    return call(y_forward_kernel, [shaped(AFTER_Y)], [block, y_fwd], [vmem(Y_SPREAD)])


def mix_stage(block, weight, scale, x_fwd, x_bwd):
    return call(
        mix_kernel,
        [shaped(AFTER_X), shaped(PARTS, F32), shaped(PARTS, F32)],
        [block, weight, scale, x_fwd, x_bwd],
        [vmem(X_SPREAD)],
        scalars=(2,),
    )


def y_backward_stage(block, y_bwd):
    return call(y_backward_kernel, [shaped(ZT)], [block, y_bwd])


def cell_stage(block, field, cotangent, point_weight, zt_bwd, zt_fwd):
    return call(
        cell_kernel,
        [shaped(ZT), shaped(CELLS), shaped(WIDE), shaped((C * XL, C * XL))],
        [block, field, cotangent, point_weight, zt_bwd, zt_fwd],
        [vmem(WIDE), vmem(WIDE), vmem(ZT_SPREAD)],
    )


def back_stage(block, weight, scale, x_fwd, x_bwd, spec_real, spec_imag, layer):
    scratch = [vmem(PARTS)] * 4 + [vmem(X_SPREAD), vmem(GRAD, BF16)]
    scratch.append(pltpu.SemaphoreType.DMA((2,)))
    return call(
        back_kernel,
        [shaped(AFTER_X), shaped(GRAD), shaped(WIDE)],
        [block, weight, scale, x_fwd, x_bwd, spec_real, spec_imag, layer],
        scratch,
        scalars=(2,),
        far_outs=(1, 2),
    )


def close_stage(block, slope, point_back, zt_bwd):
    return call(
        close_kernel,
        [shaped(WIDE)],
        [block, slope, point_back, zt_bwd],
        [vmem(ZT_SPREAD), vmem(WIDE), vmem(WIDE, BF16), pltpu.SemaphoreType.DMA((T,))],
        far_outs=(0,),
    )


def on_device(grid_field, spectral_weight, point_weight, cotangent):
    zt_fwd, zt_bwd, y_fwd, y_bwd, x_fwd, x_bwd = (jnp.asarray(a) for a in tables())
    field = grid_field.reshape(WIDE)
    cotan = cotangent.reshape(WIDE)
    weight = spectral_weight.reshape(C, C, JL, 4, LANES).transpose(0, 1, 3, 2, 4).reshape(GRAD)
    kz = lax.axis_index("gy")
    scale = (jnp.where(kz == 0, 1.0, 2.0).astype(F32) / float(X * Y * Z * T)).reshape(1)

    opened = open_stage(field)
    opened, scale = lax.optimization_barrier((opened, scale))
    halved = y_forward_stage(exchange(opened, "gy"), y_fwd)
    mixed, spec_real, spec_imag = mix_stage(exchange(halved, "gx"), weight, scale, x_fwd, x_bwd)
    along_y = y_backward_stage(exchange(mixed, "gx"), y_bwd)
    turned, slope, layer, point_back = cell_stage(
        exchange(along_y, "gy"), field, cotan, point_weight, zt_bwd, zt_fwd
    )
    halved = y_forward_stage(exchange(turned, "gy"), y_fwd)
    back, grad_spectral, layer_out = back_stage(
        exchange(halved, "gx"), weight, scale, x_fwd, x_bwd, spec_real, spec_imag, layer
    )
    along_y = y_backward_stage(exchange(back, "gx"), y_bwd)
    grad_field = close_stage(exchange(along_y, "gy"), slope, point_back, zt_bwd)

    grad_spectral = (
        grad_spectral.reshape(C, C, 4, JL, LANES)
        .transpose(0, 1, 3, 2, 4)
        .reshape(spectral_weight.shape)
    )
    return (
        layer_out.reshape(grid_field.shape),
        grad_field.reshape(grid_field.shape),
        grad_spectral,
    )


def solution(mesh):
    field = P(None, None, None, "gx", "gy", None)
    modes = P(None, None, "gx", "gy", None)
    return jax.shard_map(
        on_device,
        mesh=mesh,
        in_specs=(field, modes, P(), field),
        out_specs=(field, field, modes),
        check_vma=False,
    )
```

```python
import math

import jax
import jax.numpy as jnp
import numpy as np
from jax import lax
from jax.experimental import pallas as pl
from jax.experimental.pallas import tpu as pltpu
from jax.sharding import PartitionSpec as P

T = 4
C = 16
X = 128
Y = 128
Z = 128
MX = 64
MY = 64
MZ = 32
GX = 16
GY = 32
XL = X // GX
YL = Y // GY
JL = MY // GX
LANES = 128
GX_ORDER = [z * 8 + x * 2 + core for z in (1, 0) for x in (2, 0, 3, 1) for core in (1, 0)]

F32 = jnp.float32
BF16 = jnp.bfloat16

root_two_over_pi = math.sqrt(2.0 / math.pi)
gelu_cubic = 0.044715


def signed(kept):
    j = np.arange(kept)
    return np.where(j < kept // 2, j, j - kept)


def cos_sin(freq, length):
    q = np.mod(freq[:, None] * np.arange(length)[None, :], length)
    angle = q * (2.0 * np.pi / length)
    return np.cos(angle).astype(BF16), np.sin(angle).astype(BF16)


def tables():
    cz, sz = (a.astype(np.float64) for a in cos_sin(np.arange(MZ), Z))
    quarter = np.mod(np.arange(T)[:, None] * np.arange(T)[None, :], T)
    ct = np.array([1.0, 0.0, -1.0, 0.0])[quarter]
    st = np.array([0.0, 1.0, 0.0, -1.0])[quarter]
    both_cos = (
        cz[None, :, None, :] * ct[:, None, :, None] - sz[None, :, None, :] * st[:, None, :, None]
    )
    both_sin = (
        sz[None, :, None, :] * ct[:, None, :, None] + cz[None, :, None, :] * st[:, None, :, None]
    )
    zt_fwd = np.stack([both_cos, -both_sin], 1).reshape(T * 2 * MZ, T * Z)
    zt_bwd = zt_fwd

    cy, sy = (a.astype(np.float64) for a in cos_sin(signed(MY), Y))
    fwd = np.empty((MY, 2, Y, 2))
    fwd[:, 0, :, 0] = cy
    fwd[:, 0, :, 1] = sy
    fwd[:, 1, :, 0] = -sy
    fwd[:, 1, :, 1] = cy
    fwd = fwd.reshape(GX, JL, 2, Y * 2)[GX_ORDER]
    y_fwd = fwd.transpose(1, 2, 0, 3).reshape(MY * 2, Y * 2)
    bwd = np.empty((Y, 2, MY, 2))
    bwd[:, 0, :, 0] = cy.T
    bwd[:, 0, :, 1] = -sy.T
    bwd[:, 1, :, 0] = sy.T
    bwd[:, 1, :, 1] = cy.T
    y_bwd = bwd.reshape(Y * 2, GX, JL * 2)[:, GX_ORDER].reshape(Y * 2, MY * 2)

    cx, sx = (a.astype(np.float64) for a in cos_sin(signed(MX), X))
    fwd = np.empty((X, 2, 2, MX))
    fwd[:, 0, 0, :] = cx.T
    fwd[:, 1, 0, :] = sx.T
    fwd[:, 0, 1, :] = -sx.T
    fwd[:, 1, 1, :] = cx.T
    x_fwd = fwd.reshape(GX, XL * 2, 2 * MX)[GX_ORDER].reshape(X * 2, 2 * MX)
    bwd = np.empty((X, 2, 2, MX))
    bwd[:, 0, 0, :] = cx.T
    bwd[:, 0, 1, :] = -sx.T
    bwd[:, 1, 0, :] = sx.T
    bwd[:, 1, 1, :] = cx.T
    bwd = bwd.reshape(GX, XL, 2, 2 * MX)[GX_ORDER]
    x_bwd = bwd.transpose(1, 2, 0, 3).reshape(X * 2, 2 * MX)
    return tuple(a.astype(BF16) for a in (zt_fwd, zt_bwd, y_fwd, y_bwd, x_fwd, x_bwd))


def dot(left, right, left_dim=1, right_dim=0):
    return lax.dot_general(
        left, right, (((left_dim,), (right_dim,)), ((), ())), preferred_element_type=F32
    )


def swap_bit(low, high, step):
    lane = lax.broadcasted_iota(jnp.int32, low.shape, 1)
    upper = (lane & step) != 0
    first = jnp.where(upper, pltpu.roll(high, step, 1), low)
    second = jnp.where(upper, high, pltpu.roll(low, LANES - step, 1))
    return first, second


def swap_eight(parts):
    parts = list(parts)
    for step in (1, 2, 4):
        for i in range(8):
            if not i & step:
                parts[i], parts[i | step] = swap_bit(parts[i], parts[i | step], step)
    return parts


def gelu_parts(pre):
    square = pre * pre
    inner = pre * (root_two_over_pi + (root_two_over_pi * gelu_cubic) * square)
    half = 0.5 + 0.5 * jnp.tanh(inner)
    rise = pre * (2.0 * root_two_over_pi + (6.0 * root_two_over_pi * gelu_cubic) * square)
    return pre * half, half * (1.0 + (1.0 - half) * rise)


def cells_of(wide_ref, y):
    return jnp.concatenate(
        [wide_ref[pl.ds(t * C * XL * YL + y, C * XL, stride=YL), :] for t in range(T)], 1
    )


def put_cells(wide_ref, y, value):
    for t in range(T):
        wide_ref[pl.ds(t * C * XL * YL + y, C * XL, stride=YL), :] = value[:, t * Z : (t + 1) * Z]


def pack(spread_ref, out_ref):
    for k in range(spread_ref.shape[0]):
        block = spread_ref[k, 0 : out_ref.shape[0], :]
        out_ref[:, k * LANES : (k + 1) * LANES] = block.astype(BF16)


def unpack(in_ref, spread_ref):
    for k in range(spread_ref.shape[0]):
        block = in_ref[:, k * LANES : (k + 1) * LANES].astype(F32)
        spread_ref[k, 0 : in_ref.shape[0], :] = block


def put_modes(spread_ref, y, cells, zt_fwd):
    turned = dot(zt_fwd, cells, 1, 1)
    for kt in range(T):
        for p in range(2):
            row = (kt * 2 + p) * MZ
            spread_ref[kt, pl.ds(y * 2 + p, MZ, stride=2 * YL), :] = turned[row : row + MZ]


def modes_of(spread_ref, y):
    return jnp.concatenate(
        [
            spread_ref[kt, pl.ds(y * 2 + p, MZ, stride=2 * YL), :]
            for kt in range(T)
            for p in range(2)
        ],
        0,
    )


def build_zt(table):
    shape = (MZ, Z)
    turns = lax.broadcasted_iota(jnp.int32, shape, 0) * lax.broadcasted_iota(jnp.int32, shape, 1)
    angle = (turns & (Z - 1)).astype(F32) * (2.0 * math.pi / Z)
    cosine = jnp.cos(angle)
    sine = jnp.sin(angle)
    real = (cosine, -sine, -cosine, sine)
    imag = (-sine, -cosine, sine, cosine)
    for kt in range(T):
        for p, part in enumerate((real, imag)):
            row = (kt * 2 + p) * MZ
            for t in range(T):
                table[row : row + MZ, t * Z : (t + 1) * Z] = part[kt * t % T].astype(BF16)


def open_kernel(field_ref, out_ref, wide, spread, table):
    build_zt(table)
    wide[0:ROWS, :] = field_ref[...].astype(F32)
    for y in range(YL):
        put_modes(spread, y, cells_of(wide, y).astype(BF16), table[...])
    pack(spread, out_ref)


def y_forward_kernel(in_ref, table_ref, out_ref, spread):
    along_y = dot(table_ref[...], in_ref[...])
    for low in range(2):
        parts = [
            along_y[
                j * 2 * GX : (j + 1) * 2 * GX,
                (kth * 2 + low) * LANES : (kth * 2 + low + 1) * LANES,
            ]
            for kth in range(2)
            for j in range(JL)
        ]
        for x, part in enumerate(swap_eight(parts)):
            for s in range(2):
                spread[low, pl.ds(x * 2 + s, GX, stride=2 * XL), :] = part[s * GX : (s + 1) * GX]
    pack(spread, out_ref)


def to_spectrum(in_ref, x_fwd_ref):
    low, high = (
        dot(in_ref[:, k * LANES : (k + 1) * LANES], x_fwd_ref[...], 0, 0)
        .astype(BF16)
        .astype(F32)
        for k in range(2)
    )
    return swap_bit(low, high, MX)


def from_spectrum(real, imag, x_bwd_ref, out_ref, spread):
    for low, modes in enumerate(swap_bit(real, imag, MX)):
        along_x = dot(x_bwd_ref[...], modes.astype(BF16), 1, 1)
        parts = [along_x[x * 2 * GX : (x + 1) * 2 * GX] for x in range(XL)]
        for i, part in enumerate(swap_eight(parts)):
            kth, j = divmod(i, JL)
            for s in range(2):
                spread[kth * 2 + low, pl.ds(j * 2 + s, GX, stride=2 * JL), :] = part[
                    s * GX : (s + 1) * GX
                ]
    pack(spread, out_ref)


def weight_parts(w_ref, c):
    w = w_ref[c].astype(F32).reshape(C, 2, 8, LANES)
    return w[:, 0], w[:, 1]


def at_channel(ref, c):
    return ref[pl.ds(pl.multiple_of(c * 8, 8), 8), :]


def mix_kernel(
    in_ref, w_ref, scale_ref, x_fwd_ref, x_bwd_ref, out_ref, real_ref, imag_ref, spread
):
    real, imag = to_spectrum(in_ref, x_fwd_ref)
    real_ref[...] = real
    imag_ref[...] = imag

    def add(c, total):
        s_real = at_channel(real_ref, c)[None]
        s_imag = at_channel(imag_ref, c)[None]
        w_real, w_imag = weight_parts(w_ref, c)
        return (
            total[0] + (s_real * w_real - s_imag * w_imag),
            total[1] + (s_real * w_imag + s_imag * w_real),
        )

    zero = jnp.zeros((C, 8, LANES), F32)
    mix_real, mix_imag = lax.fori_loop(0, C, add, (zero, zero), unroll=4)
    scale = scale_ref[0]
    from_spectrum(
        (mix_real * scale).reshape(C * 8, LANES),
        (mix_imag * scale).reshape(C * 8, LANES),
        x_bwd_ref,
        out_ref,
        spread,
    )


def back_kernel(
    in_ref,
    w_ref,
    scale_ref,
    x_fwd_ref,
    x_bwd_ref,
    s_real_ref,
    s_imag_ref,
    layer_ref,
    out_ref,
    grad_hbm,
    layer_hbm,
    real_ref,
    imag_ref,
    back_real,
    back_imag,
    spread,
    grad,
    sems,
):
    send_layer = pltpu.make_async_copy(layer_ref, layer_hbm, sems.at[0])
    send_layer.start()
    real, imag = to_spectrum(in_ref, x_fwd_ref)
    real_ref[...] = real
    imag_ref[...] = imag

    def outer(c, carry):
        s_real = (at_channel(s_real_ref, c).astype(F32) * scale_ref[0])[None, None]
        s_imag = (at_channel(s_imag_ref, c).astype(F32) * scale_ref[0])[None, None]
        a_real = real_ref[...].reshape(C, 1, 8, LANES)
        a_imag = imag_ref[...].reshape(C, 1, 8, LANES)
        both = jnp.concatenate(
            [s_real * a_real + s_imag * a_imag, s_real * a_imag - s_imag * a_real], 1
        )
        grad[c] = both.reshape(C * 2 * 8, LANES).astype(BF16)
        return carry

    lax.fori_loop(0, C, outer, 0, unroll=4)
    send_grad = pltpu.make_async_copy(grad, grad_hbm, sems.at[1])
    send_grad.start()

    def one(c, carry):
        a_real = real_ref[...].reshape(C, 8, LANES)
        a_imag = imag_ref[...].reshape(C, 8, LANES)
        w_real, w_imag = weight_parts(w_ref, c)
        row = pl.ds(pl.multiple_of(c * 8, 8), 8)
        back_real[row, :] = jnp.sum(a_real * w_real + a_imag * w_imag, 0)
        back_imag[row, :] = jnp.sum(a_imag * w_real - a_real * w_imag, 0)
        return carry

    lax.fori_loop(0, C, one, 0, unroll=4)
    scale = scale_ref[0]
    from_spectrum(back_real[...] * scale, back_imag[...] * scale, x_bwd_ref, out_ref, spread)
    send_layer.wait()
    send_grad.wait()


def y_backward_kernel(in_ref, table_ref, out_ref):
    out_ref[...] = dot(table_ref[...], in_ref[...]).astype(BF16)


def point_table(point_ref, back):
    shape = (C * XL, C)
    row = lax.broadcasted_iota(jnp.int32, shape, 0)
    pick = (row // XL == lax.broadcasted_iota(jnp.int32, shape, 1)).astype(F32).astype(BF16)
    half = dot(pick, point_ref[...], 1, 0 if back else 1).astype(BF16)
    full = dot(half, pick, 1, 1)
    row = lax.broadcasted_iota(jnp.int32, full.shape, 0)
    column = lax.broadcasted_iota(jnp.int32, full.shape, 1)
    return jnp.where(row % XL == column % XL, full, 0.0).astype(BF16)


def cell_kernel(
    in_ref,
    field_ref,
    cotangent_ref,
    point_ref,
    zt_bwd_ref,
    zt_fwd_ref,
    out_ref,
    slope_ref,
    layer_ref,
    back_ref,
    wide,
    other,
    spread,
):
    point = point_table(point_ref, False)
    back_ref[...] = point_table(point_ref, True)
    unpack(in_ref, spread)
    modes = [modes_of(spread, y).astype(BF16) for y in range(YL)]
    wide[0:ROWS, :] = field_ref[...].astype(F32)
    other[0:ROWS, :] = cotangent_ref[...].astype(F32)
    for y in range(YL):
        pre = dot(modes[y], zt_bwd_ref[...], 0, 0) + dot(point, cells_of(wide, y).astype(BF16))
        value, slope = gelu_parts(pre)
        put_cells(wide, y, value)
        slope_ref[y] = (cells_of(other, y) * slope).astype(BF16)
    layer_ref[...] = wide[0:ROWS, :].astype(BF16)
    for y in range(YL):
        put_modes(spread, y, slope_ref[y], zt_fwd_ref[...])
    pack(spread, out_ref)


def close_kernel(in_ref, slope_ref, point_ref, zt_bwd_ref, out_hbm, spread, wide, out, sems):
    point = point_ref[...]
    unpack(in_ref, spread)
    for y in range(YL):
        modes = modes_of(spread, y).astype(BF16)
        put_cells(wide, y, dot(modes, zt_bwd_ref[...], 0, 0) + dot(point, slope_ref[y]))
    copies = []
    for t in range(T):
        rows = pl.ds(t * C * XL * YL, C * XL * YL)
        out[rows, :] = wide[rows, :].astype(BF16)
        copies.append(pltpu.make_async_copy(out.at[rows], out_hbm.at[rows], sems.at[t]))
        copies[t].start()
    for copy in copies:
        copy.wait()


ROWS = T * C * XL * YL
ZT = (MZ * YL * 2, T * LANES)
AFTER_Y = (GX * XL * 2, 2 * LANES)
AFTER_X = (GX * JL * 2, T * LANES)
ZT_SPREAD = (T, MZ * YL * 2 + 16, LANES)
Y_SPREAD = (2, GX * XL * 2 + 16, LANES)
X_SPREAD = (T, GX * JL * 2 + 16, LANES)
CELLS = (YL, C * XL, T * Z)
PARTS = (C * 8, LANES)


WIDE = (ROWS, Z)
WIDE_SPREAD = (ROWS + 16, Z)
GRAD = (C, C * 2 * 8, LANES)


def vmem(shape, dtype=F32):
    return pltpu.VMEM(shape, dtype)


def call(kernel, outs, operands, scratch=(), scalars=(), far_outs=(), flops=10**8):
    near = pl.BlockSpec(memory_space=pltpu.VMEM)
    smem = pl.BlockSpec(memory_space=pltpu.SMEM)
    anywhere = pl.BlockSpec(memory_space=pltpu.HBM)
    specs = [smem if i in scalars else near for i in range(len(operands))]
    out_specs = tuple(anywhere if i in far_outs else near for i in range(len(outs)))
    single = len(outs) == 1
    moved = sum(math.prod(o.shape) * o.dtype.itemsize for o in list(outs) + list(operands))
    return pl.pallas_call(
        kernel,
        out_shape=outs[0] if single else tuple(outs),
        in_specs=specs,
        out_specs=out_specs[0] if single else out_specs,
        scratch_shapes=list(scratch),
        cost_estimate=pl.CostEstimate(flops=flops, bytes_accessed=moved, transcendentals=0),
        compiler_params=pltpu.CompilerParams(vmem_limit_bytes=16 * 1024 * 1024),
    )(*operands)


def shaped(shape, dtype=BF16):
    return jax.ShapeDtypeStruct(shape, dtype)


def exchange(block, axis):
    groups = [GX_ORDER] if axis == "gx" else None
    return lax.all_to_all(
        block, axis, split_axis=0, concat_axis=0, axis_index_groups=groups, tiled=True
    )


def open_stage(field):
    scratch = [vmem(WIDE_SPREAD), vmem(ZT_SPREAD), vmem((T * 2 * MZ, T * Z), BF16)]
    return call(open_kernel, [shaped(ZT)], [field], scratch)


def y_forward_stage(block, y_fwd):
    return call(y_forward_kernel, [shaped(AFTER_Y)], [block, y_fwd], [vmem(Y_SPREAD)])


def mix_stage(block, weight, scale, x_fwd, x_bwd):
    return call(
        mix_kernel,
        [shaped(AFTER_X), shaped(PARTS, F32), shaped(PARTS, F32)],
        [block, weight, scale, x_fwd, x_bwd],
        [vmem(X_SPREAD)],
        scalars=(2,),
    )


def y_backward_stage(block, y_bwd):
    return call(y_backward_kernel, [shaped(ZT)], [block, y_bwd])


def cell_stage(block, field, cotangent, point_weight, zt_bwd, zt_fwd):
    return call(
        cell_kernel,
        [shaped(ZT), shaped(CELLS), shaped(WIDE), shaped((C * XL, C * XL))],
        [block, field, cotangent, point_weight, zt_bwd, zt_fwd],
        [vmem(WIDE_SPREAD), vmem(WIDE_SPREAD), vmem(ZT_SPREAD)],
    )


def back_stage(block, weight, scale, x_fwd, x_bwd, spec_real, spec_imag, layer):
    scratch = [vmem(PARTS)] * 4 + [vmem(X_SPREAD), vmem(GRAD, BF16)]
    scratch.append(pltpu.SemaphoreType.DMA((2,)))
    return call(
        back_kernel,
        [shaped(AFTER_X), shaped(GRAD), shaped(WIDE)],
        [block, weight, scale, x_fwd, x_bwd, spec_real, spec_imag, layer],
        scratch,
        scalars=(2,),
        far_outs=(1, 2),
    )


def close_stage(block, slope, point_back, zt_bwd):
    return call(
        close_kernel,
        [shaped(WIDE)],
        [block, slope, point_back, zt_bwd],
        [vmem(ZT_SPREAD), vmem(WIDE_SPREAD), vmem(WIDE, BF16), pltpu.SemaphoreType.DMA((T,))],
        far_outs=(0,),
    )


def on_device(grid_field, spectral_weight, point_weight, cotangent):
    zt_fwd, zt_bwd, y_fwd, y_bwd, x_fwd, x_bwd = (jnp.asarray(a) for a in tables())
    field = grid_field.reshape(WIDE)
    cotan = cotangent.reshape(WIDE)
    weight = spectral_weight.reshape(C, C, JL, 4, LANES).transpose(0, 1, 3, 2, 4).reshape(GRAD)
    kz = lax.axis_index("gy")
    scale = (jnp.where(kz == 0, 1.0, 2.0).astype(F32) / float(X * Y * Z * T)).reshape(1)

    opened = open_stage(field)
    opened, scale = lax.optimization_barrier((opened, scale))
    halved = y_forward_stage(exchange(opened, "gy"), y_fwd)
    mixed, spec_real, spec_imag = mix_stage(exchange(halved, "gx"), weight, scale, x_fwd, x_bwd)
    along_y = y_backward_stage(exchange(mixed, "gx"), y_bwd)
    turned, slope, layer, point_back = cell_stage(
        exchange(along_y, "gy"), field, cotan, point_weight, zt_bwd, zt_fwd
    )
    halved = y_forward_stage(exchange(turned, "gy"), y_fwd)
    back, grad_spectral, layer_out = back_stage(
        exchange(halved, "gx"), weight, scale, x_fwd, x_bwd, spec_real, spec_imag, layer
    )
    along_y = y_backward_stage(exchange(back, "gx"), y_bwd)
    grad_field = close_stage(exchange(along_y, "gy"), slope, point_back, zt_bwd)

    grad_spectral = (
        grad_spectral.reshape(C, C, 4, JL, LANES)
        .transpose(0, 1, 3, 2, 4)
        .reshape(spectral_weight.shape)
    )
    return (
        layer_out.reshape(grid_field.shape),
        grad_field.reshape(grid_field.shape),
        grad_spectral,
    )


def solution(mesh):
    field = P(None, None, None, "gx", "gy", None)
    modes = P(None, None, "gx", "gy", None)
    return jax.shard_map(
        on_device,
        mesh=mesh,
        in_specs=(field, modes, P(), field),
        out_specs=(field, field, modes),
        check_vma=False,
    )
```

```python
import math

import jax
import jax.numpy as jnp
import numpy as np
from jax import lax
from jax.experimental import pallas as pl
from jax.experimental.pallas import tpu as pltpu
from jax.sharding import PartitionSpec as P

T = 4
C = 16
X = 128
Y = 128
Z = 128
MX = 64
MY = 64
MZ = 32
GX = 16
GY = 32
XL = X // GX
YL = Y // GY
JL = MY // GX
LANES = 128
GX_ORDER = [z * 8 + x * 2 + core for z in (1, 0) for x in (2, 0, 3, 1) for core in (1, 0)]

F32 = jnp.float32
BF16 = jnp.bfloat16

root_two_over_pi = math.sqrt(2.0 / math.pi)
gelu_cubic = 0.044715


def signed(kept):
    j = np.arange(kept)
    return np.where(j < kept // 2, j, j - kept)


def cos_sin(freq, length):
    q = np.mod(freq[:, None] * np.arange(length)[None, :], length)
    angle = q * (2.0 * np.pi / length)
    return np.cos(angle).astype(BF16), np.sin(angle).astype(BF16)


def tables():
    cz, sz = (a.astype(np.float64) for a in cos_sin(np.arange(MZ), Z))
    quarter = np.mod(np.arange(T)[:, None] * np.arange(T)[None, :], T)
    ct = np.array([1.0, 0.0, -1.0, 0.0])[quarter]
    st = np.array([0.0, 1.0, 0.0, -1.0])[quarter]
    both_cos = (
        cz[None, :, None, :] * ct[:, None, :, None] - sz[None, :, None, :] * st[:, None, :, None]
    )
    both_sin = (
        sz[None, :, None, :] * ct[:, None, :, None] + cz[None, :, None, :] * st[:, None, :, None]
    )
    zt_fwd = np.stack([both_cos, -both_sin], 1).reshape(T * 2 * MZ, T * Z)
    zt_bwd = zt_fwd

    cy, sy = (a.astype(np.float64) for a in cos_sin(signed(MY), Y))
    fwd = np.empty((MY, 2, Y, 2))
    fwd[:, 0, :, 0] = cy
    fwd[:, 0, :, 1] = sy
    fwd[:, 1, :, 0] = -sy
    fwd[:, 1, :, 1] = cy
    fwd = fwd.reshape(GX, JL, 2, Y * 2)[GX_ORDER]
    y_fwd = fwd.transpose(1, 2, 0, 3).reshape(MY * 2, Y * 2)
    bwd = np.empty((Y, 2, MY, 2))
    bwd[:, 0, :, 0] = cy.T
    bwd[:, 0, :, 1] = -sy.T
    bwd[:, 1, :, 0] = sy.T
    bwd[:, 1, :, 1] = cy.T
    y_bwd = bwd.reshape(Y * 2, GX, JL * 2)[:, GX_ORDER].reshape(Y * 2, MY * 2)

    cx, sx = (a.astype(np.float64) for a in cos_sin(signed(MX), X))
    fwd = np.empty((X, 2, 2, MX))
    fwd[:, 0, 0, :] = cx.T
    fwd[:, 1, 0, :] = sx.T
    fwd[:, 0, 1, :] = -sx.T
    fwd[:, 1, 1, :] = cx.T
    x_fwd = fwd.reshape(GX, XL * 2, 2 * MX)[GX_ORDER].reshape(X * 2, 2 * MX)
    bwd = np.empty((X, 2, 2, MX))
    bwd[:, 0, 0, :] = cx.T
    bwd[:, 0, 1, :] = -sx.T
    bwd[:, 1, 0, :] = sx.T
    bwd[:, 1, 1, :] = cx.T
    bwd = bwd.reshape(GX, XL, 2, 2 * MX)[GX_ORDER]
    x_bwd = bwd.transpose(1, 2, 0, 3).reshape(X * 2, 2 * MX)
    return tuple(a.astype(BF16) for a in (zt_fwd, zt_bwd, y_fwd, y_bwd, x_fwd, x_bwd))


def dot(left, right, left_dim=1, right_dim=0):
    return lax.dot_general(
        left, right, (((left_dim,), (right_dim,)), ((), ())), preferred_element_type=F32
    )


def swap_bit(low, high, step):
    lane = lax.broadcasted_iota(jnp.int32, low.shape, 1)
    upper = (lane & step) != 0
    first = jnp.where(upper, pltpu.roll(high, step, 1), low)
    second = jnp.where(upper, high, pltpu.roll(low, LANES - step, 1))
    return first, second


def swap_eight(parts):
    parts = list(parts)
    for step in (1, 2, 4):
        for i in range(8):
            if not i & step:
                parts[i], parts[i | step] = swap_bit(parts[i], parts[i | step], step)
    return parts


def gelu_parts(pre):
    square = pre * pre
    inner = pre * (root_two_over_pi + (root_two_over_pi * gelu_cubic) * square)
    half = 0.5 + 0.5 * jnp.tanh(inner)
    rise = pre * (2.0 * root_two_over_pi + (6.0 * root_two_over_pi * gelu_cubic) * square)
    return pre * half, half * (1.0 + (1.0 - half) * rise)


def cells_of(wide_ref, y):
    return jnp.concatenate(
        [wide_ref[pl.ds(t * C * XL * YL + y, C * XL, stride=YL), :] for t in range(T)], 1
    )


def put_cells(wide_ref, y, value):
    for t in range(T):
        wide_ref[pl.ds(t * C * XL * YL + y, C * XL, stride=YL), :] = value[:, t * Z : (t + 1) * Z]


def pack(spread_ref, out_ref):
    for k in range(spread_ref.shape[0]):
        block = spread_ref[k, 0 : out_ref.shape[0], :]
        out_ref[:, k * LANES : (k + 1) * LANES] = block.astype(BF16)


def unpack(in_ref, spread_ref):
    for k in range(spread_ref.shape[0]):
        block = in_ref[:, k * LANES : (k + 1) * LANES].astype(F32)
        spread_ref[k, 0 : in_ref.shape[0], :] = block


def put_modes(spread_ref, y, cells, zt_fwd):
    turned = dot(zt_fwd, cells, 1, 1)
    for kt in range(T):
        for p in range(2):
            row = (kt * 2 + p) * MZ
            spread_ref[kt, pl.ds(y * 2 + p, MZ, stride=2 * YL), :] = turned[row : row + MZ]


def modes_of(spread_ref, y):
    return jnp.concatenate(
        [
            spread_ref[kt, pl.ds(y * 2 + p, MZ, stride=2 * YL), :]
            for kt in range(T)
            for p in range(2)
        ],
        0,
    )


def build_zt(table):
    shape = (MZ, Z)
    turns = lax.broadcasted_iota(jnp.int32, shape, 0) * lax.broadcasted_iota(jnp.int32, shape, 1)
    angle = (turns & (Z - 1)).astype(F32) * (2.0 * math.pi / Z)
    cosine = jnp.cos(angle)
    sine = jnp.sin(angle)
    real = (cosine, -sine, -cosine, sine)
    imag = (-sine, -cosine, sine, cosine)
    for kt in range(T):
        for p, part in enumerate((real, imag)):
            row = (kt * 2 + p) * MZ
            for t in range(T):
                table[row : row + MZ, t * Z : (t + 1) * Z] = part[kt * t % T].astype(BF16)


def open_kernel(field_ref, out_ref, wide, spread, table):
    build_zt(table)
    wide[0:ROWS, :] = field_ref[...].astype(F32)
    for y in range(YL):
        put_modes(spread, y, cells_of(wide, y).astype(BF16), table[...])
    pack(spread, out_ref)


def y_forward_kernel(in_ref, table_ref, out_ref, spread):
    along_y = dot(table_ref[...], in_ref[...])
    for low in range(2):
        parts = [
            along_y[
                j * 2 * GX : (j + 1) * 2 * GX,
                (kth * 2 + low) * LANES : (kth * 2 + low + 1) * LANES,
            ]
            for kth in range(2)
            for j in range(JL)
        ]
        for x, part in enumerate(swap_eight(parts)):
            for s in range(2):
                spread[low, pl.ds(x * 2 + s, GX, stride=2 * XL), :] = part[s * GX : (s + 1) * GX]
    pack(spread, out_ref)


def to_spectrum(in_ref, x_fwd_ref):
    low, high = (
        dot(in_ref[:, k * LANES : (k + 1) * LANES], x_fwd_ref[...], 0, 0)
        .astype(BF16)
        .astype(F32)
        for k in range(2)
    )
    return swap_bit(low, high, MX)


def from_spectrum(real, imag, x_bwd_ref, out_ref, spread):
    for low, modes in enumerate(swap_bit(real, imag, MX)):
        along_x = dot(x_bwd_ref[...], modes.astype(BF16), 1, 1)
        parts = [along_x[x * 2 * GX : (x + 1) * 2 * GX] for x in range(XL)]
        for i, part in enumerate(swap_eight(parts)):
            kth, j = divmod(i, JL)
            for s in range(2):
                spread[kth * 2 + low, pl.ds(j * 2 + s, GX, stride=2 * JL), :] = part[
                    s * GX : (s + 1) * GX
                ]
    pack(spread, out_ref)


def weight_parts(w_ref, c):
    w = w_ref[c].astype(F32).reshape(C, 2, 8, LANES)
    return w[:, 0], w[:, 1]


def at_channel(ref, c):
    return ref[pl.ds(pl.multiple_of(c * 8, 8), 8), :]


def mix_kernel(
    in_ref, w_ref, scale_ref, x_fwd_ref, x_bwd_ref, out_ref, real_ref, imag_ref, spread
):
    real, imag = to_spectrum(in_ref, x_fwd_ref)
    real_ref[...] = real
    imag_ref[...] = imag

    def add(c, total):
        s_real = at_channel(real_ref, c)[None]
        s_imag = at_channel(imag_ref, c)[None]
        w_real, w_imag = weight_parts(w_ref, c)
        return (
            total[0] + (s_real * w_real - s_imag * w_imag),
            total[1] + (s_real * w_imag + s_imag * w_real),
        )

    zero = jnp.zeros((C, 8, LANES), F32)
    mix_real, mix_imag = lax.fori_loop(0, C, add, (zero, zero), unroll=C)
    scale = scale_ref[0]
    from_spectrum(
        (mix_real * scale).reshape(C * 8, LANES),
        (mix_imag * scale).reshape(C * 8, LANES),
        x_bwd_ref,
        out_ref,
        spread,
    )


def back_kernel(
    in_ref,
    w_ref,
    scale_ref,
    x_fwd_ref,
    x_bwd_ref,
    s_real_ref,
    s_imag_ref,
    layer_ref,
    out_ref,
    grad_hbm,
    layer_hbm,
    real_ref,
    imag_ref,
    back_real,
    back_imag,
    spread,
    grad,
    sems,
):
    send_layer = pltpu.make_async_copy(layer_ref, layer_hbm, sems.at[0])
    send_layer.start()
    real, imag = to_spectrum(in_ref, x_fwd_ref)
    real_ref[...] = real
    imag_ref[...] = imag

    def outer(c, carry):
        s_real = (at_channel(s_real_ref, c).astype(F32) * scale_ref[0])[None, None]
        s_imag = (at_channel(s_imag_ref, c).astype(F32) * scale_ref[0])[None, None]
        a_real = real_ref[...].reshape(C, 1, 8, LANES)
        a_imag = imag_ref[...].reshape(C, 1, 8, LANES)
        both = jnp.concatenate(
            [s_real * a_real + s_imag * a_imag, s_real * a_imag - s_imag * a_real], 1
        )
        grad[c] = both.reshape(C * 2 * 8, LANES).astype(BF16)
        return carry

    lax.fori_loop(0, C, outer, 0, unroll=4)
    send_grad = pltpu.make_async_copy(grad, grad_hbm, sems.at[1])
    send_grad.start()

    def one(c, carry):
        a_real = real_ref[...].reshape(C, 8, LANES)
        a_imag = imag_ref[...].reshape(C, 8, LANES)
        w_real, w_imag = weight_parts(w_ref, c)
        row = pl.ds(pl.multiple_of(c * 8, 8), 8)
        back_real[row, :] = jnp.sum(a_real * w_real + a_imag * w_imag, 0)
        back_imag[row, :] = jnp.sum(a_imag * w_real - a_real * w_imag, 0)
        return carry

    lax.fori_loop(0, C, one, 0, unroll=4)
    scale = scale_ref[0]
    from_spectrum(back_real[...] * scale, back_imag[...] * scale, x_bwd_ref, out_ref, spread)
    send_layer.wait()
    send_grad.wait()


def y_backward_kernel(in_ref, table_ref, out_ref):
    out_ref[...] = dot(table_ref[...], in_ref[...]).astype(BF16)


def point_table(point_ref, back):
    shape = (C * XL, C)
    row = lax.broadcasted_iota(jnp.int32, shape, 0)
    pick = (row // XL == lax.broadcasted_iota(jnp.int32, shape, 1)).astype(F32).astype(BF16)
    half = dot(pick, point_ref[...], 1, 0 if back else 1).astype(BF16)
    full = dot(half, pick, 1, 1)
    row = lax.broadcasted_iota(jnp.int32, full.shape, 0)
    column = lax.broadcasted_iota(jnp.int32, full.shape, 1)
    return jnp.where(row % XL == column % XL, full, 0.0).astype(BF16)


def cell_kernel(
    in_ref,
    field_ref,
    cotangent_ref,
    point_ref,
    zt_bwd_ref,
    zt_fwd_ref,
    out_ref,
    slope_ref,
    layer_ref,
    back_ref,
    wide,
    other,
    spread,
):
    point = point_table(point_ref, False)
    back_ref[...] = point_table(point_ref, True)
    unpack(in_ref, spread)
    modes = [modes_of(spread, y).astype(BF16) for y in range(YL)]
    wide[0:ROWS, :] = field_ref[...].astype(F32)
    other[0:ROWS, :] = cotangent_ref[...].astype(F32)
    for y in range(YL):
        pre = dot(modes[y], zt_bwd_ref[...], 0, 0) + dot(point, cells_of(wide, y).astype(BF16))
        value, slope = gelu_parts(pre)
        put_cells(wide, y, value)
        slope_ref[y] = (cells_of(other, y) * slope).astype(BF16)
    layer_ref[...] = wide[0:ROWS, :].astype(BF16)
    for y in range(YL):
        put_modes(spread, y, slope_ref[y], zt_fwd_ref[...])
    pack(spread, out_ref)


def close_kernel(in_ref, slope_ref, point_ref, zt_bwd_ref, out_hbm, spread, wide, out, sems):
    point = point_ref[...]
    unpack(in_ref, spread)
    for y in range(YL):
        modes = modes_of(spread, y).astype(BF16)
        put_cells(wide, y, dot(modes, zt_bwd_ref[...], 0, 0) + dot(point, slope_ref[y]))
    copies = []
    for t in range(T):
        rows = pl.ds(t * C * XL * YL, C * XL * YL)
        out[rows, :] = wide[rows, :].astype(BF16)
        copies.append(pltpu.make_async_copy(out.at[rows], out_hbm.at[rows], sems.at[t]))
        copies[t].start()
    for copy in copies:
        copy.wait()


ROWS = T * C * XL * YL
ZT = (MZ * YL * 2, T * LANES)
AFTER_Y = (GX * XL * 2, 2 * LANES)
AFTER_X = (GX * JL * 2, T * LANES)
ZT_SPREAD = (T, MZ * YL * 2 + 16, LANES)
Y_SPREAD = (2, GX * XL * 2 + 16, LANES)
X_SPREAD = (T, GX * JL * 2 + 16, LANES)
CELLS = (YL, C * XL, T * Z)
PARTS = (C * 8, LANES)


WIDE = (ROWS, Z)
WIDE_SPREAD = (ROWS + 16, Z)
GRAD = (C, C * 2 * 8, LANES)


def vmem(shape, dtype=F32):
    return pltpu.VMEM(shape, dtype)


def call(kernel, outs, operands, scratch=(), scalars=(), far_outs=(), flops=10**8):
    near = pl.BlockSpec(memory_space=pltpu.VMEM)
    smem = pl.BlockSpec(memory_space=pltpu.SMEM)
    anywhere = pl.BlockSpec(memory_space=pltpu.HBM)
    specs = [smem if i in scalars else near for i in range(len(operands))]
    out_specs = tuple(anywhere if i in far_outs else near for i in range(len(outs)))
    single = len(outs) == 1
    moved = sum(math.prod(o.shape) * o.dtype.itemsize for o in list(outs) + list(operands))
    return pl.pallas_call(
        kernel,
        out_shape=outs[0] if single else tuple(outs),
        in_specs=specs,
        out_specs=out_specs[0] if single else out_specs,
        scratch_shapes=list(scratch),
        cost_estimate=pl.CostEstimate(flops=flops, bytes_accessed=moved, transcendentals=0),
        compiler_params=pltpu.CompilerParams(vmem_limit_bytes=16 * 1024 * 1024),
    )(*operands)


def shaped(shape, dtype=BF16):
    return jax.ShapeDtypeStruct(shape, dtype)


def exchange(block, axis):
    groups = [GX_ORDER] if axis == "gx" else None
    return lax.all_to_all(
        block, axis, split_axis=0, concat_axis=0, axis_index_groups=groups, tiled=True
    )


def open_stage(field):
    scratch = [vmem(WIDE_SPREAD), vmem(ZT_SPREAD), vmem((T * 2 * MZ, T * Z), BF16)]
    return call(open_kernel, [shaped(ZT)], [field], scratch)


def y_forward_stage(block, y_fwd):
    return call(y_forward_kernel, [shaped(AFTER_Y)], [block, y_fwd], [vmem(Y_SPREAD)])


def mix_stage(block, weight, scale, x_fwd, x_bwd):
    return call(
        mix_kernel,
        [shaped(AFTER_X), shaped(PARTS, F32), shaped(PARTS, F32)],
        [block, weight, scale, x_fwd, x_bwd],
        [vmem(X_SPREAD)],
        scalars=(2,),
    )


def y_backward_stage(block, y_bwd):
    return call(y_backward_kernel, [shaped(ZT)], [block, y_bwd])


def cell_stage(block, field, cotangent, point_weight, zt_bwd, zt_fwd):
    return call(
        cell_kernel,
        [shaped(ZT), shaped(CELLS), shaped(WIDE), shaped((C * XL, C * XL))],
        [block, field, cotangent, point_weight, zt_bwd, zt_fwd],
        [vmem(WIDE_SPREAD), vmem(WIDE_SPREAD), vmem(ZT_SPREAD)],
    )


def back_stage(block, weight, scale, x_fwd, x_bwd, spec_real, spec_imag, layer):
    scratch = [vmem(PARTS)] * 4 + [vmem(X_SPREAD), vmem(GRAD, BF16)]
    scratch.append(pltpu.SemaphoreType.DMA((2,)))
    return call(
        back_kernel,
        [shaped(AFTER_X), shaped(GRAD), shaped(WIDE)],
        [block, weight, scale, x_fwd, x_bwd, spec_real, spec_imag, layer],
        scratch,
        scalars=(2,),
        far_outs=(1, 2),
    )


def close_stage(block, slope, point_back, zt_bwd):
    return call(
        close_kernel,
        [shaped(WIDE)],
        [block, slope, point_back, zt_bwd],
        [vmem(ZT_SPREAD), vmem(WIDE_SPREAD), vmem(WIDE, BF16), pltpu.SemaphoreType.DMA((T,))],
        far_outs=(0,),
    )


def on_device(grid_field, spectral_weight, point_weight, cotangent):
    zt_fwd, zt_bwd, y_fwd, y_bwd, x_fwd, x_bwd = (jnp.asarray(a) for a in tables())
    field = grid_field.reshape(WIDE)
    cotan = cotangent.reshape(WIDE)
    weight = spectral_weight.reshape(C, C, JL, 4, LANES).transpose(0, 1, 3, 2, 4).reshape(GRAD)
    kz = lax.axis_index("gy")
    scale = (jnp.where(kz == 0, 1.0, 2.0).astype(F32) / float(X * Y * Z * T)).reshape(1)

    opened = open_stage(field)
    opened, scale = lax.optimization_barrier((opened, scale))
    halved = y_forward_stage(exchange(opened, "gy"), y_fwd)
    mixed, spec_real, spec_imag = mix_stage(exchange(halved, "gx"), weight, scale, x_fwd, x_bwd)
    along_y = y_backward_stage(exchange(mixed, "gx"), y_bwd)
    turned, slope, layer, point_back = cell_stage(
        exchange(along_y, "gy"), field, cotan, point_weight, zt_bwd, zt_fwd
    )
    halved = y_forward_stage(exchange(turned, "gy"), y_fwd)
    back, grad_spectral, layer_out = back_stage(
        exchange(halved, "gx"), weight, scale, x_fwd, x_bwd, spec_real, spec_imag, layer
    )
    along_y = y_backward_stage(exchange(back, "gx"), y_bwd)
    grad_field = close_stage(exchange(along_y, "gy"), slope, point_back, zt_bwd)

    grad_spectral = (
        grad_spectral.reshape(C, C, 4, JL, LANES)
        .transpose(0, 1, 3, 2, 4)
        .reshape(spectral_weight.shape)
    )
    return (
        layer_out.reshape(grid_field.shape),
        grad_field.reshape(grid_field.shape),
        grad_spectral,
    )


def solution(mesh):
    field = P(None, None, None, "gx", "gy", None)
    modes = P(None, None, "gx", "gy", None)
    return jax.shard_map(
        on_device,
        mesh=mesh,
        in_specs=(field, modes, P(), field),
        out_specs=(field, field, modes),
        check_vma=False,
    )
```

```python
import math

import jax
import jax.numpy as jnp
import numpy as np
from jax import lax
from jax.experimental import pallas as pl
from jax.experimental.pallas import tpu as pltpu
from jax.sharding import PartitionSpec as P

T = 4
C = 16
X = 128
Y = 128
Z = 128
MX = 64
MY = 64
MZ = 32
GX = 16
GY = 32
XL = X // GX
YL = Y // GY
JL = MY // GX
LANES = 128
GX_ORDER = [z * 8 + x * 2 + core for z in (1, 0) for x in (1, 3, 0, 2) for core in (1, 0)]

F32 = jnp.float32
BF16 = jnp.bfloat16

root_two_over_pi = math.sqrt(2.0 / math.pi)
gelu_cubic = 0.044715


def signed(kept):
    j = np.arange(kept)
    return np.where(j < kept // 2, j, j - kept)


def cos_sin(freq, length):
    q = np.mod(freq[:, None] * np.arange(length)[None, :], length)
    angle = q * (2.0 * np.pi / length)
    return np.cos(angle).astype(BF16), np.sin(angle).astype(BF16)


def tables():
    cz, sz = (a.astype(np.float64) for a in cos_sin(np.arange(MZ), Z))
    quarter = np.mod(np.arange(T)[:, None] * np.arange(T)[None, :], T)
    ct = np.array([1.0, 0.0, -1.0, 0.0])[quarter]
    st = np.array([0.0, 1.0, 0.0, -1.0])[quarter]
    both_cos = (
        cz[None, :, None, :] * ct[:, None, :, None] - sz[None, :, None, :] * st[:, None, :, None]
    )
    both_sin = (
        sz[None, :, None, :] * ct[:, None, :, None] + cz[None, :, None, :] * st[:, None, :, None]
    )
    zt_fwd = np.stack([both_cos, -both_sin], 1).reshape(T * 2 * MZ, T * Z)
    zt_bwd = zt_fwd

    cy, sy = (a.astype(np.float64) for a in cos_sin(signed(MY), Y))
    fwd = np.empty((MY, 2, Y, 2))
    fwd[:, 0, :, 0] = cy
    fwd[:, 0, :, 1] = sy
    fwd[:, 1, :, 0] = -sy
    fwd[:, 1, :, 1] = cy
    fwd = fwd.reshape(GX, JL, 2, Y * 2)[GX_ORDER]
    y_fwd = fwd.transpose(1, 2, 0, 3).reshape(MY * 2, Y * 2)
    bwd = np.empty((Y, 2, MY, 2))
    bwd[:, 0, :, 0] = cy.T
    bwd[:, 0, :, 1] = -sy.T
    bwd[:, 1, :, 0] = sy.T
    bwd[:, 1, :, 1] = cy.T
    y_bwd = bwd.reshape(Y * 2, GX, JL * 2)[:, GX_ORDER].reshape(Y * 2, MY * 2)

    cx, sx = (a.astype(np.float64) for a in cos_sin(signed(MX), X))
    fwd = np.empty((X, 2, 2, MX))
    fwd[:, 0, 0, :] = cx.T
    fwd[:, 1, 0, :] = sx.T
    fwd[:, 0, 1, :] = -sx.T
    fwd[:, 1, 1, :] = cx.T
    x_fwd = fwd.reshape(GX, XL * 2, 2 * MX)[GX_ORDER].reshape(X * 2, 2 * MX)
    bwd = np.empty((X, 2, 2, MX))
    bwd[:, 0, 0, :] = cx.T
    bwd[:, 0, 1, :] = -sx.T
    bwd[:, 1, 0, :] = sx.T
    bwd[:, 1, 1, :] = cx.T
    bwd = bwd.reshape(GX, XL, 2, 2 * MX)[GX_ORDER]
    x_bwd = bwd.transpose(1, 2, 0, 3).reshape(X * 2, 2 * MX)
    return tuple(a.astype(BF16) for a in (zt_fwd, zt_bwd, y_fwd, y_bwd, x_fwd, x_bwd))


def dot(left, right, left_dim=1, right_dim=0):
    return lax.dot_general(
        left, right, (((left_dim,), (right_dim,)), ((), ())), preferred_element_type=F32
    )


def swap_bit(low, high, step):
    lane = lax.broadcasted_iota(jnp.int32, low.shape, 1)
    upper = (lane & step) != 0
    first = jnp.where(upper, pltpu.roll(high, step, 1), low)
    second = jnp.where(upper, high, pltpu.roll(low, LANES - step, 1))
    return first, second


def swap_eight(parts):
    parts = list(parts)
    for step in (1, 2, 4):
        for i in range(8):
            if not i & step:
                parts[i], parts[i | step] = swap_bit(parts[i], parts[i | step], step)
    return parts


def gelu_parts(pre):
    square = pre * pre
    inner = pre * (root_two_over_pi + (root_two_over_pi * gelu_cubic) * square)
    half = 0.5 + 0.5 * jnp.tanh(inner)
    rise = pre * (2.0 * root_two_over_pi + (6.0 * root_two_over_pi * gelu_cubic) * square)
    return pre * half, half * (1.0 + (1.0 - half) * rise)


def cells_of(wide_ref, y):
    return jnp.concatenate(
        [wide_ref[pl.ds(t * C * XL * YL + y, C * XL, stride=YL), :] for t in range(T)], 1
    )


def put_cells(wide_ref, y, value):
    for t in range(T):
        wide_ref[pl.ds(t * C * XL * YL + y, C * XL, stride=YL), :] = value[:, t * Z : (t + 1) * Z]


def pack(spread_ref, out_ref):
    for k in range(spread_ref.shape[0]):
        block = spread_ref[k, 0 : out_ref.shape[0], :]
        out_ref[:, k * LANES : (k + 1) * LANES] = block.astype(BF16)


def unpack(in_ref, spread_ref):
    for k in range(spread_ref.shape[0]):
        block = in_ref[:, k * LANES : (k + 1) * LANES].astype(F32)
        spread_ref[k, 0 : in_ref.shape[0], :] = block


def put_modes(spread_ref, y, cells, zt_fwd):
    turned = dot(zt_fwd, cells, 1, 1)
    for kt in range(T):
        for p in range(2):
            row = (kt * 2 + p) * MZ
            spread_ref[kt, pl.ds(y * 2 + p, MZ, stride=2 * YL), :] = turned[row : row + MZ]


def modes_of(spread_ref, y):
    return jnp.concatenate(
        [
            spread_ref[kt, pl.ds(y * 2 + p, MZ, stride=2 * YL), :]
            for kt in range(T)
            for p in range(2)
        ],
        0,
    )


def build_zt(table):
    shape = (MZ, Z)
    turns = lax.broadcasted_iota(jnp.int32, shape, 0) * lax.broadcasted_iota(jnp.int32, shape, 1)
    angle = (turns & (Z - 1)).astype(F32) * (2.0 * math.pi / Z)
    cosine = jnp.cos(angle)
    sine = jnp.sin(angle)
    real = (cosine, -sine, -cosine, sine)
    imag = (-sine, -cosine, sine, cosine)
    for kt in range(T):
        for p, part in enumerate((real, imag)):
            row = (kt * 2 + p) * MZ
            for t in range(T):
                table[row : row + MZ, t * Z : (t + 1) * Z] = part[kt * t % T].astype(BF16)


def open_kernel(field_ref, out_ref, wide, spread, table):
    build_zt(table)
    wide[0:ROWS, :] = field_ref[...].astype(F32)
    for y in range(YL):
        put_modes(spread, y, cells_of(wide, y).astype(BF16), table[...])
    pack(spread, out_ref)


def y_forward_kernel(in_ref, table_ref, out_ref, spread):
    along_y = dot(table_ref[...], in_ref[...])
    for low in range(2):
        parts = [
            along_y[
                j * 2 * GX : (j + 1) * 2 * GX,
                (kth * 2 + low) * LANES : (kth * 2 + low + 1) * LANES,
            ]
            for kth in range(2)
            for j in range(JL)
        ]
        for x, part in enumerate(swap_eight(parts)):
            for s in range(2):
                spread[low, pl.ds(x * 2 + s, GX, stride=2 * XL), :] = part[s * GX : (s + 1) * GX]
    pack(spread, out_ref)


def to_spectrum(in_ref, x_fwd_ref):
    low, high = (
        dot(in_ref[:, k * LANES : (k + 1) * LANES], x_fwd_ref[...], 0, 0)
        .astype(BF16)
        .astype(F32)
        for k in range(2)
    )
    return swap_bit(low, high, MX)


def from_spectrum(real, imag, x_bwd_ref, out_ref, spread):
    for low, modes in enumerate(swap_bit(real, imag, MX)):
        along_x = dot(x_bwd_ref[...], modes.astype(BF16), 1, 1)
        parts = [along_x[x * 2 * GX : (x + 1) * 2 * GX] for x in range(XL)]
        for i, part in enumerate(swap_eight(parts)):
            kth, j = divmod(i, JL)
            for s in range(2):
                spread[kth * 2 + low, pl.ds(j * 2 + s, GX, stride=2 * JL), :] = part[
                    s * GX : (s + 1) * GX
                ]
    pack(spread, out_ref)


def weight_parts(w_ref, c):
    w = w_ref[c].astype(F32).reshape(C, 2, 8, LANES)
    return w[:, 0], w[:, 1]


def at_channel(ref, c):
    return ref[pl.ds(pl.multiple_of(c * 8, 8), 8), :]


def mix_kernel(
    in_ref, w_ref, scale_ref, x_fwd_ref, x_bwd_ref, out_ref, real_ref, imag_ref, spread
):
    real, imag = to_spectrum(in_ref, x_fwd_ref)
    real_ref[...] = real
    imag_ref[...] = imag

    def add(c, total):
        s_real = at_channel(real_ref, c)[None]
        s_imag = at_channel(imag_ref, c)[None]
        w_real, w_imag = weight_parts(w_ref, c)
        return (
            total[0] + (s_real * w_real - s_imag * w_imag),
            total[1] + (s_real * w_imag + s_imag * w_real),
        )

    zero = jnp.zeros((C, 8, LANES), F32)
    mix_real, mix_imag = lax.fori_loop(0, C, add, (zero, zero), unroll=C)
    scale = scale_ref[0]
    from_spectrum(
        (mix_real * scale).reshape(C * 8, LANES),
        (mix_imag * scale).reshape(C * 8, LANES),
        x_bwd_ref,
        out_ref,
        spread,
    )


def back_kernel(
    in_ref,
    w_ref,
    scale_ref,
    x_fwd_ref,
    x_bwd_ref,
    s_real_ref,
    s_imag_ref,
    layer_ref,
    out_ref,
    grad_hbm,
    layer_hbm,
    real_ref,
    imag_ref,
    back_real,
    back_imag,
    spread,
    grad,
    sems,
):
    send_layer = pltpu.make_async_copy(layer_ref, layer_hbm, sems.at[0])
    send_layer.start()
    real, imag = to_spectrum(in_ref, x_fwd_ref)
    real_ref[...] = real
    imag_ref[...] = imag

    def outer(c, carry):
        s_real = (at_channel(s_real_ref, c).astype(F32) * scale_ref[0])[None, None]
        s_imag = (at_channel(s_imag_ref, c).astype(F32) * scale_ref[0])[None, None]
        a_real = real_ref[...].reshape(C, 1, 8, LANES)
        a_imag = imag_ref[...].reshape(C, 1, 8, LANES)
        both = jnp.concatenate(
            [s_real * a_real + s_imag * a_imag, s_real * a_imag - s_imag * a_real], 1
        )
        grad[c] = both.reshape(C * 2 * 8, LANES).astype(BF16)
        return carry

    lax.fori_loop(0, C, outer, 0, unroll=4)
    send_grad = pltpu.make_async_copy(grad, grad_hbm, sems.at[1])
    send_grad.start()

    def one(c, carry):
        a_real = real_ref[...].reshape(C, 8, LANES)
        a_imag = imag_ref[...].reshape(C, 8, LANES)
        w_real, w_imag = weight_parts(w_ref, c)
        row = pl.ds(pl.multiple_of(c * 8, 8), 8)
        back_real[row, :] = jnp.sum(a_real * w_real + a_imag * w_imag, 0)
        back_imag[row, :] = jnp.sum(a_imag * w_real - a_real * w_imag, 0)
        return carry

    lax.fori_loop(0, C, one, 0, unroll=4)
    scale = scale_ref[0]
    from_spectrum(back_real[...] * scale, back_imag[...] * scale, x_bwd_ref, out_ref, spread)
    send_layer.wait()
    send_grad.wait()


def y_backward_kernel(in_ref, table_ref, out_ref):
    out_ref[...] = dot(table_ref[...], in_ref[...]).astype(BF16)


def point_table(point_ref, back):
    shape = (C * XL, C)
    row = lax.broadcasted_iota(jnp.int32, shape, 0)
    pick = (row // XL == lax.broadcasted_iota(jnp.int32, shape, 1)).astype(F32).astype(BF16)
    half = dot(pick, point_ref[...], 1, 0 if back else 1).astype(BF16)
    full = dot(half, pick, 1, 1)
    row = lax.broadcasted_iota(jnp.int32, full.shape, 0)
    column = lax.broadcasted_iota(jnp.int32, full.shape, 1)
    return jnp.where(row % XL == column % XL, full, 0.0).astype(BF16)


def cell_kernel(
    in_ref,
    field_ref,
    cotangent_ref,
    point_ref,
    zt_bwd_ref,
    zt_fwd_ref,
    out_ref,
    slope_ref,
    layer_ref,
    back_ref,
    wide,
    other,
    spread,
):
    point = point_table(point_ref, False)
    back_ref[...] = point_table(point_ref, True)
    unpack(in_ref, spread)
    modes = [modes_of(spread, y).astype(BF16) for y in range(YL)]
    wide[0:ROWS, :] = field_ref[...].astype(F32)
    other[0:ROWS, :] = cotangent_ref[...].astype(F32)
    for y in range(YL):
        pre = dot(modes[y], zt_bwd_ref[...], 0, 0) + dot(point, cells_of(wide, y).astype(BF16))
        value, slope = gelu_parts(pre)
        put_cells(wide, y, value)
        slope_ref[y] = (cells_of(other, y) * slope).astype(BF16)
    layer_ref[...] = wide[0:ROWS, :].astype(BF16)
    for y in range(YL):
        put_modes(spread, y, slope_ref[y], zt_fwd_ref[...])
    pack(spread, out_ref)


def close_kernel(in_ref, slope_ref, point_ref, zt_bwd_ref, out_hbm, spread, wide, out, sems):
    point = point_ref[...]
    unpack(in_ref, spread)
    for y in range(YL):
        modes = modes_of(spread, y).astype(BF16)
        put_cells(wide, y, dot(modes, zt_bwd_ref[...], 0, 0) + dot(point, slope_ref[y]))
    copies = []
    for t in range(T):
        rows = pl.ds(t * C * XL * YL, C * XL * YL)
        out[rows, :] = wide[rows, :].astype(BF16)
        copies.append(pltpu.make_async_copy(out.at[rows], out_hbm.at[rows], sems.at[t]))
        copies[t].start()
    for copy in copies:
        copy.wait()


ROWS = T * C * XL * YL
ZT = (MZ * YL * 2, T * LANES)
AFTER_Y = (GX * XL * 2, 2 * LANES)
AFTER_X = (GX * JL * 2, T * LANES)
ZT_SPREAD = (T, MZ * YL * 2 + 16, LANES)
Y_SPREAD = (2, GX * XL * 2 + 16, LANES)
X_SPREAD = (T, GX * JL * 2 + 16, LANES)
CELLS = (YL, C * XL, T * Z)
PARTS = (C * 8, LANES)


WIDE = (ROWS, Z)
WIDE_SPREAD = (ROWS + 16, Z)
GRAD = (C, C * 2 * 8, LANES)


def vmem(shape, dtype=F32):
    return pltpu.VMEM(shape, dtype)


def call(kernel, outs, operands, scratch=(), scalars=(), far_outs=(), flops=10**8):
    near = pl.BlockSpec(memory_space=pltpu.VMEM)
    smem = pl.BlockSpec(memory_space=pltpu.SMEM)
    anywhere = pl.BlockSpec(memory_space=pltpu.HBM)
    specs = [smem if i in scalars else near for i in range(len(operands))]
    out_specs = tuple(anywhere if i in far_outs else near for i in range(len(outs)))
    single = len(outs) == 1
    moved = sum(math.prod(o.shape) * o.dtype.itemsize for o in list(outs) + list(operands))
    return pl.pallas_call(
        kernel,
        out_shape=outs[0] if single else tuple(outs),
        in_specs=specs,
        out_specs=out_specs[0] if single else out_specs,
        scratch_shapes=list(scratch),
        cost_estimate=pl.CostEstimate(flops=flops, bytes_accessed=moved, transcendentals=0),
        compiler_params=pltpu.CompilerParams(vmem_limit_bytes=16 * 1024 * 1024),
    )(*operands)


def shaped(shape, dtype=BF16):
    return jax.ShapeDtypeStruct(shape, dtype)


def exchange(block, axis):
    groups = [GX_ORDER] if axis == "gx" else None
    return lax.all_to_all(
        block, axis, split_axis=0, concat_axis=0, axis_index_groups=groups, tiled=True
    )


def open_stage(field):
    scratch = [vmem(WIDE_SPREAD), vmem(ZT_SPREAD), vmem((T * 2 * MZ, T * Z), BF16)]
    return call(open_kernel, [shaped(ZT)], [field], scratch)


def y_forward_stage(block, y_fwd):
    return call(y_forward_kernel, [shaped(AFTER_Y)], [block, y_fwd], [vmem(Y_SPREAD)])


def mix_stage(block, weight, scale, x_fwd, x_bwd):
    return call(
        mix_kernel,
        [shaped(AFTER_X), shaped(PARTS, F32), shaped(PARTS, F32)],
        [block, weight, scale, x_fwd, x_bwd],
        [vmem(X_SPREAD)],
        scalars=(2,),
    )


def y_backward_stage(block, y_bwd):
    return call(y_backward_kernel, [shaped(ZT)], [block, y_bwd])


def cell_stage(block, field, cotangent, point_weight, zt_bwd, zt_fwd):
    return call(
        cell_kernel,
        [shaped(ZT), shaped(CELLS), shaped(WIDE), shaped((C * XL, C * XL))],
        [block, field, cotangent, point_weight, zt_bwd, zt_fwd],
        [vmem(WIDE_SPREAD), vmem(WIDE_SPREAD), vmem(ZT_SPREAD)],
    )


def back_stage(block, weight, scale, x_fwd, x_bwd, spec_real, spec_imag, layer):
    scratch = [vmem(PARTS)] * 4 + [vmem(X_SPREAD), vmem(GRAD, BF16)]
    scratch.append(pltpu.SemaphoreType.DMA((2,)))
    return call(
        back_kernel,
        [shaped(AFTER_X), shaped(GRAD), shaped(WIDE)],
        [block, weight, scale, x_fwd, x_bwd, spec_real, spec_imag, layer],
        scratch,
        scalars=(2,),
        far_outs=(1, 2),
    )


def close_stage(block, slope, point_back, zt_bwd):
    return call(
        close_kernel,
        [shaped(WIDE)],
        [block, slope, point_back, zt_bwd],
        [vmem(ZT_SPREAD), vmem(WIDE_SPREAD), vmem(WIDE, BF16), pltpu.SemaphoreType.DMA((T,))],
        far_outs=(0,),
    )


def on_device(grid_field, spectral_weight, point_weight, cotangent):
    zt_fwd, zt_bwd, y_fwd, y_bwd, x_fwd, x_bwd = (jnp.asarray(a) for a in tables())
    field = grid_field.reshape(WIDE)
    cotan = cotangent.reshape(WIDE)
    weight = spectral_weight.reshape(C, C, JL, 4, LANES).transpose(0, 1, 3, 2, 4).reshape(GRAD)
    kz = lax.axis_index("gy")
    scale = (jnp.where(kz == 0, 1.0, 2.0).astype(F32) / float(X * Y * Z * T)).reshape(1)

    opened = open_stage(field)
    opened, scale = lax.optimization_barrier((opened, scale))
    halved = y_forward_stage(exchange(opened, "gy"), y_fwd)
    mixed, spec_real, spec_imag = mix_stage(exchange(halved, "gx"), weight, scale, x_fwd, x_bwd)
    along_y = y_backward_stage(exchange(mixed, "gx"), y_bwd)
    turned, slope, layer, point_back = cell_stage(
        exchange(along_y, "gy"), field, cotan, point_weight, zt_bwd, zt_fwd
    )
    halved = y_forward_stage(exchange(turned, "gy"), y_fwd)
    back, grad_spectral, layer_out = back_stage(
        exchange(halved, "gx"), weight, scale, x_fwd, x_bwd, spec_real, spec_imag, layer
    )
    along_y = y_backward_stage(exchange(back, "gx"), y_bwd)
    grad_field = close_stage(exchange(along_y, "gy"), slope, point_back, zt_bwd)

    grad_spectral = (
        grad_spectral.reshape(C, C, 4, JL, LANES)
        .transpose(0, 1, 3, 2, 4)
        .reshape(spectral_weight.shape)
    )
    return (
        layer_out.reshape(grid_field.shape),
        grad_field.reshape(grid_field.shape),
        grad_spectral,
    )


def solution(mesh):
    field = P(None, None, None, "gx", "gy", None)
    modes = P(None, None, "gx", "gy", None)
    return jax.shard_map(
        on_device,
        mesh=mesh,
        in_specs=(field, modes, P(), field),
        out_specs=(field, field, modes),
        check_vma=False,
    )
```
